32 devices in a mesh: ta: 32 (over z, y, x, core).
Axes of the slice: x: 2, y: 2, z: 4, core: 2. Of those that a mesh axis runs over, the one named last changes fastest.
Arguments:
- frames: bfloat16 [16384, 512], P('ta'), may hold values from -8 to 8
- cotangent: float32 [16384, 512], P('ta'), may hold values from -30 to 30
- mem_index: int32 [1024, 4], P('ta'), may hold values from 0 to 1022, as said below
- master: float32 [2, 3146752], P(None, 'ta')
- moment: float32 [2, 3146752], P(None, 'ta')
- second: float32 [2, 3146752], P(None, 'ta')
- average: float32 [2, 3146752], P(None, 'ta')
Outputs:
- output: float32 [16384, 512], P('ta')
- grad_frames: float32 [16384, 512], P('ta')
- gain_grads: float32 [2, 1024], P(None, 'ta')
- new_moment: float32 [2, 3146752], P(None, 'ta')
- new_second: float32 [2, 3146752], P(None, 'ta')
- new_master: float32 [2, 3146752], P(None, 'ta')
- new_average: float32 [2, 3146752], P(None, 'ta')
The draws below stay inside these ranges and needn't reach their ends.
Inputs may be any that keep to these rules, and one draw needn't show every extreme that they name: `mem_index`: for segment g of the stream, slot 0 names one of the first min(g, 32) segments (0 when g is 0), slots 1 to 2 name one of the segments max(g - 64, 0) to g - 1 (0 when g is 0), and slot 3 names g - 1 (0 when g is 0); a slot is visible only when its number is below g.
All inputs are finite; a program needn't handle non-finite values.
Results may differ from the reference program's by a relative error of at most 0.023.
Values may be sent and summed in bfloat16 or wider, within the bound.
No kernel may reach another device: no remote copies, remote signals or barrier semaphores. Data moves between devices by JAX's collectives and lax.ppermute only.
A program may use at most 192 MiB of HBM per device.

```python
import math
import jax
import jax.numpy as jnp
from jax import lax

D = 512
HEADS = 8
FF = 2048
HEAD_DIM = 64
SEG = 16
LEFT = 30
RIGHT = 4
MEM = 4
WIN = 4
KEYS = 68
LAYERS = 2
STEP = 10
SEG_DEV = 32
TOKENS = 16384
SEGS = 1024
PL = 3146752


def region_bounds():
    first_end = 3 * D * D
    second_end = first_end + D * D
    third_end = second_end + D * FF
    fourth_end = third_end + FF * D
    return (first_end, second_end, third_end, fourth_end)


def unit_noise(key):
    return jax.random.normal(key, (LAYERS, PL), jnp.float32)


def master_values(key):
    first_end, second_end, third_end, fourth_end = region_bounds()
    target_positions = jnp.arange(PL, dtype=jnp.int32)
    base = unit_noise(key)
    column = target_positions % (3 * D)
    qkv_std = jnp.where(column < 2 * D, 1.5, 1.0) / math.sqrt(D)
    spread = jnp.where(target_positions < first_end, qkv_std, jnp.where(target_positions < second_end, math.sqrt(8.0 / D), jnp.where(target_positions < third_end, 1.0 / math.sqrt(D), 1.0 / math.sqrt(FF))))
    gain_part = 1.0 + 0.3 * jnp.clip(base / 2.0, -1.0, 1.0)
    return jnp.where(target_positions[None, :] >= fourth_end, gain_part, base * spread[None, :])


def grad_scale():
    first_end, second_end, third_end, fourth_end = region_bounds()
    target_positions = jnp.arange(PL, dtype=jnp.int32)
    factor = jnp.where(target_positions < first_end, 0.3, jnp.where(target_positions < second_end, 0.4, jnp.where(target_positions < third_end, 0.25, jnp.where(target_positions < fourth_end, 0.5, 1.0))))
    return (2.2 * factor * math.sqrt(TOKENS))[None, :]


def draw_master(key, part):
    return master_values(jax.random.fold_in(key, 11))


def draw_average(key, part):
    return master_values(jax.random.fold_in(key, 12))


def draw_moment(key, part):
    return unit_noise(jax.random.fold_in(key, 13)) * grad_scale()


def draw_second(key, part):
    factor = jax.random.uniform(jax.random.fold_in(key, 14), (LAYERS, PL), jnp.float32, 0.0, math.log(4.0))
    return grad_scale() * grad_scale() * jnp.exp(factor)


def draw_frames(key, part):
    key_common = jax.random.fold_in(key, 31)
    key_rough = jax.random.fold_in(key, 32)
    common = jnp.clip(jax.random.normal(key_common, (SEGS, D), jnp.float32), -4.0, 4.0)
    rough = jnp.clip(jax.random.normal(key_rough, (TOKENS, D), jnp.float32), -4.0, 4.0)
    return (0.9 * jnp.repeat(common, SEG, axis=0) + 0.44 * rough).astype(jnp.bfloat16)


def draw_cotangent(key, part):
    along = jnp.arange(TOKENS, dtype=jnp.float32) / (TOKENS - 1.0)
    base = jnp.clip(jax.random.normal(key, (TOKENS, D), jnp.float32), -5.0, 5.0)
    rise = 1.0 + 2.0 * along
    return base * rise[:, None]


def draw_mem_index(key, part):
    seg_ids = jnp.arange(SEGS, dtype=jnp.int32)
    key_first = jax.random.fold_in(key, 21)
    key_rest = jax.random.fold_in(key, 22)
    first_slot = jax.random.randint(key_first, (SEGS,), 0, jnp.maximum(jnp.minimum(seg_ids, SEG_DEV), 1))
    low_end = jnp.maximum(seg_ids - 2 * SEG_DEV, 0)
    high_end = jnp.maximum(seg_ids, 1)
    middle_slots = jax.random.randint(key_rest, (SEGS, MEM - 2), low_end[:, None], high_end[:, None])
    last_slot = jnp.maximum(seg_ids - 1, 0)
    return jnp.concatenate([first_slot[:, None], middle_slots, last_slot[:, None]], axis=1).astype(jnp.int32)


def setup_inputs(seed: int = 0) -> dict:
    key_list = jax.random.split(jax.random.key(seed), 8)
    return {
        "frames": draw_frames(jax.random.fold_in(key_list[7], 71), 0),
        "cotangent": draw_cotangent(jax.random.fold_in(key_list[7], 71), 0),
        "mem_index": draw_mem_index(jax.random.fold_in(key_list[7], 71), 0),
        "master": draw_master(jax.random.fold_in(key_list[7], 71), 0),
        "moment": draw_moment(jax.random.fold_in(key_list[7], 71), 0),
        "second": draw_second(jax.random.fold_in(key_list[7], 71), 0),
        "average": draw_average(jax.random.fold_in(key_list[7], 71), 0),
    }


@jax.custom_vjp
def low(v):
    return lax.optimization_barrier(v.astype(jnp.bfloat16)).astype(jnp.float32)

@jax.custom_vjp
def low_back(v):
    return v

def low_keep(v):
    return (low(v), None)

def low_pass(kept, grad):
    return (grad,)

def back_keep(v):
    return (v, None)

def back_low(kept, grad):
    return (low(grad),)
low.defvjp(low_keep, low_pass)
low_back.defvjp(back_keep, back_low)

def matmul(left_side, right_side):
    return jnp.dot(left_side, right_side, precision=lax.Precision.HIGHEST, preferred_element_type=jnp.float32)

def norm_rows(values, gain):
    centred = values - lax.optimization_barrier(jnp.mean(values, axis=-1, keepdims=True))
    return centred * lax.rsqrt(lax.optimization_barrier(jnp.mean(centred * centred, axis=-1, keepdims=True)) + 1e-05) * gain

def unpack(row, model_width, hidden_width):
    piece_sizes = [3 * model_width * model_width, model_width * model_width, model_width * hidden_width, hidden_width * model_width, 2 * model_width]
    shapes = [(model_width, 3 * model_width), (model_width, model_width), (model_width, hidden_width), (hidden_width, model_width), (2, model_width)]
    pieces = []
    offset = 0
    for piece_size, shape in zip(piece_sizes, shapes):
        pieces.append(row[offset:offset + piece_size].reshape(shape))
        offset = offset + piece_size
    return pieces

def key_masks(first_seg, seg_count, total_frames, mem_index):
    seg_ids = first_seg + jnp.arange(seg_count, dtype=jnp.int32)
    offsets = jnp.arange(WIN * SEG, dtype=jnp.int32)
    target_positions = seg_ids[:, None] * SEG - LEFT + offsets[None, :]
    window_ok = (offsets[None, :] < LEFT + SEG + RIGHT) & (target_positions >= 0) & (target_positions < total_frames)
    memory_ok = mem_index < seg_ids[:, None]
    return jnp.concatenate([window_ok, memory_ok], axis=1)

def encoder_layer(stream, row, mem_index):
    weight_qkv, weight_out, weight_up, weight_down, gains = unpack(row, D, FF)
    total_frames = stream.shape[0]
    seg_count = total_frames // SEG
    hidden_one = low(norm_rows(stream, gains[0]))
    projected = low_back(low(matmul(hidden_one, weight_qkv)))
    queries = projected[:, :D]
    keyvals = projected[:, D:]
    summary = low(lax.optimization_barrier(jnp.mean(hidden_one.reshape(seg_count, SEG, D), axis=1)))
    chosen = jnp.take(summary, mem_index.reshape(-1), axis=0)
    memory_kv = low_back(low(matmul(chosen, weight_qkv[:, D:]))).reshape(seg_count, MEM, 2 * D)
    extended = jnp.concatenate([jnp.zeros((LEFT, 2 * D), jnp.float32), keyvals, jnp.zeros(((WIN - 1) * SEG - LEFT, 2 * D), jnp.float32)], axis=0)
    windows = jnp.concatenate([extended[SEG * block_at:SEG * block_at + total_frames].reshape(seg_count, SEG, 2 * D) for block_at in range(WIN)], axis=1)
    key_rows = jnp.concatenate([windows, memory_kv], axis=1)
    attend_mask = key_masks(0, seg_count, total_frames, mem_index)
    query_heads = queries.reshape(seg_count, SEG, HEADS, HEAD_DIM)
    key_heads = key_rows[:, :, :D].reshape(seg_count, KEYS, HEADS, HEAD_DIM)
    value_heads = key_rows[:, :, D:].reshape(seg_count, KEYS, HEADS, HEAD_DIM)
    scores = low_back(jnp.einsum('sqhe,skhe->shqk', query_heads, key_heads, precision=lax.Precision.HIGHEST) * HEAD_DIM ** (-0.5))
    scores = jnp.where(attend_mask[:, None, None, :], scores, -1e+30)
    row_max = lax.optimization_barrier(jnp.max(scores, axis=-1, keepdims=True))
    exponent_terms = jnp.exp(scores - row_max)
    attn_weights = low(exponent_terms / lax.optimization_barrier(jnp.sum(exponent_terms, axis=-1, keepdims=True)))
    mixed = low_back(low(jnp.einsum('shqk,skhe->sqhe', attn_weights, value_heads, precision=lax.Precision.HIGHEST))).reshape(total_frames, D)
    after_attn = stream + low_back(matmul(mixed, weight_out))
    hidden_two = low(norm_rows(after_attn, gains[1]))
    up_proj = low_back(matmul(hidden_two, weight_up))
    activated = low(jax.nn.gelu(up_proj))
    return after_attn + low_back(matmul(activated, weight_down))

def reference(frames, cotangent, mem_index, master, moment, second, average):
    working = lax.optimization_barrier(master.astype(jnp.bfloat16)).astype(jnp.float32)

    def forward(stream, params):
        for layer_lookup in range(LAYERS):
            stream = encoder_layer(stream, params[layer_lookup], mem_index)
        return stream
    output, pullback = jax.vjp(forward, frames.astype(jnp.float32), working)
    grad_frames, parameter_gradients = pullback(cotangent)
    gain_grads = parameter_gradients[:, PL - 2 * D:]
    new_moment = 0.5 * moment + 0.5 * parameter_gradients
    new_second = 0.5 * second + 0.5 * parameter_gradients * parameter_gradients
    correction = 1.0 - 0.5 ** STEP
    update = new_moment / correction / (jnp.sqrt(new_second / correction) + 1e-08) + 0.1 * master
    new_master = master - 0.08 * update
    new_average = 0.9 * average + 0.1 * new_master
    return (output, grad_frames, gain_grads, new_moment, new_second, new_master, new_average)
```

```python
import functools

import jax
import jax.numpy as jnp
from jax import lax
from jax.experimental import pallas as pl
from jax.experimental.pallas import tpu as pltpu
from jax.sharding import PartitionSpec as P

D = 512
HEADS = 8
FF = 2048
SEG = 16
LEFT = 30
RIGHT = 4
MEM = 4
STEP = 10
FIRST = 32
NEG = -1e30

TOK = 512
NSEG = TOK // SEG
LH = 32
RH = 16
EXT = LH + TOK + 2 * RH
ROWS = EXT + NSEG * MEM
BLK = 4
NBLK = NSEG // BLK
QB = BLK * SEG
KB = 128
WB = KB - BLK * MEM

TILES = 1536
QKV0, WO0, WU0, WD0 = 0, 384, 512, 1024
MATS = TILES * 16 * 128

F32 = jnp.float32
BF16 = jnp.bfloat16
VM = pl.BlockSpec(memory_space=pltpu.VMEM)
SM = pl.BlockSpec(memory_space=pltpu.SMEM)
ANYS = pl.BlockSpec(memory_space=pl.ANY)


def mm(a, b):
    return lax.dot_general(a, b, (((1,), (0,)), ((), ())), preferred_element_type=F32)


def mm_nt(a, b):
    return lax.dot_general(a, b, (((1,), (1,)), ((), ())), preferred_element_type=F32)


def mm_tn(a, b):
    return lax.dot_general(a, b, (((0,), (0,)), ((), ())), preferred_element_type=F32)


def wblk(w, base, nj, i0, ni, j0, nj_take):
    cols = [
        jnp.concatenate([w[base + (i0 + i) * nj + j0 + j] for i in range(ni)], axis=0)
        for j in range(nj_take)
    ]
    return cols[0] if nj_take == 1 else jnp.concatenate(cols, axis=1)


def gain_row(g_ref, which):
    g = g_ref[...].astype(F32)
    return jnp.concatenate([g[4 * which + k : 4 * which + k + 1] for k in range(4)], axis=1)


def norm_parts(v):
    mean = jnp.mean(v, axis=-1, keepdims=True)
    cen = v - mean
    rstd = lax.rsqrt(jnp.mean(cen * cen, axis=-1, keepdims=True) + 1e-05)
    return cen * rstd, rstd


def norm_back(dh, xhat, rstd, gain):
    dx = dh * gain
    return rstd * (
        dx
        - jnp.mean(dx, axis=-1, keepdims=True)
        - xhat * jnp.mean(dx * xhat, axis=-1, keepdims=True)
    )


def head_of_layer(x, gain):
    xhat, _ = norm_parts(x)
    h1 = (xhat * gain).astype(BF16)
    summ = jnp.sum(h1.astype(F32).reshape(NSEG, SEG, D), axis=1) * (1.0 / SEG)
    return h1, summ.astype(BF16)


def first_kernel(x_ref, g_ref, h1_ref, sum_ref):
    h1, summ = head_of_layer(x_ref[...].astype(F32), gain_row(g_ref, 0))
    h1_ref[...] = h1
    sum_ref[...] = summ


def lane_lo(rows):
    return lax.broadcasted_iota(jnp.int32, (rows, 128), 1) < 64


def split_heads(m, lo):
    z = jnp.zeros_like(m)
    return jnp.concatenate([jnp.where(lo, m, z), jnp.where(lo, z, m)], axis=0)


def onehot_of(loc_ref):
    ids = lax.broadcasted_iota(jnp.int32, (NSEG * MEM, 128), 1)
    return jnp.where(loc_ref[...] == ids, 1.0, 0.0).astype(BF16)


def fwd_kernel(
    x_ref, h1_ref, hl_ref, hr_ref, tab_ref, loc_ref, col_ref, g_ref, gn_ref, w_ref,
    out_ref, h1n_ref, sumn_ref, hx_ref, q_ref, kv_ref, p_ref, o_ref, a_ref, h2_ref, gp_ref, act_ref,
    *, last,
):
    hx_ref[0:LH] = hl_ref[...]
    hx_ref[LH : LH + TOK] = h1_ref[...]
    hx_ref[LH + TOK : LH + TOK + RH] = hr_ref[...]
    hx_ref[LH + TOK + RH : EXT] = jnp.zeros((RH, D), BF16)
    hx_ref[EXT:ROWS] = mm(onehot_of(loc_ref), tab_ref[...]).astype(BF16)
    for jp in range(6):
        wc = wblk(w_ref, QKV0, 12, 0, 32, 2 * jp, 2)
        if jp < 2:
            q_ref[:, 256 * jp : 256 * jp + 256] = mm(h1_ref[...], wc).astype(BF16)
        else:
            c0 = 256 * (jp - 2)
            kv_ref[:, c0 : c0 + 256] = mm(hx_ref[...], wc).astype(BF16)

    qi = lax.broadcasted_iota(jnp.int32, (QB, KB), 0) // SEG
    ci = lax.broadcasted_iota(jnp.int32, (QB, KB), 1)
    off = ci - SEG * qi - (LH - LEFT)
    near = jnp.where((off >= 0) & (off < LEFT + SEG + RIGHT) & (ci < WB), 1.0, 0.0)
    band = near + jnp.where((ci >= WB) & ((ci - WB) // MEM == qi), 1.0, 0.0)
    lo = lane_lo(KB)

    def block(b, carry):
        r0 = pl.multiple_of(b * QB, QB)
        m0 = pl.multiple_of(EXT + b * (BLK * MEM), BLK * MEM)
        vis = band * col_ref[pl.ds(b, 1), :] > 0.5
        for p in range(4):
            kc = jnp.concatenate(
                [kv_ref[pl.ds(r0, WB), 128 * p : 128 * p + 128],
                 kv_ref[pl.ds(m0, BLK * MEM), 128 * p : 128 * p + 128]], axis=0)
            vc = jnp.concatenate(
                [kv_ref[pl.ds(r0, WB), D + 128 * p : D + 128 * p + 128],
                 kv_ref[pl.ds(m0, BLK * MEM), D + 128 * p : D + 128 * p + 128]], axis=0)
            qp = q_ref[pl.ds(r0, QB), 128 * p : 128 * p + 128]
            s = mm_nt(qp, split_heads(kc, lo)) * 0.125
            halves = []
            for h in range(2):
                sh = jnp.where(vis, s[:, 128 * h : 128 * h + 128], NEG)
                e = jnp.exp(sh - jnp.max(sh, axis=-1, keepdims=True))
                halves.append(e / jnp.sum(e, axis=-1, keepdims=True))
            pb = jnp.concatenate(halves, axis=1).astype(BF16)
            p_ref[b * 4 + p] = pb
            o_ref[pl.ds(r0, QB), 128 * p : 128 * p + 128] = mm(pb, split_heads(vc, lo)).astype(BF16)
        return carry

    lax.fori_loop(0, NBLK, block, 0)

    a = x_ref[...].astype(F32) + mm(o_ref[...], wblk(w_ref, WO0, 4, 0, 32, 0, 4))
    a_ref[...] = a
    xhat, _ = norm_parts(a)
    h2_ref[...] = (xhat * gain_row(g_ref, 1)).astype(BF16)
    out_ref[...] = a

    def ffn(c, carry):
        u = mm(h2_ref[...], wblk(w_ref, WU0, 16, 0, 32, 2 * c, 2))
        cc = 0.7978845608028654
        u2 = u * u
        t = jnp.tanh(cc * u * (1.0 + 0.044715 * u2))
        act = (0.5 * u * (1.0 + t)).astype(BF16)
        gp = 0.5 * (1.0 + t) + 0.5 * u * (1.0 - t * t) * cc * (1.0 + 3 * 0.044715 * u2)
        c0 = pl.multiple_of(c * 256, 256)
        act_ref[:, pl.ds(c0, 256)] = act
        gp_ref[:, pl.ds(c0, 256)] = gp.astype(BF16)
        out_ref[...] += mm(act, wblk(w_ref, WD0, 4, 16 * c, 16, 0, 4))
        return carry

    lax.fori_loop(0, FF // 256, ffn, 0)
    if not last:
        h1n, sumn = head_of_layer(out_ref[...], gain_row(gn_ref, 0))
        h1n_ref[...] = h1n
        sumn_ref[...] = sumn
    else:
        h1n_ref[...] = jnp.zeros_like(h1n_ref)
        sumn_ref[...] = jnp.zeros_like(sumn_ref)


def sds(shape, dtype):
    return jax.ShapeDtypeStruct(shape, dtype)


PARAMS = dict(vmem_limit_bytes=56 * 1024 * 1024)


def run(kernel, outs, ins, specs=None, scratch=(), flops=0, nbytes=0, **kw):
    return pl.pallas_call(
        kernel,
        out_shape=outs,
        in_specs=specs or [VM] * len(ins),
        out_specs=jax.tree.map(lambda _: VM, outs) if "out_specs" not in kw else kw["out_specs"],
        scratch_shapes=list(scratch),
        compiler_params=pltpu.CompilerParams(**PARAMS),
        cost_estimate=pl.CostEstimate(flops=flops, bytes_accessed=nbytes, transcendentals=0),
    )(*ins)


def bwd_kernel(
    dx_ref, w_ref, g_ref, loc_ref, q_ref, kv_ref, p_ref, a_ref, gp_ref,
    da_ref, dxb_ref, dub_ref, dab_ref, dq_ref, dkvb_ref, dh_ref, dtab_ref, dgb_ref,
    dkv_ref, dob_ref,
):
    dxb_ref[...] = dx_ref[...].astype(BF16)
    da_ref[...] = jnp.zeros_like(da_ref)

    def ffn(c, carry):
        c0 = pl.multiple_of(c * 256, 256)
        dact = mm_nt(dxb_ref[...], wblk(w_ref, WD0, 4, 16 * c, 16, 0, 4))
        du = (dact * gp_ref[:, pl.ds(c0, 256)].astype(F32)).astype(BF16)
        dub_ref[:, pl.ds(c0, 256)] = du
        da_ref[...] += mm_nt(du, wblk(w_ref, WU0, 16, 0, 32, 2 * c, 2))
        return carry

    lax.fori_loop(0, FF // 256, ffn, 0)
    xhat, rstd = norm_parts(a_ref[...])
    dh2 = da_ref[...]
    dgb_ref[...] = jnp.sum(dh2 * xhat, axis=0, keepdims=True)
    da = dx_ref[...] + norm_back(dh2, xhat, rstd, gain_row(g_ref, 1))
    da_ref[...] = da
    dab_ref[...] = da.astype(BF16)
    dob_ref[...] = mm_nt(dab_ref[...], wblk(w_ref, WO0, 4, 0, 32, 0, 4)).astype(BF16)

    dkv_ref[...] = jnp.zeros_like(dkv_ref)
    lo = lane_lo(KB)

    def block(b, carry):
        r0 = pl.multiple_of(b * QB, QB)
        m0 = pl.multiple_of(EXT + b * (BLK * MEM), BLK * MEM)
        for p in range(4):
            kc0, vc0 = 128 * p, D + 128 * p
            kc = jnp.concatenate(
                [kv_ref[pl.ds(r0, WB), kc0 : kc0 + 128], kv_ref[pl.ds(m0, BLK * MEM), kc0 : kc0 + 128]], axis=0)
            vc = jnp.concatenate(
                [kv_ref[pl.ds(r0, WB), vc0 : vc0 + 128], kv_ref[pl.ds(m0, BLK * MEM), vc0 : vc0 + 128]], axis=0)
            qp = q_ref[pl.ds(r0, QB), kc0 : kc0 + 128]
            dop = dob_ref[pl.ds(r0, QB), kc0 : kc0 + 128]
            pb = p_ref[b * 4 + p]
            dp = mm_nt(dop, split_heads(vc, lo))
            dv2 = mm_tn(pb, dop)
            ds = []
            for h in range(2):
                ph = pb[:, 128 * h : 128 * h + 128].astype(F32)
                dph = dp[:, 128 * h : 128 * h + 128]
                ds.append(ph * (dph - jnp.sum(dph * ph, axis=-1, keepdims=True)))
            dsb = jnp.concatenate(ds, axis=1).astype(BF16)
            dq_ref[pl.ds(r0, QB), kc0 : kc0 + 128] = (mm(dsb, split_heads(kc, lo)) * 0.125).astype(BF16)
            dk2 = mm_tn(dsb, qp) * 0.125
            dk = jnp.where(lo, dk2[:128], dk2[128:])
            dv = jnp.where(lo, dv2[:128], dv2[128:])
            dkv_ref[pl.ds(r0, WB), kc0 : kc0 + 128] += dk[:WB]
            dkv_ref[pl.ds(r0, WB), vc0 : vc0 + 128] += dv[:WB]
            dkv_ref[pl.ds(m0, BLK * MEM), kc0 : kc0 + 128] = dk[WB:]
            dkv_ref[pl.ds(m0, BLK * MEM), vc0 : vc0 + 128] = dv[WB:]
        return carry

    lax.fori_loop(0, NBLK, block, 0)
    dkvb_ref[...] = dkv_ref[...].astype(BF16)

    dh_ref[...] = jnp.zeros_like(dh_ref)
    for jp in range(6):
        wc = wblk(w_ref, QKV0, 12, 0, 32, 2 * jp, 2)
        if jp < 2:
            dh_ref[LH : LH + TOK] += mm_nt(dq_ref[:, 256 * jp : 256 * jp + 256], wc)
        else:
            c0 = 256 * (jp - 2)
            dh_ref[...] += mm_nt(dkvb_ref[:, c0 : c0 + 256], wc)
    dch = dh_ref[EXT:ROWS]
    hi = dch.astype(BF16)
    oh = onehot_of(loc_ref)
    dtab_ref[...] = mm_tn(oh, hi) + mm_tn(oh, (dch - hi.astype(F32)).astype(BF16))


def dw_kernel(hx_ref, h1_ref, dq_ref, dkv_ref, o_ref, dab_ref, h2_ref, dub_ref, act_ref, dxb_ref, g_ref):
    def put(val, base, nj, i0, j0):
        v = val.astype(BF16)
        for i in range(val.shape[0] // 16):
            for j in range(val.shape[1] // 128):
                g_ref[base + (i0 + i) * nj + j0 + j] = v[16 * i : 16 * i + 16, 128 * j : 128 * j + 128]

    def down(c, carry):
        c0 = pl.multiple_of(c * 256, 256)
        put(mm_tn(act_ref[:, pl.ds(c0, 256)], dxb_ref[...]), WD0, 4, 16 * c, 0)
        return carry

    lax.fori_loop(0, FF // 256, down, 0)

    def up(c, carry):
        c0 = pl.multiple_of(c * 256, 256)
        put(mm_tn(h2_ref[...], dub_ref[:, pl.ds(c0, 256)]), WU0, 16, 0, 2 * c)
        return carry

    lax.fori_loop(0, FF // 256, up, 0)
    for j in range(2):
        put(mm_tn(o_ref[...], dab_ref[:, 256 * j : 256 * j + 256]), WO0, 4, 0, 2 * j)
        put(mm_tn(h1_ref[...], dq_ref[:, 256 * j : 256 * j + 256]), QKV0, 12, 0, 2 * j)
    for j in range(4):
        put(mm_tn(hx_ref[...], dkv_ref[:, 256 * j : 256 * j + 256]), QKV0, 12, 0, 4 + 2 * j)


def nb_kernel(dh_ref, hal_ref, har_ref, dsum_ref, x_ref, da_ref, g_ref, dx_ref, dga_ref, acc_ref):
    acc_ref[...] = dh_ref[LH : LH + TOK]
    acc_ref[TOK - LH : TOK] += hal_ref[...]
    acc_ref[0:RH] += har_ref[...]
    for s in range(NSEG):
        acc_ref[SEG * s : SEG * s + SEG] += dsum_ref[s : s + 1, :] * (1.0 / SEG)
    xhat, rstd = norm_parts(x_ref[...].astype(F32))
    dh = acc_ref[...]
    dga_ref[...] = jnp.sum(dh * xhat, axis=0, keepdims=True)
    dx_ref[...] = da_ref[...] + norm_back(dh, xhat, rstd, gain_row(g_ref, 0))


def shift(value, by, n):
    return lax.ppermute(value, "ta", [(i, i + by) for i in range(n) if 0 <= i + by < n])


def from_first(value, me, n, root=0):
    step = n // 2
    while step:
        got = lax.ppermute(value, "ta", [(i ^ root, (i + step) ^ root) for i in range(0, n, 2 * step)])
        value = jnp.where(((me ^ root) % (2 * step)) == step, got, value)
        step //= 2
    return value


def to_first(value, me, n):
    step = 1
    while step < n:
        value = value + lax.ppermute(value, "ta", [(i + step, i) for i in range(0, n, 2 * step)])
        step *= 2
    return value


def sum_all(value, n):
    step = 1
    while step < n:
        value = value + lax.ppermute(value, "ta", [(i, i ^ step) for i in range(n)])
        step *= 2
    return value


def tiles_of(rows, ni, nj):
    return rows.reshape(ni, 16, nj, 128).transpose(0, 2, 1, 3).reshape(ni * nj, 16, 128)


def rows_of(tiles, ni, nj):
    return tiles.reshape(ni, nj, 16, 128).transpose(0, 2, 1, 3).reshape(ni * nj * 16, 128)


PIECES = ((QKV0, 32, 12), (WO0, 32, 4), (WU0, 32, 16), (WD0, 128, 4))


def gather_plain(aligned):
    full = lax.all_gather(aligned.reshape(-1, 128), "ta", axis=0, tiled=True)
    return jnp.concatenate(
        [tiles_of(full[16 * b : 16 * (b + ni * nj)], ni, nj) for b, ni, nj in PIECES], axis=0
    )


def reduce_plain(tiles):
    full = jnp.concatenate([rows_of(tiles[b : b + ni * nj], ni, nj) for b, ni, nj in PIECES], axis=0)
    return lax.psum_scatter(full, "ta", scatter_dimension=0, tiled=True).astype(F32).reshape(-1)


def per_device(frames, cotangent, mem_index, master, moment, second, average):
    n = lax.axis_size("ta")
    me = lax.axis_index("ta")
    layers, share = master.shape
    step = 2 * D // n
    tail = shift(master[:, share - 2 * D :], 1, n)
    ext = jnp.concatenate([tail, master], axis=1)
    aligned = lax.dynamic_slice(ext, (0, 2 * D - step * me), (layers, MATS // n)).astype(BF16)
    gains = from_first(master[:, share - 2 * D :].astype(BF16).reshape(layers, 8, 128), me, n, n - 1)
    weights = [gather_plain(aligned[l]) for l in range(layers)]

    first_seg = me * NSEG
    seg_ids = first_seg + jnp.arange(NSEG, dtype=jnp.int32)
    slot = jnp.arange(MEM, dtype=jnp.int32)
    loc = jnp.where(slot[None, :] == 0, mem_index, mem_index - first_seg + 96).reshape(-1, 1)
    pos = me * TOK - LH + QB * jnp.arange(NBLK)[:, None] + jnp.arange(WB)[None, :]
    col = jnp.concatenate(
        [(pos >= 0) & (pos < n * TOK), (mem_index < seg_ids[:, None]).reshape(NBLK, BLK * MEM)], axis=1
    ).astype(F32)

    h1, summ = run(first_kernel, (sds((TOK, D), BF16), sds((NSEG, D), BF16)), (frames, gains[0]))
    x = frames
    saved = []
    for l in range(layers):
        hl = shift(h1[TOK - LH :], 1, n)
        hr = shift(h1[:RH], -1, n)
        table = jnp.concatenate(
            [from_first(summ, me, n), shift(summ, 2, n), shift(summ, 1, n), summ], axis=0
        )
        outs = (
            sds((TOK, D), F32), sds((TOK, D), BF16), sds((NSEG, D), BF16), sds((ROWS, D), BF16),
            sds((TOK, D), BF16), sds((ROWS, 2 * D), BF16), sds((NBLK * 4, QB, 256), BF16), sds((TOK, D), BF16),
            sds((TOK, D), F32), sds((TOK, D), BF16), sds((TOK, FF), BF16), sds((TOK, FF), BF16),
        )
        res = run(
            functools.partial(fwd_kernel, last=l == layers - 1),
            outs,
            (x, h1, hl, hr, table, loc, col, gains[l], gains[min(l + 1, layers - 1)], weights[l]),
            flops=3 * 10**9, nbytes=30 * 10**6,
        )
        saved.append((x, h1) + tuple(res[3:]))
        x, h1, summ = res[:3]
    output = x

    dx = cotangent
    reduced = [None] * layers
    gain_rows = [None] * layers
    for l in reversed(range(layers)):
        xin, h1, hx, q, kv, prob, o, a, h2, gp, act = saved[l]
        outs = (
            sds((TOK, D), F32), sds((TOK, D), BF16), sds((TOK, FF), BF16), sds((TOK, D), BF16), sds((TOK, D), BF16),
            sds((ROWS, 2 * D), BF16), sds((ROWS, D), F32), sds((128, D), F32), sds((1, D), F32),
        )
        da, dxb, dub, dab, dq, dkvb, dh, dtab, dgb = run(
            bwd_kernel, outs, (dx, weights[l], gains[l], loc, q, kv, prob, a, gp),
            scratch=[pltpu.VMEM((ROWS, 2 * D), F32), pltpu.VMEM((TOK, D), BF16)],
            flops=4 * 10**9, nbytes=30 * 10**6,
        )
        grads = run(
            dw_kernel, sds((TILES, 16, 128), BF16), (hx, h1, dq, dkvb, o, dab, h2, dub, act, dxb),
            flops=4 * 10**9, nbytes=30 * 10**6,
        )
        reduced[l] = reduce_plain(grads)
        hal = shift(dh[:LH], -1, n)
        har = shift(dh[LH + TOK : LH + TOK + RH], 1, n)
        root = to_first(dtab[:NSEG], me, n)
        dsum = jnp.where(me == 0, root, 0.0) + shift(dtab[32:64], -2, n) + shift(dtab[64:96], -1, n) + dtab[96:]
        dx, dga = run(
            nb_kernel, (sds((TOK, D), F32), sds((1, D), F32)), (dh, hal, har, dsum, xin, da, gains[l]),
            scratch=[pltpu.VMEM((TOK, D), F32)], flops=10**6, nbytes=6 * 10**6,
        )
        gain_rows[l] = jnp.concatenate([dga, dgb], axis=1)

    gsum = sum_all(jnp.concatenate(gain_rows, axis=0), n)
    own = jnp.stack(reduced)
    head = jnp.where(me == n - 1, gsum, shift(own[:, : 2 * D], -1, n))
    grad = lax.dynamic_slice(jnp.concatenate([own, head], axis=1), (0, step * me), (layers, share))
    gain_out = lax.dynamic_slice(gsum, (0, step * me), (layers, step))
    new_moment = 0.5 * moment + 0.5 * grad
    new_second = 0.5 * second + 0.5 * grad * grad
    correction = 1.0 - 0.5**STEP
    update = new_moment / correction / (jnp.sqrt(new_second / correction) + 1e-08) + 0.1 * master
    new_master = master - 0.08 * update
    new_average = 0.9 * average + 0.1 * new_master
    return (output, dx, gain_out, new_moment, new_second, new_master, new_average)


def solution(mesh):
    rows, flat = P("ta", None), P(None, "ta")
    return jax.shard_map(
        per_device,
        mesh=mesh,
        in_specs=(rows, rows, rows, flat, flat, flat, flat),
        out_specs=(rows, rows, flat, flat, flat, flat, flat),
        check_vma=False,
    )
```

```python
import functools

import jax
import jax.numpy as jnp
from jax import lax
from jax.experimental import pallas as pl
from jax.experimental.pallas import tpu as pltpu
from jax.sharding import PartitionSpec as P

D = 512
HEADS = 8
FF = 2048
SEG = 16
LEFT = 30
RIGHT = 4
MEM = 4
STEP = 10
FIRST = 32
NEG = -1e30

TOK = 512
NSEG = TOK // SEG
LH = 32
RH = 16
EXT = LH + TOK + 2 * RH
ROWS = EXT + NSEG * MEM
BLK = 4
NBLK = NSEG // BLK
QB = BLK * SEG
KB = 128
WB = KB - BLK * MEM

TILES = 1536
QKV0, WO0, WU0, WD0 = 0, 384, 512, 1024
MATS = TILES * 16 * 128
GROUPS = 32
BT = TILES // GROUPS
PT = 36

F32 = jnp.float32
BF16 = jnp.bfloat16
VM = pl.BlockSpec(memory_space=pltpu.VMEM)
SM = pl.BlockSpec(memory_space=pltpu.SMEM)
ANYS = pl.BlockSpec(memory_space=pl.ANY)


def mm(a, b):
    return lax.dot_general(a, b, (((1,), (0,)), ((), ())), preferred_element_type=F32)


def mm_nt(a, b):
    return lax.dot_general(a, b, (((1,), (1,)), ((), ())), preferred_element_type=F32)


def mm_tn(a, b):
    return lax.dot_general(a, b, (((0,), (0,)), ((), ())), preferred_element_type=F32)


def wblk(w, base, nj, i0, ni, j0, nj_take):
    cols = [
        jnp.concatenate([w[base + (i0 + i) * nj + j0 + j] for i in range(ni)], axis=0)
        for j in range(nj_take)
    ]
    return cols[0] if nj_take == 1 else jnp.concatenate(cols, axis=1)


def place(me, rc, ra, rb, k):
    core = (me % 2) ^ rc
    x = ((me // 2) % 2) ^ jnp.where(core == 0, ra, rb)
    y = ((me // 4) % 2) ^ jnp.where(core == 0, rb, ra)
    z = (me // 8 + k) % 4
    return ((z * 2 + y) * 2 + x) * 2 + core


def load_weights(me, pieces, w_ref, sems, gt_ref=None):
    if len(pieces) < 5:
        if gt_ref is not None:
            pltpu.make_async_copy(pieces[1], gt_ref, sems.at[1, 0]).start()
        for d in range(GROUPS):
            per = TILES // GROUPS
            pltpu.make_async_copy(
                pieces[0].at[pl.ds(per * d, per)], w_ref.at[pl.ds(per * d, per)], sems.at[0, d]
            ).start()
        return
    if len(pieces) == 5:
        for m in range(4):
            for k in range(4):
                for rc, src in ((0, pieces[m].at[k]), (1, pieces[4].at[m, k])):
                    d = place(me, rc, m % 2, m // 2, -k % 4)
                    pltpu.make_async_copy(src, w_ref.at[pl.ds(d * BT, BT)], sems.at[0, d]).start()
        return
    for rc in range(2):
        for m in range(4):
            for k in range(4):
                d = place(me, rc, m % 2, m // 2, -k % 4)
                t = d * BT
                pltpu.make_async_copy(
                    pieces[4 * rc + m].at[k], w_ref.at[pl.ds(t, PT)], sems.at[0, d]
                ).start()
                late = pieces[8 + 4 * rc + k].at[m]
                pltpu.make_async_copy(
                    late.at[pl.ds(0, BT - PT)], w_ref.at[pl.ds(t + PT, BT - PT)], sems.at[1, d]
                ).start()
                if gt_ref is not None:

                    @pl.when(d == GROUPS - 1)
                    def _():
                        pltpu.make_async_copy(late.at[BT - PT], gt_ref, sems.at[1, GROUPS]).start()


def await_gains(pieces, gt_ref, sems):
    pltpu.make_async_copy(gt_ref, gt_ref, sems.at[1, 0 if len(pieces) < 16 else GROUPS]).wait()


def await_weights(pieces, w_ref, sems, lo, hi):
    for d in range(lo, hi):
        t = d * BT
        if len(pieces) < 16:
            pltpu.make_async_copy(
                w_ref.at[pl.ds(t, BT)], w_ref.at[pl.ds(t, BT)], sems.at[0, d]
            ).wait()
            continue
        pltpu.make_async_copy(w_ref.at[pl.ds(t, PT)], w_ref.at[pl.ds(t, PT)], sems.at[0, d]).wait()
        pltpu.make_async_copy(
            w_ref.at[pl.ds(t + PT, BT - PT)], w_ref.at[pl.ds(t + PT, BT - PT)], sems.at[1, d]
        ).wait()


def gain_row(g_ref, layer, which):
    g = g_ref[...].astype(F32)
    r = 8 * layer + 4 * which
    return jnp.concatenate([g[r + k : r + k + 1] for k in range(4)], axis=1)


def norm_parts(v):
    mean = jnp.mean(v, axis=-1, keepdims=True)
    cen = v - mean
    rstd = lax.rsqrt(jnp.mean(cen * cen, axis=-1, keepdims=True) + 1e-05)
    return cen * rstd, rstd


def norm_back(dh, xhat, rstd, gain):
    dx = dh * gain
    return rstd * (
        dx
        - jnp.mean(dx, axis=-1, keepdims=True)
        - xhat * jnp.mean(dx * xhat, axis=-1, keepdims=True)
    )


def seg_mean(h):
    return (jnp.sum(h.astype(F32).reshape(NSEG, SEG, D), axis=1) * (1.0 / SEG)).astype(BF16)


def head_of_layer(x, gain):
    xhat, _ = norm_parts(x)
    h1 = (xhat * gain).astype(BF16)
    return h1, seg_mean(h1)


def first_kernel(x_ref, sum_ref):
    xhat, _ = norm_parts(x_ref[...].astype(F32))
    sum_ref[...] = seg_mean(xhat)


def lane_lo(rows):
    return lax.broadcasted_iota(jnp.int32, (rows, 128), 1) < 64


def split_heads(m, lo):
    z = jnp.zeros_like(m)
    return jnp.concatenate([jnp.where(lo, m, z), jnp.where(lo, z, m)], axis=0)


def onehot_of(loc_ref):
    ids = lax.broadcasted_iota(jnp.int32, (NSEG * MEM, 128), 1)
    return jnp.where(loc_ref[...] == ids, 1.0, 0.0).astype(BF16)


def block_keys(kv_ref, b, col):
    r0 = pl.multiple_of(b * QB, QB)
    m0 = pl.multiple_of(EXT + b * (BLK * MEM), BLK * MEM)
    return jnp.concatenate(
        [kv_ref[pl.ds(r0, WB), col : col + 128], kv_ref[pl.ds(m0, BLK * MEM), col : col + 128]], axis=0
    )


def attend(me, n, q_ref, kv_ref, vis_ref, p_ref, o_ref):
    ki = lax.broadcasted_iota(jnp.int32, (KB, 128), 0)
    qi = (lax.broadcasted_iota(jnp.int32, (KB, 128), 1) % QB) // SEG
    off = ki - SEG * qi - (LH - LEFT)
    near = jnp.where((off >= 0) & (off < LEFT + SEG + RIGHT) & (ki < WB), 1.0, 0.0)
    memb = jnp.where((ki >= WB) & ((ki - WB) // MEM == qi), 1.0, 0.0)
    first = jnp.where(me == 0, LH, 0)
    end = jnp.where(me == n - 1, LH + TOK, EXT)
    lo = lane_lo(QB)

    def block(b, carry):
        r0 = pl.multiple_of(b * QB, QB)
        m0 = pl.multiple_of(b * (BLK * MEM), BLK * MEM)
        inside = (ki + r0 >= first) & (ki + r0 < end)
        memv = jnp.concatenate(
            [jnp.zeros((WB, 128), F32), vis_ref[pl.ds(m0, BLK * MEM), :]], axis=0
        )
        seen = jnp.where(inside, near, 0.0) + memb * memv > 0.5
        for p in range(4):
            kc, vc = block_keys(kv_ref, b, 128 * p), block_keys(kv_ref, b, D + 128 * p)
            s = mm_nt(kc, split_heads(q_ref[pl.ds(r0, QB), 128 * p : 128 * p + 128], lo))
            s = jnp.where(seen, s, NEG)
            e = jnp.exp(s - jnp.max(s, axis=0, keepdims=True))
            pb = (e * (1.0 / jnp.sum(e, axis=0, keepdims=True))).astype(BF16)
            p_ref[b * 4 + p] = pb
            o2 = mm_tn(pb, vc)
            o_ref[pl.ds(r0, QB), 128 * p : 128 * p + 128] = jnp.where(lo, o2[:QB], o2[QB:]).astype(BF16)
        return carry

    lax.fori_loop(0, NBLK, block, 0)


def attend_back(q_ref, kv_ref, p_ref, do_ref, dq_ref, dkv_ref):
    dkv_ref[...] = jnp.zeros_like(dkv_ref)
    lo = lane_lo(QB)

    def block(b, carry):
        r0 = pl.multiple_of(b * QB, QB)
        m0 = pl.multiple_of(EXT + b * (BLK * MEM), BLK * MEM)
        for p in range(4):
            kc0, vc0 = 128 * p, D + 128 * p
            kc, vc = block_keys(kv_ref, b, kc0), block_keys(kv_ref, b, vc0)
            qq = split_heads(q_ref[pl.ds(r0, QB), kc0 : kc0 + 128], lo)
            dd = split_heads(do_ref[pl.ds(r0, QB), kc0 : kc0 + 128], lo)
            pb = p_ref[b * 4 + p]
            pf = pb.astype(F32)
            pd = pf * mm_nt(vc, dd)
            ds = (pd - pf * jnp.sum(pd, axis=0, keepdims=True)).astype(BF16)
            dv, dk = mm(pb, dd), mm(ds, qq)
            dq2 = mm_tn(ds, kc)
            dq_ref[pl.ds(r0, QB), kc0 : kc0 + 128] = (jnp.where(lo, dq2[:QB], dq2[QB:]) * 0.125).astype(BF16)
            dkv_ref[pl.ds(r0, WB), kc0 : kc0 + 128] += dk[:WB]
            dkv_ref[pl.ds(r0, WB), vc0 : vc0 + 128] += dv[:WB]
            dkv_ref[pl.ds(m0, BLK * MEM), kc0 : kc0 + 128] = dk[WB:]
            dkv_ref[pl.ds(m0, BLK * MEM), vc0 : vc0 + 128] = dv[WB:]
        return carry

    lax.fori_loop(0, NBLK, block, 0)


class Copies:
    def __init__(self, sems):
        self.sems, self.used, self.open = sems, 0, []

    def start(self, src, dst):
        copy = pltpu.make_async_copy(src, dst, self.sems.at[self.used])
        self.used += 1
        copy.start()
        return copy

    def out(self, src, dst):
        self.open.append(self.start(src, dst))

    def finish(self):
        for copy in self.open:
            copy.wait()


def project(hx_ref, w_ref, q_ref, kv_ref):
    q = mm(hx_ref[LH : LH + TOK], wblk(w_ref, QKV0, 12, 0, 32, 0, 4)).astype(BF16)
    q_ref[...] = q * jnp.asarray(0.125, BF16)
    for j in range(2):
        kv_ref[:, 512 * j : 512 * j + 512] = mm(hx_ref[...], wblk(w_ref, QKV0, 12, 0, 32, 4 + 4 * j, 4)).astype(BF16)


def feed_forward(h2_ref, w_ref, act_ref, gp_ref, out_ref, step):
    for c in range(4):
        u = mm(h2_ref[...], wblk(w_ref, WU0, 16, 0, 32, 4 * c, 4))
        cc, c3 = 0.7978845608028654, 0.7978845608028654 * 0.044715
        u2 = u * u
        t = jnp.tanh(u * (cc + c3 * u2))
        hu = 0.5 * u
        act = (hu + hu * t).astype(BF16)
        gp = 0.5 + 0.5 * t + hu * (1.0 - t * t) * (cc + 3 * c3 * u2)
        act_ref[:, 512 * c : 512 * c + 512] = act
        gp_ref[:, 512 * c : 512 * c + 512] = gp.astype(BF16)
        out_ref[...] += mm(act, wblk(w_ref, WD0, 4, 32 * c, 32, 0, 4))
        step(c)


def back_main(dx_ref, w_ref, gains, q_ref, kv_ref, p_ref, a_ref, gp_ref, da_ref, dxb_ref, dub_ref, dab_ref, dq_ref,
              dkvb_ref, dh_ref, dgb_ref, dkv_ref, dob_ref, step):
    dxb_ref[...] = dx_ref[...].astype(BF16)
    step("dxb")
    for c in range(4):
        dact = mm_nt(dxb_ref[...], wblk(w_ref, WD0, 4, 32 * c, 32, 0, 4))
        du = (dact * gp_ref[:, 512 * c : 512 * c + 512].astype(F32)).astype(BF16)
        dub_ref[:, 512 * c : 512 * c + 512] = du
        dh2 = mm_nt(du, wblk(w_ref, WU0, 16, 0, 32, 4 * c, 4))
        if c:
            da_ref[...] += dh2
        else:
            da_ref[...] = dh2
    step("dub")
    xhat, rstd = norm_parts(a_ref[...])
    dh2 = da_ref[...]
    dgb_ref[...] = jnp.sum(dh2 * xhat, axis=0, keepdims=True)
    da = dx_ref[...] + norm_back(dh2, xhat, rstd, gains)
    da_ref[...] = da
    dab_ref[...] = da.astype(BF16)
    step("dab")
    dob_ref[...] = mm_nt(dab_ref[...], wblk(w_ref, WO0, 4, 0, 32, 0, 4)).astype(BF16)
    step("attend")
    attend_back(q_ref, kv_ref, p_ref, dob_ref, dq_ref, dkv_ref)
    dkvb_ref[...] = dkv_ref[...].astype(BF16)
    step("dkvb")
    dh_ref[...] = mm_nt(dkvb_ref[...], wblk(w_ref, QKV0, 12, 0, 32, 4, 8))
    dh_ref[LH : LH + TOK] += mm_nt(dq_ref[...], wblk(w_ref, QKV0, 12, 0, 32, 0, 4))
    step("dh")


def table_grad(loc_ref, dh_ref, dtab_ref):
    dch = dh_ref[EXT:ROWS]
    hi = dch.astype(BF16)
    oh = onehot_of(loc_ref)
    dtab_ref[...] = mm_tn(oh, hi) + mm_tn(oh, (dch - hi.astype(F32)).astype(BF16))


def low_kernel(me_ref, x_ref, hl_ref, hr_ref, root_ref, b2_ref, summ_ref, loc_ref, vis_ref, *rest, np_, n):
    pieces, rest = rest[:np_], rest[np_:]
    (out_ref, h1n_ref, sumn_ref, gt_ref, hx_o, q_o, kv_o, p_o, o_o, a_o, h2_o, gp_o, act_o,
     w_ref, sems, hx_ref, q_ref, kv_ref, p_ref, o_ref, a_ref, h2_ref, gp_ref, act_ref, osem) = rest
    me = me_ref[0]
    load_weights(me, pieces, w_ref, sems, gt_ref)
    copies = Copies(osem)
    await_gains(pieces, gt_ref, sems)
    ga = gain_row(gt_ref, 0, 0)
    for ref, rows, at in ((hl_ref, LH, 0), (x_ref, TOK, LH), (hr_ref, RH, LH + TOK)):
        xhat, _ = norm_parts(ref[0:rows].astype(F32))
        hx_ref[at : at + rows] = (xhat * ga).astype(BF16)
    means = jnp.concatenate([root_ref[...], b2_ref[...], hl_ref[LH:], summ_ref[...]], axis=0)
    hx_ref[LH + TOK + RH : EXT] = jnp.zeros((RH, D), BF16)
    hx_ref[EXT:ROWS] = mm(onehot_of(loc_ref), (means.astype(F32) * ga).astype(BF16)).astype(BF16)
    copies.out(hx_ref, hx_o)
    await_weights(pieces, w_ref, sems, 0, 8)
    project(hx_ref, w_ref, q_ref, kv_ref)
    copies.out(q_ref, q_o)
    copies.out(kv_ref, kv_o)
    attend(me, n, q_ref, kv_ref, vis_ref, p_ref, o_ref)
    copies.out(p_ref, p_o)
    copies.out(o_ref, o_o)
    await_weights(pieces, w_ref, sems, 8, 32)
    a = x_ref[...].astype(F32) + mm(o_ref[...], wblk(w_ref, WO0, 4, 0, 32, 0, 4))
    a_ref[...] = a
    copies.out(a_ref, a_o)
    xhat, _ = norm_parts(a)
    h2_ref[...] = (xhat * gain_row(gt_ref, 0, 1)).astype(BF16)
    copies.out(h2_ref, h2_o)
    out_ref[...] = a
    feed_forward(h2_ref, w_ref, act_ref, gp_ref, out_ref, lambda c: None)
    copies.out(act_ref, act_o)
    copies.out(gp_ref, gp_o)
    h1n, sumn = head_of_layer(out_ref[...], gain_row(gt_ref, 1, 0))
    h1n_ref[...] = h1n
    sumn_ref[...] = sumn
    copies.finish()


def top_kernel(me_ref, x_ref, h1_ref, hl_ref, hr_ref, root_ref, b2_ref, summ_ref, loc_ref, vis_ref, gt_ref, cot_any,
               *rest, np_, n):
    pieces, rest = rest[:np_], rest[np_:]
    (out_o, da_ref, dh_ref, dtab_ref, dgb_ref, hx_o, o_o, h2_o, act_o, dxb_o, dub_o, dab_o, dq_o, dkvb_o,
     w_ref, sems, hx_ref, q_ref, kv_ref, p_ref, o_ref, a_ref, h2_ref, gp_ref, act_ref,
     out_ref, dx_ref, dxb_ref, dub_ref, dab_ref, dq_ref, dkvb_ref, dkv_ref, dob_ref, osem) = rest
    me = me_ref[0]
    load_weights(me, pieces, w_ref, sems)
    copies = Copies(osem)
    cot = copies.start(cot_any, dx_ref)
    hx_ref[0:LH] = hl_ref[0:LH]
    hx_ref[LH : LH + TOK] = h1_ref[...]
    hx_ref[LH + TOK : LH + TOK + RH] = hr_ref[...]
    hx_ref[LH + TOK + RH : EXT] = jnp.zeros((RH, D), BF16)
    table = jnp.concatenate([root_ref[...], b2_ref[...], hl_ref[LH:], summ_ref[...]], axis=0)
    hx_ref[EXT:ROWS] = mm(onehot_of(loc_ref), table).astype(BF16)
    copies.out(hx_ref, hx_o)
    await_weights(pieces, w_ref, sems, 0, 8)
    project(hx_ref, w_ref, q_ref, kv_ref)
    attend(me, n, q_ref, kv_ref, vis_ref, p_ref, o_ref)
    copies.out(o_ref, o_o)
    await_weights(pieces, w_ref, sems, 8, 32)
    a = x_ref[...] + mm(o_ref[...], wblk(w_ref, WO0, 4, 0, 32, 0, 4))
    a_ref[...] = a
    xhat, _ = norm_parts(a)
    h2_ref[...] = (xhat * gain_row(gt_ref, 1, 1)).astype(BF16)
    copies.out(h2_ref, h2_o)
    out_ref[...] = a
    feed_forward(h2_ref, w_ref, act_ref, gp_ref, out_ref, lambda c: None)
    copies.out(act_ref, act_o)
    copies.out(out_ref, out_o)
    cot.wait()
    done = {"dxb": ((dxb_ref, dxb_o),), "dub": ((dub_ref, dub_o),), "dab": ((dab_ref, dab_o),),
            "dkvb": ((dkvb_ref, dkvb_o), (dq_ref, dq_o))}

    def step(name):
        for pair in done.get(name, ()):
            copies.out(*pair)

    back_main(dx_ref, w_ref, gain_row(gt_ref, 1, 1), q_ref, kv_ref, p_ref, a_ref, gp_ref, da_ref, dxb_ref, dub_ref,
              dab_ref, dq_ref, dkvb_ref, dh_ref, dgb_ref, dkv_ref, dob_ref, step)
    table_grad(loc_ref, dh_ref, dtab_ref)
    copies.finish()


def norm_one_back(dh_ref, hal_ref, har_ref, dsum, x, gain, da_ref, acc_ref):
    acc_ref[...] = dh_ref[LH : LH + TOK]
    acc_ref[TOK - LH : TOK] += hal_ref[0:LH]
    acc_ref[0:RH] += har_ref[...]
    for s in range(NSEG):
        acc_ref[SEG * s : SEG * s + SEG] += dsum[s : s + 1, :] * (1.0 / SEG)
    xhat, rstd = norm_parts(x)
    dh = acc_ref[...]
    return da_ref[...] + norm_back(dh, xhat, rstd, gain), jnp.sum(dh * xhat, axis=0, keepdims=True)


def summed(me_ref, hal_ref, root_ref, b2_ref, dtab_ref):
    mine = dtab_ref[96:128] + hal_ref[LH:] + b2_ref[...]
    return mine + jnp.where(me_ref[0] == 0, root_ref[...], 0.0)


def bottom_kernel(me_ref, hal_ref, har_ref, root_ref, b2_ref, dtabp_ref, dhp_ref, x_ref, dap_ref, loc_ref, gt_ref, *rest,
                  np_):
    pieces, rest = rest[:np_], rest[np_:]
    (q_any, kv_any, p_any, a_any, gp_any, dga_ref, da_ref, dh_ref, dtab_ref, dgb_ref, dxb_o, dub_o, dab_o, dq_o, dkvb_o,
     w_ref, sems, q_ref, kv_ref, p_ref, a_ref, gp_ref, dx_ref, dxb_ref, dub_ref, dab_ref, dq_ref, dkvb_ref, dkv_ref,
     dob_ref, osem) = rest
    load_weights(me_ref[0], pieces, w_ref, sems)
    copies = Copies(osem)
    loads = [copies.start(*pair) for pair in
             ((gp_any, gp_ref), (a_any, a_ref), (q_any, q_ref), (kv_any, kv_ref), (p_any, p_ref))]
    dx, dga = norm_one_back(
        dhp_ref, hal_ref, har_ref, summed(me_ref, hal_ref, root_ref, b2_ref, dtabp_ref), x_ref[...],
        gain_row(gt_ref, 1, 0), dap_ref, dx_ref,
    )
    dx_ref[...] = dx
    dga_ref[...] = dga
    await_weights(pieces, w_ref, sems, 0, 32)
    loads[0].wait()
    done = {"dxb": ((dxb_ref, dxb_o),), "dub": ((dub_ref, dub_o),), "dab": ((dab_ref, dab_o),),
            "dkvb": ((dkvb_ref, dkvb_o), (dq_ref, dq_o))}

    def step(name):
        if name == "dub":
            loads[1].wait()
        if name == "attend":
            for load in loads[2:]:
                load.wait()
        for pair in done.get(name, ()):
            copies.out(*pair)

    back_main(dx_ref, w_ref, gain_row(gt_ref, 0, 1), q_ref, kv_ref, p_ref, a_ref, gp_ref, da_ref, dxb_ref, dub_ref,
              dab_ref, dq_ref, dkvb_ref, dh_ref, dgb_ref, dkv_ref, dob_ref, step)
    table_grad(loc_ref, dh_ref, dtab_ref)
    copies.finish()


def last_kernel(me_ref, hal_ref, har_ref, root_ref, b2_ref, dtab_ref, dh_ref, x_ref, da_ref, gt_ref, dx_ref, dga_ref, acc_ref):
    dx, dga = norm_one_back(
        dh_ref, hal_ref, har_ref, summed(me_ref, hal_ref, root_ref, b2_ref, dtab_ref), x_ref[...].astype(F32),
        gain_row(gt_ref, 0, 0), da_ref, acc_ref,
    )
    dx_ref[...] = dx
    dga_ref[...] = dga


def dw_kernel(me_ref, *rest, part, nouts):
    srcs, rest = rest[:9], rest[9:]
    outs, rest = rest[-12 - nouts : -12], rest[-12:]
    hx_ref, dq_ref, dkv_ref, o_ref, dab_ref, h2_ref, dub_ref, act_ref, dxb_ref, g_ref, sem, isem = rest
    copies = Copies(isem)
    loads = {}
    for i in {0: (7, 8, 5, 6), 1: (3, 4, 0, 1, 2), None: (7, 8, 5, 6, 3, 4, 0, 1, 2)}[part]:
        loads[i] = copies.start(srcs[i], rest[i])

    def put(val, base, nj, i0, j0):
        v = val.astype(BF16)
        for i in range(val.shape[0] // 16):
            for j in range(val.shape[1] // 128):
                g_ref[base + (i0 + i) * nj + j0 + j] = v[16 * i : 16 * i + 16, 128 * j : 128 * j + 128]

    def send(lo, hi):
        if nouts == 1:
            tiles = pl.ds(lo * 16, (hi - lo) * 16)
            pltpu.make_async_copy(g_ref.at[tiles], outs[0].at[tiles], sem).start()
            return
        me = me_ref[0]
        units = {}
        for u in range(lo, hi):
            units.setdefault(u // 3, []).append(u % 3)
        for d, thirds in units.items():
            core = d % 2
            rx, ry = ((me // 2) % 2) ^ (d // 2 % 2), ((me // 4) % 2) ^ (d // 4 % 2)
            ra, rb = (rx, ry) if core == 0 else (ry, rx)
            k = (d // 8 - me // 8 + 4) % 4
            t0, t1 = 16 * thirds[0], 16 * thirds[-1] + 16
            for rc in range(2):

                @pl.when((me % 2) ^ core == rc)
                def _():
                    split = PT if nouts == 4 else BT
                    e0, e1 = min(t0, split), min(t1, split)
                    if e1 > e0:
                        pltpu.make_async_copy(
                            g_ref.at[pl.ds(d * BT + e0, e1 - e0)],
                            outs[nouts // 2 * rc].at[rb, ra, k, pl.ds(e0, e1 - e0)], sem,
                        ).start()
                    l0, l1 = max(t0, split), max(t1, split)
                    if l1 > l0:
                        pltpu.make_async_copy(
                            g_ref.at[pl.ds(d * BT + l0, l1 - l0)],
                            outs[2 * rc + 1].at[k, rb, ra, pl.ds(l0 - split, l1 - l0)], sem,
                        ).start()

    if part != 1:
        loads[7].wait()
        loads[8].wait()

        def down(c, carry):
            c0 = pl.multiple_of(c * 256, 256)
            put(mm_tn(act_ref[:, pl.ds(c0, 256)], dxb_ref[...]), WD0, 4, 16 * c, 0)
            return carry

        lax.fori_loop(0, FF // 256, down, 0)
        send(64, 96)
        loads[5].wait()
        loads[6].wait()

        def up(c, carry):
            c0 = pl.multiple_of(c * 256, 256)
            put(mm_tn(h2_ref[...], dub_ref[:, pl.ds(c0, 256)]), WU0, 16, 0, 2 * c)
            return carry

        lax.fori_loop(0, FF // 256, up, 0)
        send(32, 64)
    if part != 0:
        for i in (3, 4, 0, 1, 2):
            loads[i].wait()
        for j in range(2):
            put(mm_tn(o_ref[...], dab_ref[:, 256 * j : 256 * j + 256]), WO0, 4, 0, 2 * j)
        send(24, 32)
        for j in range(2):
            put(mm_tn(hx_ref[LH : LH + TOK], dq_ref[:, 256 * j : 256 * j + 256]), QKV0, 12, 0, 2 * j)
        for j in range(4):
            put(mm_tn(hx_ref[...], dkv_ref[:, 256 * j : 256 * j + 256]), QKV0, 12, 0, 4 + 2 * j)
        send(0, 24)
    first, count = {0: (WU0, 1024), 1: (0, 512), None: (0, TILES)}[part]
    all_of = g_ref.at[pl.ds(first, count)]
    pltpu.make_async_copy(all_of, all_of, sem).wait()


def sds(shape, dtype):
    return jax.ShapeDtypeStruct(shape, dtype)


PARAMS = dict(vmem_limit_bytes=56 * 1024 * 1024)


def run(kernel, outs, ins, specs=None, scratch=(), flops=0, nbytes=0, aliases=None, **kw):
    return pl.pallas_call(
        kernel,
        out_shape=outs,
        input_output_aliases=aliases or {},
        in_specs=specs or [VM] * len(ins),
        out_specs=jax.tree.map(lambda _: VM, outs) if "out_specs" not in kw else kw["out_specs"],
        scratch_shapes=list(scratch),
        compiler_params=pltpu.CompilerParams(**PARAMS),
        cost_estimate=pl.CostEstimate(flops=flops, bytes_accessed=nbytes, transcendentals=0),
    )(*ins)


def shift(value, by, n):
    return lax.ppermute(value, "ta", [(i, i + by) for i in range(n) if 0 <= i + by < n])


def strides(n):
    out = []
    while n > 1:
        radix = 2 if n == 2 else 4
        n //= radix
        out.append((n, radix))
    return out


def spread_round(value, stride, radix, n, root=0):
    parts = [
        lax.ppermute(value, "ta", [(i ^ root, (i + j * stride) ^ root) for i in range(0, n, radix * stride)])
        for j in range(1, radix)
    ]
    return functools.reduce(jnp.add, parts, value)


def collect_round(value, stride, radix, n):
    parts = [
        lax.ppermute(value, "ta", [(i + j * stride, i) for i in range(0, n, radix * stride)])
        for j in range(1, radix)
    ]
    return functools.reduce(jnp.add, parts, value)


def from_first(value, me, n, root=0):
    value = jnp.where(me == root, value, jnp.zeros_like(value))
    for stride, radix in strides(n):
        value = spread_round(value, stride, radix, n, root)
    return value


def sum_all(value, n):
    step = 1
    while step < n:
        value = value + lax.ppermute(value, "ta", [(i, i ^ step) for i in range(n)])
        step *= 2
    return value


def tiles_of(rows, ni, nj):
    return rows.reshape(ni, 16, nj, 128).transpose(0, 2, 1, 3).reshape(ni * nj, 16, 128)


def rows_of(tiles, ni, nj):
    return tiles.reshape(ni, nj, 16, 128).transpose(0, 2, 1, 3).reshape(ni * nj * 16, 128)


PIECES = ((QKV0, 32, 12), (WO0, 32, 4), (WU0, 32, 16), (WD0, 128, 4))


def gather_plain(aligned):
    full = lax.all_gather(aligned.reshape(-1, 128), "ta", axis=0, tiled=True)
    return jnp.concatenate(
        [tiles_of(full[16 * b : 16 * (b + ni * nj)], ni, nj) for b, ni, nj in PIECES], axis=0
    )


def reduce_plain(tiles):
    full = jnp.concatenate([rows_of(tiles[b : b + ni * nj], ni, nj) for b, ni, nj in PIECES], axis=0)
    return lax.psum_scatter(full, "ta", scatter_dimension=0, tiled=True).astype(F32).reshape(-1)


def links(n, kind, by=1):
    pairs = []
    for i in range(n):
        if kind == "core":
            pairs.append((i, i ^ 1))
        elif kind == "z":
            pairs.append((i, (i + 8 * by) % n))
        else:
            pairs.append((i, i ^ (2 if (kind == "a") == (i % 2 == 0) else 4)))
    return pairs


def move(value, kind, by=1):
    return lax.ppermute(value, "ta", links(32, kind, by))


def after(value, *others):
    return lax.optimization_barrier((value,) + others)[0]


def reduce_fast(keep_p, keep_q, send_p, send_q, root, tree, n):
    up, uq = keep_p.astype(F32) + move(send_p, "core"), keep_q.astype(F32) + move(send_q, "core")
    root = collect_round(root, *tree[0], n)
    p1 = move(up[1].astype(BF16), "b")
    zs = [move(uq[k].astype(BF16), "z", k) for k in range(1, 4)]
    root = collect_round(after(root, up, uq), *tree[1], n)
    q = functools.reduce(jnp.add, zs, uq[0])
    p = up[0] + p1
    q1 = move(q[1].astype(BF16), "b")
    p1 = move(p[1].astype(BF16), "a")
    root = collect_round(after(root, p, q), *tree[2], n)
    q, p = q[0] + q1, p[0] + p1
    q1 = move(q[1].astype(BF16), "a")
    zs = [move(p[k].astype(BF16), "z", k) for k in range(1, 4)]
    root = after(root, q, p)
    p = functools.reduce(jnp.add, zs, p[0])
    return jnp.concatenate([p, q[0] + q1], axis=0), root


def to_tiles(rows, me):
    third = 3 * me + jnp.arange(3).reshape(3, 1, 1, 1)
    qkv = tiles_of(rows, 4, 12).reshape(3, 16, 16, 128)
    four = rows.reshape(3, 4, 16, 4, 128).transpose(0, 1, 3, 2, 4).reshape(3, 16, 16, 128)
    wide = rows.reshape(3, 16, 16, 128).transpose(0, 2, 1, 3)
    out = jnp.where(third < 24, qkv, jnp.where((third >= 32) & (third < 64), wide, four))
    return out.reshape(48, 16, 128)


def to_rows(tiles, me):
    third = 3 * me + jnp.arange(3).reshape(3, 1, 1)
    qkv = rows_of(tiles, 4, 12).reshape(3, 256, 128)
    four = tiles.reshape(3, 4, 4, 16, 128).transpose(0, 1, 3, 2, 4).reshape(3, 256, 128)
    wide = tiles.reshape(3, 16, 16, 128).transpose(0, 2, 1, 3).reshape(3, 256, 128)
    out = jnp.where(third < 24, qkv, jnp.where((third >= 32) & (third < 64), wide, four))
    return out.reshape(-1)


def per_device(frames, cotangent, mem_index, master, moment, second, average):
    n = lax.axis_size("ta")
    me = lax.axis_index("ta")
    layers, share = master.shape
    step = 2 * D // n
    tail = shift(master[:, share - 2 * D :], 1, n)
    ext = jnp.concatenate([tail, master], axis=1)
    aligned = lax.dynamic_slice(ext, (0, 2 * D - step * me), (layers, MATS // n)).astype(BF16)
    gains = master[:, share - 2 * D :].astype(BF16).reshape(1, 16, 128)
    fast = n == GROUPS
    summ = run(first_kernel, sds((NSEG, D), BF16), (frames,))
    ahead = shift(jnp.concatenate([frames[TOK - LH :], summ], axis=0), 1, n)
    halo, behind2 = (ahead, shift(frames[:RH], -1, n)), shift(summ, 2, n)
    if fast:
        tiles = [to_tiles(aligned[l].reshape(-1, 128), me) for l in range(layers)]
        block = jnp.concatenate([tiles[0], gains])
        p, q = block[:PT], block[PT:]
        root = jnp.where(me == 0, summ, jnp.zeros_like(summ))
        (s0, r0), (s1, r1), (s2, r2) = strides(n)
        own = [p] + [move(p, "z", k) for k in range(1, 4)]
        qa, qb = move(q, "a"), move(q, "b")
        root = spread_round(root, s0, r0, n)
        own = after(jnp.stack(own), root)
        pa, pb = move(own, "a"), move(own, "b")
        qs = jnp.stack([q, qa, qb, move(qa, "b")])
        root = spread_round(root, s1, r1, n)
        pa = after(pa, root)
        pab = move(pa, "b")
        qs = after(qs, root)
        qz = [qs] + [move(qs, "z", k) for k in range(1, 4)]
        ps = [own, pa, pb, pab]
        root = spread_round(root, s2, r2, n)
        weights = [tuple(ps + [move(v, "core") for v in ps] + qz + [move(v, "core") for v in qz])]
        for l in range(1, layers):
            weights.append((lax.all_gather(after(tiles[l], own, pa), "ta", axis=0, tiled=True),))
    else:
        weights = [(gather_plain(aligned[l]),) for l in range(layers)]
        weights[0] += (from_first(gains[0], me, n, n - 1),)
        root = from_first(summ, me, n)
    wscr = [pltpu.VMEM((TILES, 16, 128), BF16), pltpu.SemaphoreType.DMA((2, GROUPS + 1))]
    mev = me.astype(jnp.int32).reshape(1)

    first_seg = me * NSEG
    seg_ids = first_seg + jnp.arange(NSEG, dtype=jnp.int32)
    slot = jnp.arange(MEM, dtype=jnp.int32)
    loc = jnp.where(slot[None, :] == 0, mem_index, mem_index - first_seg + 96).reshape(-1, 1)
    loc = jnp.broadcast_to(loc, (NSEG * MEM, 128))
    vis = (mem_index < seg_ids[:, None]).astype(F32).reshape(-1, 1)
    vis = jnp.broadcast_to(vis, (NSEG * MEM, 128))

    def vmem(*shape_types):
        return [pltpu.VMEM(shape, dtype) for shape, dtype in shape_types]

    tf, tb = ((TOK, D), F32), ((TOK, D), BF16)
    wide, rows16, kv16 = ((TOK, FF), BF16), ((ROWS, D), BF16), ((ROWS, 2 * D), BF16)
    prob, rows32, kv32 = ((NBLK * 4, KB, 128), BF16), ((ROWS, D), F32), ((ROWS, 2 * D), F32)
    drow, dtab_t = ((1, D), F32), ((128, D), F32)

    def call(kernel, ins, specs, outs, scratch, aliases=None, flops=3 * 10**9):
        return run(
            kernel, tuple(sds(*o) for o, _ in outs), tuple(ins), specs=specs,
            out_specs=tuple(VM if keep else ANYS for _, keep in outs), scratch=scratch,
            aliases=aliases, flops=flops, nbytes=10**7,
        )

    def sems(count):
        return [pltpu.SemaphoreType.DMA((count,))]

    saved = (rows16, tb, kv16, prob, tb, tf, tb, wide, wide)
    low = call(
        functools.partial(low_kernel, np_=len(weights[0]), n=n),
        (mev, frames, *halo, root, behind2, summ, loc, vis) + weights[0],
        [SM] + [VM] * 8 + [ANYS] * len(weights[0]),
        [(tf, True), (tb, True), (((NSEG, D), BF16), True), (((16, 128), BF16), True)] + [(t, False) for t in saved],
        wscr + vmem(*saved) + sems(9),
    )
    x1, h1, summ, gt, hx0, q0, kv0, p0, o0, a0, h20, gp0, act0 = low
    halo = (shift(jnp.concatenate([h1[TOK - LH :], summ], axis=0), 1, n), shift(h1[:RH], -1, n))
    behind2 = shift(summ, 2, n)
    root = from_first(summ, me, n)
    top = call(
        functools.partial(top_kernel, np_=len(weights[1]), n=n),
        (mev, x1, h1, *halo, root, behind2, summ, loc, vis, gt, cotangent) + weights[1],
        [SM] + [VM] * 10 + [ANYS] * (1 + len(weights[1])),
        [(tf, False), (tf, True), (rows32, True), (dtab_t, True), (drow, True)]
        + [(t, False) for t in (rows16, tb, tb, wide, tb, wide, tb, tb, kv16)],
        wscr + vmem(rows16, tb, kv16, prob, tb, tf, tb, wide, wide, tf, tf, tb, wide, tb, tb, kv16, kv32, tb) + sems(11),
        flops=8 * 10**9,
    )
    output, da, dh, dtab, dgb1, hx1, o1, h21, act1, dxb, dub, dab, dq, dkvb = top
    dws = vmem(rows16, tb, kv16, tb, tb, tb, wide, wide, tb, ((TILES, 16, 128), BF16))
    dws += [pltpu.SemaphoreType.DMA] + sems(9)
    tree = strides(n)[::-1]

    def backward_moves(dh, dtab):
        behind = shift(jnp.concatenate([dh[:LH], dtab[64:96]], axis=0), -1, n)
        return behind, shift(dh[LH + TOK : LH + TOK + RH], 1, n), shift(dtab[32:64], -2, n)

    hal, har, b2 = backward_moves(dh, dtab)
    root = dtab[:NSEG]
    plain = (((TILES, 16, 128), BF16), False)
    ins = [mev, hx1, dq, dkvb, o1, dab, h21, dub, act1, dxb]
    half = call(
        functools.partial(dw_kernel, part=0, nouts=1), ins, [SM] + [ANYS] * 9, [plain], dws, flops=2 * 10**9
    )
    root = collect_round(root, *tree[0], n)
    ins[-1] = after(dxb, root, hal, har, b2)
    root = after(root, half[0])
    grads = call(
        functools.partial(dw_kernel, part=1, nouts=1), ins + list(half), [SM] + [ANYS] * 10, [plain], dws,
        aliases={10: 0}, flops=10**9,
    )
    for level in tree[1:]:
        root = collect_round(root, *level, n)
    reduced = [None] * layers
    if fast:
        part = lax.psum_scatter(grads[0], "ta", scatter_dimension=0, tiled=True)
        reduced[1] = to_rows(part.astype(F32), me)
    else:
        reduced[1] = reduce_plain(grads[0])
    bottom = call(
        functools.partial(bottom_kernel, np_=len(weights[0])),
        (mev, hal, har, root, b2, dtab, dh, x1, da, loc, gt) + weights[0] + (q0, kv0, p0, a0, gp0),
        [SM] + [VM] * 10 + [ANYS] * (len(weights[0]) + 5),
        [(drow, True), (tf, True), (rows32, True), (dtab_t, True), (drow, True)]
        + [(t, False) for t in (tb, wide, tb, tb, kv16)],
        wscr + vmem(tb, kv16, prob, tf, wide, tf, tb, wide, tb, tb, kv16, kv32, tb) + sems(10),
        flops=5 * 10**9,
    )
    dga1, da, dh, dtab, dgb0, dxb, dub, dab, dq, dkvb = bottom
    if fast:
        pq = [(((2, 2, 4, PT, 16, 128), BF16), False), (((4, 2, 2, BT - PT, 16, 128), BF16), False)]
        gouts = pq + pq
    else:
        gouts = [plain]
    grads = call(
        functools.partial(dw_kernel, part=None, nouts=len(gouts)),
        (mev, hx0, dq, dkvb, o0, dab, h20, dub, act0, dxb), [SM] + [ANYS] * 9, gouts, dws,
    )
    hal, har, b2 = backward_moves(dh, dtab)
    root = dtab[:NSEG]
    if fast:
        total, root = reduce_fast(*grads, root, tree, n)
        reduced[0] = to_rows(total, me)
    else:
        reduced[0] = reduce_plain(grads[0])
        for level in tree:
            root = collect_round(root, *level, n)
    dx, dga0 = call(
        functools.partial(last_kernel), (mev, hal, har, root, b2, dtab, dh, frames, da, gt),
        [SM] + [VM] * 9, [(tf, True), (drow, True)], vmem(tf), flops=10**7,
    )
    gain_rows = [jnp.concatenate([dga0, dgb0], axis=1), jnp.concatenate([dga1, dgb1], axis=1)]

    gsum = sum_all(jnp.concatenate(gain_rows, axis=0), n)
    own = jnp.stack(reduced)
    head = jnp.where(me == n - 1, gsum, shift(own[:, : 2 * D], -1, n))
    grad = lax.dynamic_slice(jnp.concatenate([own, head], axis=1), (0, step * me), (layers, share))
    gain_out = lax.dynamic_slice(gsum, (0, step * me), (layers, step))
    new_moment = 0.5 * moment + 0.5 * grad
    new_second = 0.5 * second + 0.5 * grad * grad
    correction = 1.0 - 0.5**STEP
    update = new_moment / correction / (jnp.sqrt(new_second / correction) + 1e-08) + 0.1 * master
    new_master = master - 0.08 * update
    new_average = 0.9 * average + 0.1 * new_master
    return (output, dx, gain_out, new_moment, new_second, new_master, new_average)


def solution(mesh):
    rows, flat = P("ta", None), P(None, "ta")
    return jax.shard_map(
        per_device,
        mesh=mesh,
        in_specs=(rows, rows, rows, flat, flat, flat, flat),
        out_specs=(rows, rows, flat, flat, flat, flat, flat),
        check_vma=False,
    )
```

```python
import functools

import jax
import jax.numpy as jnp
from jax import lax
from jax.experimental import pallas as pl
from jax.experimental.pallas import tpu as pltpu
from jax.sharding import PartitionSpec as P

D = 512
HEADS = 8
FF = 2048
SEG = 16
LEFT = 30
RIGHT = 4
MEM = 4
STEP = 10
UN = 4
NEG = -1e30

TOK = 512
NSEG = TOK // SEG
LH = 32
RH = 16
EXT = LH + TOK + 2 * RH
ROWS = EXT + NSEG * MEM
BLK = 4
NBLK = NSEG // BLK
QB = BLK * SEG
KB = 128
WB = KB - BLK * MEM

TILES = 1536
QKV0, WO0, WU0, WD0 = 0, 384, 512, 1024
MATS = TILES * 16 * 128
GROUPS = 32
BT = TILES // GROUPS

F32 = jnp.float32
BF16 = jnp.bfloat16
VM = pl.BlockSpec(memory_space=pltpu.VMEM)
SM = pl.BlockSpec(memory_space=pltpu.SMEM)
ANYS = pl.BlockSpec(memory_space=pl.ANY)


def mm(a, b):
    return lax.dot_general(a, b, (((1,), (0,)), ((), ())), preferred_element_type=F32)


def mm_nt(a, b):
    return lax.dot_general(a, b, (((1,), (1,)), ((), ())), preferred_element_type=F32)


def mm_tn(a, b):
    return lax.dot_general(a, b, (((0,), (0,)), ((), ())), preferred_element_type=F32)


def wblk(w, base, nj, i0, ni, j0, nj_take):
    cols = [
        jnp.concatenate([w[base + (i0 + i) * nj + j0 + j] for i in range(ni)], axis=0)
        for j in range(nj_take)
    ]
    return cols[0] if nj_take == 1 else jnp.concatenate(cols, axis=1)


def place(me, rc, ra, rb, k):
    core = (me % 2) ^ rc
    x = ((me // 2) % 2) ^ jnp.where(core == 0, ra, rb)
    y = ((me // 4) % 2) ^ jnp.where(core == 0, rb, ra)
    z = (me // 8 + k) % 4
    return ((z * 2 + y) * 2 + x) * 2 + core


def load_weights(me, pieces, w_ref, sems, lo, hi, gt_ref=None):
    if len(pieces) < 8:
        if gt_ref is not None:
            pltpu.make_async_copy(pieces[1], gt_ref, sems.at[GROUPS]).start()
        for d in range(lo, hi):
            t = pl.ds(BT * d, BT)
            pltpu.make_async_copy(pieces[0].at[t], w_ref.at[t], sems.at[d]).start()
        return
    for rc in range(2):
        for m in range(4):
            for k in range(4):
                d = place(me, rc, m % 2, m // 2, -k % 4)
                piece = pieces[4 * rc + m].at[k]

                @pl.when((d >= lo) & (d < hi))
                def _():
                    pltpu.make_async_copy(
                        piece.at[pl.ds(0, BT)], w_ref.at[pl.ds(d * BT, BT)], sems.at[d]
                    ).start()

                if gt_ref is not None:

                    @pl.when(d == GROUPS - 1)
                    def _():
                        pltpu.make_async_copy(piece.at[BT], gt_ref, sems.at[GROUPS]).start()


def await_weights(w_ref, sems, lo, hi):
    for d in range(lo, hi):
        part = w_ref.at[pl.ds(d * BT, BT)]
        pltpu.make_async_copy(part, part, sems.at[d]).wait()


def gain_row(g_ref, layer, which):
    g = g_ref[...].astype(F32)
    r = 8 * layer + 4 * which
    return jnp.concatenate([g[r + k : r + k + 1] for k in range(4)], axis=1)


def norm_parts(v):
    mean = jnp.mean(v, axis=-1, keepdims=True)
    cen = v - mean
    rstd = lax.rsqrt(jnp.mean(cen * cen, axis=-1, keepdims=True) + 1e-05)
    return cen * rstd, rstd


def norm_back(dh, xhat, rstd, gain):
    dx = dh * gain
    return rstd * (
        dx
        - jnp.mean(dx, axis=-1, keepdims=True)
        - xhat * jnp.mean(dx * xhat, axis=-1, keepdims=True)
    )


def seg_mean(h):
    return (jnp.sum(h.astype(F32).reshape(NSEG, SEG, D), axis=1) * (1.0 / SEG)).astype(BF16)


def head_of_layer(x, gain):
    xhat, _ = norm_parts(x)
    h1 = (xhat * gain).astype(BF16)
    return h1, seg_mean(h1)


def send_on(me, rows_ref, means, ahead_ref, back_ref, root_ref, sum_ref):
    sum_ref[...] = means
    ahead_ref[0:LH] = rows_ref[TOK - LH : TOK]
    ahead_ref[LH:] = means
    back_ref[...] = rows_ref[0:RH]
    root_ref[...] = jnp.where(me == 0, means, jnp.zeros_like(means))


def first_kernel(me_ref, x_ref, ahead_ref, back_ref, root_ref, sum_ref):
    xhat, _ = norm_parts(x_ref[...].astype(F32))
    send_on(me_ref[0], x_ref, seg_mean(xhat), ahead_ref, back_ref, root_ref, sum_ref)


def lane_lo(rows):
    return lax.broadcasted_iota(jnp.int32, (rows, 128), 1) < 64


def split_heads(m, lo):
    z = jnp.zeros_like(m)
    return jnp.concatenate([jnp.where(lo, m, z), jnp.where(lo, z, m)], axis=0)


def onehot_of(loc_ref):
    ids = lax.broadcasted_iota(jnp.int32, (NSEG * MEM, 128), 1)
    return jnp.where(loc_ref[...] == ids, 1.0, 0.0).astype(BF16)


def block_keys(kv_ref, b, col):
    r0 = pl.multiple_of(b * QB, QB)
    m0 = pl.multiple_of(EXT + b * (BLK * MEM), BLK * MEM)
    return jnp.concatenate(
        [kv_ref[pl.ds(r0, WB), col : col + 128], kv_ref[pl.ds(m0, BLK * MEM), col : col + 128]], axis=0
    )


def attend(me, n, q_ref, kv_ref, vis_ref, p_ref, o_ref, s_ref):
    ki = lax.broadcasted_iota(jnp.int32, (KB, 128), 0)
    qi = (lax.broadcasted_iota(jnp.int32, (KB, 128), 1) % QB) // SEG
    off = ki - SEG * qi - (LH - LEFT)
    near = jnp.where((off >= 0) & (off < LEFT + SEG + RIGHT) & (ki < WB), 1.0, 0.0)
    memb = jnp.where((ki >= WB) & ((ki - WB) // MEM == qi), 1.0, 0.0)
    first = jnp.where(me == 0, LH, 0)
    end = jnp.where(me == n - 1, LH + TOK, EXT)
    lo = lane_lo(QB)

    def scores(b, carry):
        r0 = pl.multiple_of(b * QB, QB)
        m0 = pl.multiple_of(b * (BLK * MEM), BLK * MEM)
        inside = (ki + r0 >= first) & (ki + r0 < end)
        memv = jnp.concatenate(
            [jnp.zeros((WB, 128), F32), vis_ref[pl.ds(m0, BLK * MEM), :]], axis=0
        )
        seen = jnp.where(inside, near, 0.0) + memb * memv > 0.5
        for p in range(4):
            kc = block_keys(kv_ref, b, 128 * p)
            s = mm_nt(kc, split_heads(q_ref[pl.ds(r0, QB), 128 * p : 128 * p + 128], lo))
            s_ref[b * 4 + p] = jnp.where(seen, s, NEG)
        return carry

    def softmax(i, carry):
        s = s_ref[i]
        e = jnp.exp(s - jnp.max(s, axis=0, keepdims=True))
        p_ref[i] = (e * (1.0 / jnp.sum(e, axis=0, keepdims=True))).astype(BF16)
        return carry

    def mix(b, carry):
        r0 = pl.multiple_of(b * QB, QB)
        for p in range(4):
            o2 = mm_tn(p_ref[b * 4 + p], block_keys(kv_ref, b, D + 128 * p))
            o_ref[pl.ds(r0, QB), 128 * p : 128 * p + 128] = jnp.where(lo, o2[:QB], o2[QB:]).astype(BF16)
        return carry

    lax.fori_loop(0, NBLK, scores, 0, unroll=UN)
    lax.fori_loop(0, 4 * NBLK, softmax, 0, unroll=4)
    lax.fori_loop(0, NBLK, mix, 0, unroll=UN)


def attend_back(q_ref, kv_ref, p_ref, do_ref, dq_ref, dkv_ref, s_ref):
    dkv_ref[...] = jnp.zeros_like(dkv_ref)
    lo = lane_lo(QB)

    def weights(b, carry):
        r0 = pl.multiple_of(b * QB, QB)
        m0 = pl.multiple_of(EXT + b * (BLK * MEM), BLK * MEM)
        for p in range(4):
            vc0 = D + 128 * p
            dd = split_heads(do_ref[pl.ds(r0, QB), 128 * p : 128 * p + 128], lo)
            s_ref[b * 4 + p] = mm_nt(block_keys(kv_ref, b, vc0), dd)
            dv = mm(p_ref[b * 4 + p], dd)
            dkv_ref[pl.ds(r0, WB), vc0 : vc0 + 128] += dv[:WB]
            dkv_ref[pl.ds(m0, BLK * MEM), vc0 : vc0 + 128] = dv[WB:]
        return carry

    def softmax(i, carry):
        pf = p_ref[i].astype(F32)
        pd = pf * s_ref[i]
        p_ref[i] = (pd - pf * jnp.sum(pd, axis=0, keepdims=True)).astype(BF16)
        return carry

    def queries(b, carry):
        r0 = pl.multiple_of(b * QB, QB)
        m0 = pl.multiple_of(EXT + b * (BLK * MEM), BLK * MEM)
        for p in range(4):
            kc0 = 128 * p
            ds = p_ref[b * 4 + p]
            dk = mm(ds, split_heads(q_ref[pl.ds(r0, QB), kc0 : kc0 + 128], lo))
            dq2 = mm_tn(ds, block_keys(kv_ref, b, kc0))
            dq_ref[pl.ds(r0, QB), kc0 : kc0 + 128] = (jnp.where(lo, dq2[:QB], dq2[QB:]) * 0.125).astype(BF16)
            dkv_ref[pl.ds(r0, WB), kc0 : kc0 + 128] += dk[:WB]
            dkv_ref[pl.ds(m0, BLK * MEM), kc0 : kc0 + 128] = dk[WB:]
        return carry

    lax.fori_loop(0, NBLK, weights, 0, unroll=UN)
    lax.fori_loop(0, 4 * NBLK, softmax, 0, unroll=4)
    lax.fori_loop(0, NBLK, queries, 0, unroll=UN)


class Copies:
    def __init__(self, sems):
        self.sems, self.used, self.open = sems, 0, []

    def start(self, src, dst):
        copy = pltpu.make_async_copy(src, dst, self.sems.at[self.used])
        self.used += 1
        copy.start()
        return copy

    def out(self, src, dst):
        self.open.append(self.start(src, dst))

    def finish(self):
        for copy in self.open:
            copy.wait()


def project(hx_ref, w_ref, q_ref, kv_ref):
    q = mm(hx_ref[LH : LH + TOK], wblk(w_ref, QKV0, 12, 0, 32, 0, 4)).astype(BF16)
    q_ref[...] = q * jnp.asarray(0.125, BF16)
    for j in range(2):
        kv_ref[:, 512 * j : 512 * j + 512] = mm(hx_ref[...], wblk(w_ref, QKV0, 12, 0, 32, 4 + 4 * j, 4)).astype(BF16)


def feed_forward(h2_ref, w_ref, act_ref, gp_ref, out_ref, step):
    for c in range(4):
        u = mm(h2_ref[...], wblk(w_ref, WU0, 16, 0, 32, 4 * c, 4))
        cc, c3 = 0.7978845608028654, 0.7978845608028654 * 0.044715
        u2 = u * u
        t = jnp.tanh(u * (cc + c3 * u2))
        hu = 0.5 * u
        act = (hu + hu * t).astype(BF16)
        gp = 0.5 + 0.5 * t + hu * (1.0 - t * t) * (cc + 3 * c3 * u2)
        act_ref[:, 512 * c : 512 * c + 512] = act
        gp_ref[:, 512 * c : 512 * c + 512] = gp.astype(BF16)
        out_ref[...] += mm(act, wblk(w_ref, WD0, 4, 32 * c, 32, 0, 4))
        step(c)


def back_ffn(dx_ref, w_ref, gains, a_ref, gp_ref, da_ref, dxb_ref, dub_ref, dab_ref, dgb_ref, step):
    dxb_ref[...] = dx_ref[...].astype(BF16)
    step("dxb")
    for c in range(4):
        dact = mm_nt(dxb_ref[...], wblk(w_ref, WD0, 4, 32 * c, 32, 0, 4))
        du = (dact * gp_ref[:, 512 * c : 512 * c + 512].astype(F32)).astype(BF16)
        dub_ref[:, 512 * c : 512 * c + 512] = du
        dh2 = mm_nt(du, wblk(w_ref, WU0, 16, 0, 32, 4 * c, 4))
        if c:
            da_ref[...] += dh2
        else:
            da_ref[...] = dh2
    step("dub")
    xhat, rstd = norm_parts(a_ref[...])
    dh2 = da_ref[...]
    dgb_ref[...] = jnp.sum(dh2 * xhat, axis=0, keepdims=True)
    da = dx_ref[...] + norm_back(dh2, xhat, rstd, gains)
    da_ref[...] = da
    dab_ref[...] = da.astype(BF16)
    step("dab")


def back_attn(dab_ref, w_ref, q_ref, kv_ref, p_ref, dq_ref, dkvb_ref, dh_ref, dkv_ref, dob_ref, s_ref, step):
    dob_ref[...] = mm_nt(dab_ref[...], wblk(w_ref, WO0, 4, 0, 32, 0, 4)).astype(BF16)
    step("attend")
    attend_back(q_ref, kv_ref, p_ref, dob_ref, dq_ref, dkv_ref, s_ref)
    dkvb_ref[...] = dkv_ref[...].astype(BF16)
    step("dkvb")
    dh_ref[...] = mm_nt(dkvb_ref[...], wblk(w_ref, QKV0, 12, 0, 32, 4, 8))
    dh_ref[LH : LH + TOK] += mm_nt(dq_ref[...], wblk(w_ref, QKV0, 12, 0, 32, 0, 4))


def table_grad(loc_ref, dh_ref, hal_ref, har_ref, root_ref, b2_ref, mine_ref):
    dch = dh_ref[EXT:ROWS]
    hi = dch.astype(BF16)
    oh = onehot_of(loc_ref)
    dtab = mm_tn(oh, hi) + mm_tn(oh, (dch - hi.astype(F32)).astype(BF16))
    hal_ref[0:LH] = dh_ref[0:LH]
    hal_ref[LH:] = dtab[64:96]
    har_ref[...] = dh_ref[LH + TOK : LH + TOK + RH]
    root_ref[...] = dtab[0:32]
    b2_ref[...] = dtab[32:64]
    mine_ref[...] = dtab[96:128]
    return dtab


def low_attn_kernel(me_ref, x_ref, hl_ref, hr_ref, root_ref, b2_ref, summ_ref, loc_ref, vis_ref, *rest, np_, n):
    pieces, rest = rest[:np_], rest[np_:]
    gt_ref, hx_o, q_o, kv_o, p_o, o_o, w_ref, sems, hx_ref, q_ref, kv_ref, p_ref, o_ref, s_ref, osem = rest
    me = me_ref[0]
    load_weights(me, pieces, w_ref, sems, 0, 8, gt_ref)
    copies = Copies(osem)
    pltpu.make_async_copy(gt_ref, gt_ref, sems.at[GROUPS]).wait()
    ga = gain_row(gt_ref, 0, 0)
    for ref, rows, at in ((hl_ref, LH, 0), (x_ref, TOK, LH), (hr_ref, RH, LH + TOK)):
        xhat, _ = norm_parts(ref[0:rows].astype(F32))
        hx_ref[at : at + rows] = (xhat * ga).astype(BF16)
    means = jnp.concatenate([root_ref[...], b2_ref[...], hl_ref[LH:], summ_ref[...]], axis=0)
    hx_ref[LH + TOK + RH : EXT] = jnp.zeros((RH, D), BF16)
    hx_ref[EXT:ROWS] = mm(onehot_of(loc_ref), (means.astype(F32) * ga).astype(BF16)).astype(BF16)
    copies.out(hx_ref, hx_o)
    await_weights(w_ref, sems, 0, 8)
    project(hx_ref, w_ref, q_ref, kv_ref)
    copies.out(q_ref, q_o)
    copies.out(kv_ref, kv_o)
    attend(me, n, q_ref, kv_ref, vis_ref, p_ref, o_ref, s_ref)
    copies.out(p_ref, p_o)
    copies.out(o_ref, o_o)
    copies.finish()


def low_ffn_kernel(me_ref, x_ref, o_ref, gt_ref, *rest, np_):
    pieces, rest = rest[:np_], rest[np_:]
    (out_ref, h1n_ref, ahead_ref, back_ref, root_ref, sumn_ref, a_o, h2_o, gp_o, act_o,
     w_ref, sems, a_ref, h2_ref, gp_ref, act_ref, osem) = rest
    load_weights(me_ref[0], pieces, w_ref, sems, 8, 32)
    copies = Copies(osem)
    await_weights(w_ref, sems, 8, 11)
    a = x_ref[...].astype(F32) + mm(o_ref[...], wblk(w_ref, WO0, 4, 0, 32, 0, 4))
    a_ref[...] = a
    copies.out(a_ref, a_o)
    xhat, _ = norm_parts(a)
    h2_ref[...] = (xhat * gain_row(gt_ref, 0, 1)).astype(BF16)
    copies.out(h2_ref, h2_o)
    out_ref[...] = a
    await_weights(w_ref, sems, 11, 32)
    feed_forward(h2_ref, w_ref, act_ref, gp_ref, out_ref, lambda c: None)
    copies.out(act_ref, act_o)
    copies.out(gp_ref, gp_o)
    h1n, sumn = head_of_layer(out_ref[...], gain_row(gt_ref, 1, 0))
    h1n_ref[...] = h1n
    send_on(me_ref[0], h1n_ref, sumn, ahead_ref, back_ref, root_ref, sumn_ref)
    copies.finish()


def top_kernel(me_ref, x_ref, h1_ref, hl_ref, hr_ref, root_ref, b2_ref, summ_ref, loc_ref, vis_ref, gt_ref, cot_any,
               *rest, np_, n):
    pieces, rest = rest[:np_], rest[np_:]
    (out_o, da_ref, dhown_ref, hal_ref, har_ref, rootg_ref, b2g_ref, mine_ref, dgb_ref, hx_o, o_o, h2_o, act_o, dxb_o, dub_o, dab_o, dq_o, dkvb_o,
     w_ref, sems, hx_ref, q_ref, kv_ref, p_ref, o_ref, a_ref, h2_ref, gp_ref, act_ref,
     out_ref, dx_ref, dxb_ref, dub_ref, dab_ref, dq_ref, dkvb_ref, dkv_ref, dob_ref, dh_ref, s_ref, osem) = rest
    me = me_ref[0]
    load_weights(me, pieces, w_ref, sems, 0, 32)
    copies = Copies(osem)
    cot = copies.start(cot_any, dx_ref)
    hx_ref[0:LH] = hl_ref[0:LH]
    hx_ref[LH : LH + TOK] = h1_ref[...]
    hx_ref[LH + TOK : LH + TOK + RH] = hr_ref[...]
    hx_ref[LH + TOK + RH : EXT] = jnp.zeros((RH, D), BF16)
    table = jnp.concatenate([root_ref[...], b2_ref[...], hl_ref[LH:], summ_ref[...]], axis=0)
    hx_ref[EXT:ROWS] = mm(onehot_of(loc_ref), table).astype(BF16)
    copies.out(hx_ref, hx_o)
    await_weights(w_ref, sems, 0, 8)
    project(hx_ref, w_ref, q_ref, kv_ref)
    attend(me, n, q_ref, kv_ref, vis_ref, p_ref, o_ref, s_ref)
    copies.out(o_ref, o_o)
    await_weights(w_ref, sems, 8, 32)
    a = x_ref[...] + mm(o_ref[...], wblk(w_ref, WO0, 4, 0, 32, 0, 4))
    a_ref[...] = a
    xhat, _ = norm_parts(a)
    h2_ref[...] = (xhat * gain_row(gt_ref, 1, 1)).astype(BF16)
    copies.out(h2_ref, h2_o)
    out_ref[...] = a
    feed_forward(h2_ref, w_ref, act_ref, gp_ref, out_ref, lambda c: None)
    copies.out(act_ref, act_o)
    copies.out(out_ref, out_o)
    cot.wait()
    done = {"dxb": ((dxb_ref, dxb_o),), "dub": ((dub_ref, dub_o),), "dab": ((dab_ref, dab_o),),
            "dkvb": ((dkvb_ref, dkvb_o), (dq_ref, dq_o))}

    def step(name):
        for pair in done.get(name, ()):
            copies.out(*pair)

    back_ffn(dx_ref, w_ref, gain_row(gt_ref, 1, 1), a_ref, gp_ref, da_ref, dxb_ref, dub_ref, dab_ref, dgb_ref, step)
    back_attn(dab_ref, w_ref, q_ref, kv_ref, p_ref, dq_ref, dkvb_ref, dh_ref, dkv_ref, dob_ref, s_ref, step)
    dhown_ref[...] = dh_ref[LH : LH + TOK]
    table_grad(loc_ref, dh_ref, hal_ref, har_ref, rootg_ref, b2g_ref, mine_ref)
    copies.finish()


def norm_one_back(dh_ref, hal_ref, har_ref, dsum, x, gain, da_ref, acc_ref):
    acc_ref[...] = dh_ref[...]
    acc_ref[TOK - LH : TOK] += hal_ref[0:LH]
    acc_ref[0:RH] += har_ref[...]
    for s in range(NSEG):
        acc_ref[SEG * s : SEG * s + SEG] += dsum[s : s + 1, :] * (1.0 / SEG)
    xhat, rstd = norm_parts(x)
    dh = acc_ref[...]
    return da_ref[...] + norm_back(dh, xhat, rstd, gain), jnp.sum(dh * xhat, axis=0, keepdims=True)


def summed(me_ref, hal_ref, root_ref, b2_ref, mine_ref):
    return mine_ref[...] + hal_ref[LH:] + b2_ref[...] + jnp.where(me_ref[0] == 0, root_ref[...], 0.0)


def bottom_ffn_kernel(me_ref, hal_ref, har_ref, root_ref, b2_ref, dtabp_ref, dhp_ref, x_ref, dap_ref, gt_ref, *rest, np_):
    pieces, rest = rest[:np_], rest[np_:]
    (a_any, gp_any, dga_ref, da_ref, dgb_ref, dxb_o, dub_o, dab_o,
     w_ref, sems, a_ref, gp_ref, dx_ref, dxb_ref, dub_ref, dab_ref, osem) = rest
    load_weights(me_ref[0], pieces, w_ref, sems, 10, 32)
    copies = Copies(osem)
    loads = [copies.start(*pair) for pair in ((gp_any, gp_ref), (a_any, a_ref))]
    dx, dga = norm_one_back(
        dhp_ref, hal_ref, har_ref, summed(me_ref, hal_ref, root_ref, b2_ref, dtabp_ref), x_ref[...],
        gain_row(gt_ref, 1, 0), dap_ref, dx_ref,
    )
    dx_ref[...] = dx
    dga_ref[...] = dga
    await_weights(w_ref, sems, 10, 32)
    loads[0].wait()
    done = {"dxb": (dxb_ref, dxb_o), "dub": (dub_ref, dub_o), "dab": (dab_ref, dab_o)}

    def step(name):
        if name == "dub":
            loads[1].wait()
        copies.out(*done[name])

    back_ffn(dx_ref, w_ref, gain_row(gt_ref, 0, 1), a_ref, gp_ref, da_ref, dxb_ref, dub_ref, dab_ref, dgb_ref, step)
    copies.finish()


def bottom_attn_kernel(me_ref, dab_ref, loc_ref, frames_ref, ahead0_ref, hr0_ref, root0_ref, b20_ref, summ0_ref, *rest, np_):
    pieces, rest = rest[:np_], rest[np_:]
    (q_any, kv_any, p_any, dga_ref, dhown_ref, hal_ref, har_ref, rootg_ref, b2g_ref, mine_ref, dq_o, dkvb_o,
     w_ref, sems, q_ref, kv_ref, p_ref, dq_ref, dkvb_ref, dkv_ref, dob_ref, dh_ref, s_ref, osem) = rest
    load_weights(me_ref[0], pieces, w_ref, sems, 0, 11)
    copies = Copies(osem)
    loads = [copies.start(*pair) for pair in ((q_any, q_ref), (kv_any, kv_ref), (p_any, p_ref))]
    await_weights(w_ref, sems, 0, 11)

    def step(name):
        if name == "attend":
            for load in loads:
                load.wait()
        else:
            copies.out(dkvb_ref, dkvb_o)
            copies.out(dq_ref, dq_o)

    back_attn(dab_ref, w_ref, q_ref, kv_ref, p_ref, dq_ref, dkvb_ref, dh_ref, dkv_ref, dob_ref, s_ref, step)
    dhown_ref[...] = dh_ref[LH : LH + TOK]
    dtab = table_grad(loc_ref, dh_ref, hal_ref, har_ref, rootg_ref, b2g_ref, mine_ref)
    means = jnp.concatenate([root0_ref[...], b20_ref[...], ahead0_ref[LH:], summ0_ref[...]], axis=0)
    total = jnp.sum(dtab * means.astype(F32), axis=0, keepdims=True)
    for ref, rows, at in ((ahead0_ref, LH, 0), (frames_ref, TOK, LH), (hr0_ref, RH, LH + TOK)):
        xhat, _ = norm_parts(ref[0:rows].astype(F32))
        total += jnp.sum(dh_ref[at : at + rows] * xhat, axis=0, keepdims=True)
    dga_ref[...] = total
    copies.finish()


def last_kernel(me_ref, hal_ref, har_ref, root_ref, b2_ref, dtab_ref, dh_ref, x_ref, da_ref, gt_ref, dx_ref, acc_ref):
    dx, _ = norm_one_back(
        dh_ref, hal_ref, har_ref, summed(me_ref, hal_ref, root_ref, b2_ref, dtab_ref), x_ref[...].astype(F32),
        gain_row(gt_ref, 0, 0), da_ref, acc_ref,
    )
    dx_ref[...] = dx


def dw_kernel(me_ref, *rest, part, nouts, gains=False):
    srcs, rest = rest[:9], rest[9:]
    if gains:
        gain_ref, rest = rest[0], rest[1:]
    outs, rest = rest[-12 - nouts : -12], rest[-12:]
    hx_ref, dq_ref, dkv_ref, o_ref, dab_ref, h2_ref, dub_ref, act_ref, dxb_ref, g_ref, sem, isem = rest
    copies = Copies(isem)
    loads = {}
    for i in {0: (7, 8), 1: (5, 6), 2: (3, 4, 0, 1, 2)}[part]:
        loads[i] = copies.start(srcs[i], rest[i])

    def put(val, base, nj, i0, j0):
        v = val.astype(BF16)
        for i in range(val.shape[0] // 16):
            for j in range(val.shape[1] // 128):
                g_ref[base + (i0 + i) * nj + j0 + j] = v[16 * i : 16 * i + 16, 128 * j : 128 * j + 128]

    def send(lo, hi):
        if nouts == 1:
            tiles = pl.ds(lo * 16, (hi - lo) * 16)
            pltpu.make_async_copy(g_ref.at[tiles], outs[0].at[tiles], sem).start()
            return
        me = me_ref[0]
        units = {}
        for u in range(lo, hi):
            units.setdefault(u // 3, []).append(u % 3)
        for d, thirds in units.items():
            core = d % 2
            rx, ry = ((me // 2) % 2) ^ (d // 2 % 2), ((me // 4) % 2) ^ (d // 4 % 2)
            ra, rb = (rx, ry) if core == 0 else (ry, rx)
            k = (d // 8 - me // 8 + 4) % 4
            t0, t1 = 16 * thirds[0], 16 * thirds[-1] + 16
            for rc in range(2):

                @pl.when((me % 2) ^ core == rc)
                def _():
                    pltpu.make_async_copy(
                        g_ref.at[pl.ds(d * BT + t0, t1 - t0)], outs[rc].at[rb, ra, k, pl.ds(t0, t1 - t0)], sem
                    ).start()

    if part == 0:
        loads[7].wait()
        loads[8].wait()

        def down(c, carry):
            c0 = pl.multiple_of(c * 256, 256)
            put(mm_tn(act_ref[:, pl.ds(c0, 256)], dxb_ref[...]), WD0, 4, 16 * c, 0)
            return carry

        lax.fori_loop(0, FF // 256, down, 0)
        send(64, 96)
    if part == 1:
        loads[5].wait()
        loads[6].wait()

        def up(c, carry):
            c0 = pl.multiple_of(c * 256, 256)
            put(mm_tn(h2_ref[...], dub_ref[:, pl.ds(c0, 256)]), WU0, 16, 0, 2 * c)
            return carry

        lax.fori_loop(0, FF // 256, up, 0)
        send(32, 64)
    if part == 2:
        for i in (3, 4, 0, 1, 2):
            loads[i].wait()
        for j in range(2):
            put(mm_tn(o_ref[...], dab_ref[:, 256 * j : 256 * j + 256]), WO0, 4, 0, 2 * j)
        send(24, 32)
        for j in range(2):
            put(mm_tn(hx_ref[LH : LH + TOK], dq_ref[:, 256 * j : 256 * j + 256]), QKV0, 12, 0, 2 * j)
        for j in range(4):
            put(mm_tn(hx_ref[...], dkv_ref[:, 256 * j : 256 * j + 256]), QKV0, 12, 0, 4 + 2 * j)
        send(0, 24)
        if gains:
            for i in range(GROUPS):
                pltpu.make_async_copy(
                    gain_ref, outs[i // 16].at[i % 2, i // 2 % 2, i // 4 % 4, BT], sem
                ).start()
            for i in range(GROUPS):
                pltpu.make_async_copy(gain_ref, gain_ref, sem).wait()
    first, count = {0: (WD0, 512), 1: (WU0, 512), 2: (0, 512)}[part]
    all_of = g_ref.at[pl.ds(first, count)]
    pltpu.make_async_copy(all_of, all_of, sem).wait()


def sds(shape, dtype):
    return jax.ShapeDtypeStruct(shape, dtype)


PARAMS = dict(vmem_limit_bytes=56 * 1024 * 1024)


def run(kernel, outs, ins, specs=None, scratch=(), flops=0, nbytes=0, aliases=None, **kw):
    return pl.pallas_call(
        kernel,
        out_shape=outs,
        input_output_aliases=aliases or {},
        in_specs=specs or [VM] * len(ins),
        out_specs=jax.tree.map(lambda _: VM, outs) if "out_specs" not in kw else kw["out_specs"],
        scratch_shapes=list(scratch),
        compiler_params=pltpu.CompilerParams(**PARAMS),
        cost_estimate=pl.CostEstimate(flops=flops, bytes_accessed=nbytes, transcendentals=0),
    )(*ins)


def shift(value, by, n):
    return lax.ppermute(value, "ta", [(i, i + by) for i in range(n) if 0 <= i + by < n])


def strides(n):
    return [(1 << k, 2) for k in reversed(range(n.bit_length() - 1))]


def spread_round(value, digit, done, n):
    stride, radix = digit
    keep = [i for i in range(n) if all(i // s % r == 0 for s, r in strides(n) if (s, r) not in done)]
    parts = [lax.ppermute(value, "ta", [(i, i + j * stride) for i in keep]) for j in range(1, radix)]
    return functools.reduce(jnp.add, parts, value)


def collect_round(value, digit, done, n):
    stride, radix = digit
    keep = [i for i in range(n) if all(i // s % r == 0 for s, r in [digit] + done)]
    parts = [lax.ppermute(value, "ta", [(i + j * stride, i) for i in keep]) for j in range(1, radix)]
    return functools.reduce(jnp.add, parts, value)


def from_first(value, me, n, root=0):
    value = jnp.where(me == root, value, jnp.zeros_like(value))
    if root:
        value = shift(value, -root, n)
    digits = strides(n)
    for i in range(len(digits)):
        value = spread_round(value, digits[i], digits[:i], n)
    return value


def sum_all(value, n):
    step = 1
    while step < n:
        value = value + lax.ppermute(value, "ta", [(i, i ^ step) for i in range(n)])
        step *= 2
    return value


def tiles_of(rows, ni, nj):
    return rows.reshape(ni, 16, nj, 128).transpose(0, 2, 1, 3).reshape(ni * nj, 16, 128)


def rows_of(tiles, ni, nj):
    return tiles.reshape(ni, nj, 16, 128).transpose(0, 2, 1, 3).reshape(ni * nj * 16, 128)


PIECES = ((QKV0, 32, 12), (WO0, 32, 4), (WU0, 32, 16), (WD0, 128, 4))


def gather_plain(aligned):
    full = lax.all_gather(aligned.reshape(-1, 128), "ta", axis=0, tiled=True)
    return jnp.concatenate(
        [tiles_of(full[16 * b : 16 * (b + ni * nj)], ni, nj) for b, ni, nj in PIECES], axis=0
    )


def reduce_plain(tiles):
    full = jnp.concatenate([rows_of(tiles[b : b + ni * nj], ni, nj) for b, ni, nj in PIECES], axis=0)
    return lax.psum_scatter(full, "ta", scatter_dimension=0, tiled=True).astype(F32).reshape(-1)


def links(n, kind, by=1):
    pairs = []
    for i in range(n):
        if kind == "core":
            pairs.append((i, i ^ 1))
        elif kind == "z":
            pairs.append((i, (i + 8 * by) % n))
        else:
            pairs.append((i, i ^ (2 if (kind == "a") == (i % 2 == 0) else 4)))
    return pairs


def move(value, kind, by=1):
    return lax.ppermute(value, "ta", links(32, kind, by))


def after(value, *others):
    return lax.optimization_barrier((value,) + others)[0]


def to_tiles(rows, me):
    third = 3 * me + jnp.arange(3).reshape(3, 1, 1, 1)
    qkv = tiles_of(rows, 4, 12).reshape(3, 16, 16, 128)
    four = rows.reshape(3, 4, 16, 4, 128).transpose(0, 1, 3, 2, 4).reshape(3, 16, 16, 128)
    wide = rows.reshape(3, 16, 16, 128).transpose(0, 2, 1, 3)
    out = jnp.where(third < 24, qkv, jnp.where((third >= 32) & (third < 64), wide, four))
    return out.reshape(48, 16, 128)


def to_rows(tiles, me):
    third = 3 * me + jnp.arange(3).reshape(3, 1, 1)
    qkv = rows_of(tiles, 4, 12).reshape(3, 256, 128)
    four = tiles.reshape(3, 4, 4, 16, 128).transpose(0, 1, 3, 2, 4).reshape(3, 256, 128)
    wide = tiles.reshape(3, 16, 16, 128).transpose(0, 2, 1, 3).reshape(3, 256, 128)
    out = jnp.where(third < 24, qkv, jnp.where((third >= 32) & (third < 64), wide, four))
    return out.reshape(-1)


def head_rows(tiles, me):
    third = 3 * me
    four = ((third >= 24) & (third < 32)) | (third >= 64)
    return jnp.where(four, jnp.concatenate([tiles[:4, 0], tiles[:4, 1]], axis=0), tiles[:8, 0]).reshape(-1)


def per_device(frames, cotangent, mem_index, master, moment, second, average):
    n = lax.axis_size("ta")
    me = lax.axis_index("ta")
    mev = me.astype(jnp.int32).reshape(1)
    layers, share = master.shape
    step = 2 * D // n
    fast = n == GROUPS
    digits = strides(n)

    def vmem(*shape_types):
        return [pltpu.VMEM(shape, dtype) for shape, dtype in shape_types]

    def sems(count):
        return [pltpu.SemaphoreType.DMA((count,))]

    def call(kernel, ins, specs, outs, scratch, aliases=None, flops=3 * 10**9):
        return run(
            kernel, tuple(sds(*o) for o, _ in outs), tuple(ins), specs=specs,
            out_specs=tuple(VM if keep else ANYS for _, keep in outs), scratch=scratch,
            aliases=aliases, flops=flops, nbytes=10**7,
        )

    tf, tb = ((TOK, D), F32), ((TOK, D), BF16)
    wide, rows16, kv16 = ((TOK, FF), BF16), ((ROWS, D), BF16), ((ROWS, 2 * D), BF16)
    prob, rows32, kv32 = ((NBLK * 4, KB, 128), BF16), ((ROWS, D), F32), ((ROWS, 2 * D), F32)
    drow, dtab_t, sums = ((1, D), F32), ((128, D), F32), ((NSEG, D), BF16)
    tiles_t = ((TILES, 16, 128), BF16)
    score = ((NBLK * 4, KB, 128), F32)
    wscr = vmem(tiles_t) + sems(GROUPS + 1)

    msgs = [(((LH + NSEG, D), BF16), True), (((RH, D), BF16), True), (sums, True), (sums, True)]

    def forward_moves(ahead, back, summ):
        return shift(ahead, 1, n), shift(back, -1, n), shift(summ, 2, n)

    tail = shift(master[:, share - 2 * D :], 1, n)
    ahead, back, root, summ = call(first_kernel, (mev, frames), [SM, VM], msgs, [], flops=10**7)
    hl, hr, behind2 = forward_moves(ahead, back, summ)

    ext = jnp.concatenate([tail, master], axis=1)
    aligned = lax.dynamic_slice(ext, (0, 2 * D - step * me), (layers, MATS // n)).astype(BF16)
    gains = master[:, share - 2 * D :].astype(BF16).reshape(1, 16, 128)
    if fast:
        tiles = [to_tiles(aligned[l].reshape(-1, 128), me) for l in range(layers)]
        zd = 2
        for i in range(zd):
            root = spread_round(root, digits[i], digits[:i], n)
        b0 = after(jnp.concatenate([tiles[0], gains]), root, hl, hr, behind2)
        own0 = jnp.stack([b0] + [move(b0, "z", k) for k in range(1, 4)])
        for i in range(zd, len(digits)):
            root = spread_round(root, digits[i], digits[:i], n)
        own0 = after(own0, root)
        a0, s0 = move(own0, "a"), move(own0, "b")
        b1 = after(tiles[1], own0)
        own1 = jnp.stack([b1] + [move(b1, "z", k) for k in range(1, 4)])
        a0 = after(a0, s0, own1)
        as0 = move(a0, "b")
        w0 = [own0, a0, s0, as0]
        w0 += [move(after(v, own1), "core") for v in w0]
        own1 = after(own1, as0)
        a1, s1 = move(own1, "a"), move(own1, "b")
        w0 = tuple(w0)
    else:
        w0 = (gather_plain(aligned[0]), from_first(gains[0], me, n, n - 1))
        root = from_first(root, me, n)
    low_parts = (hl, hr, root, behind2, summ)

    first_seg = me * NSEG
    seg_ids = first_seg + jnp.arange(NSEG, dtype=jnp.int32)
    slot = jnp.arange(MEM, dtype=jnp.int32)
    loc = jnp.where(slot[None, :] == 0, mem_index, mem_index - first_seg + 96).reshape(-1, 1)
    loc = jnp.broadcast_to(loc, (NSEG * MEM, 128))
    vis = (mem_index < seg_ids[:, None]).astype(F32).reshape(-1, 1)
    vis = jnp.broadcast_to(vis, (NSEG * MEM, 128))

    hid = (rows16, tb, kv16, prob, tb)
    gt, hx0, q0, kv0, p0, o0 = call(
        functools.partial(low_attn_kernel, np_=len(w0), n=n), (mev, frames, *low_parts, loc, vis) + w0,
        [SM] + [VM] * 8 + [ANYS] * len(w0), [(((16, 128), BF16), True)] + [(t, False) for t in hid],
        wscr + vmem(*hid, score) + sems(5),
    )
    if fast:
        a1 = after(a1, o0)
        as1 = move(a1, "b")
        w1 = [own1, a1, s1]
        w1 = w1 + [as1] + [move(after(v, o0), "core") for v in w1]
    hid = (tf, tb, wide, wide)
    x1, h1, ahead, back, root, summ, a0, h20, gp0, act0 = call(
        functools.partial(low_ffn_kernel, np_=len(w0)), (mev, frames, o0, gt) + w0,
        [SM] + [VM] * 3 + [ANYS] * len(w0), [(tf, True), (tb, True)] + msgs + [(t, False) for t in hid],
        wscr + vmem(*hid) + sems(4),
    )
    if fast:
        ahead, back, root, summ, as1, *_ = lax.optimization_barrier((ahead, back, root, summ, as1, *w1[4:]))
        w1[3] = as1
    hl, hr, behind2 = forward_moves(ahead, back, summ)
    for i in range(len(digits)):
        root = spread_round(root, digits[i], digits[:i], n)
    if fast:
        w1 = tuple(w1 + [move(as1, "core")])
    else:
        w1 = (gather_plain(aligned[1]),)

    grads_out = [(tf, True), (((LH + NSEG, D), F32), True), (((RH, D), F32), True)] + [(((NSEG, D), F32), True)] * 3
    kept = (rows16, tb, tb, wide, tb, wide, tb, tb, kv16)
    output, da, dh, hal, har, root, b2, mine, dgb1, hx1, o1, h21, act1, dxb, dub, dab, dq, dkvb = call(
        functools.partial(top_kernel, np_=len(w1), n=n),
        (mev, x1, h1, hl, hr, root, behind2, summ, loc, vis, gt, cotangent) + w1,
        [SM] + [VM] * 10 + [ANYS] * (1 + len(w1)),
        [(tf, False), (tf, True)] + grads_out + [(drow, True)] + [(t, False) for t in kept],
        wscr + vmem(rows16, tb, kv16, prob, tb, tf, tb, wide, wide, tf, tf, tb, wide, tb, tb, kv16, kv32, tb, rows32, score) + sems(11),
        flops=8 * 10**9,
    )

    def backward_moves(hal, har, b2):
        return shift(hal, -1, n), shift(har, 1, n), shift(b2, -2, n)

    tree = digits[-1:] + digits[:-1]

    def collect(root, i):
        return collect_round(root, tree[i], tree[:i], n)

    dws = vmem(rows16, tb, kv16, tb, tb, tb, wide, wide, tb, tiles_t)
    dws += [pltpu.SemaphoreType.DMA] + sems(9)

    def weight_grads(part, ins, partial, gains=None):
        extra = BT + (1 if fast and gains_in else 0)
        outs = [(((2, 2, 4, extra, 16, 128), BF16), False)] * 2 if fast else [(tiles_t, False)]
        count = len(outs)
        ins = [mev] + list(ins) + ([] if gains is None else [gains])
        specs = [SM] + [ANYS] * 9 + [VM] * (len(ins) - 10)
        return call(
            functools.partial(dw_kernel, part=part, nouts=count, gains=gains is not None),
            ins + list(partial), specs + [ANYS] * len(partial), outs, dws,
            aliases={len(ins) + i: i for i in range(len(partial))}, flops=10**9,
        )

    gains_in = False
    hal, har, b2 = backward_moves(hal, har, b2)
    root = collect(root, 0)
    ins = [hx1, dq, dkvb, o1, dab, h21, dub, act1, after(dxb, root, hal, har, b2)]
    part = ()
    for i in range(2):
        part = weight_grads(i, ins, part)
        root = collect(root, i + 1)
        ins[6], ins[4] = after(dub, root), after(dab, root)
        root = after(root, part[0])
    for i in range(3, len(tree)):
        root = collect(root, i)
    grads = weight_grads(2, ins, part)

    def add(a, b):
        return (a.astype(F32) + b.astype(F32)).astype(BF16)

    if fast:
        v1 = after(add(grads[0], move(grads[1], "core")), root)
        got = move(v1[1], "b")
        x1 = after(x1, v1)
    else:
        reduced1 = reduce_plain(grads[0])

    dga1, da, dgb0, dxb, dub, dab = call(
        functools.partial(bottom_ffn_kernel, np_=len(w0)), (mev, hal, har, root, b2, mine, dh, x1, da, gt) + w0 + (a0, gp0),
        [SM] + [VM] * 9 + [ANYS] * (len(w0) + 2),
        [(drow, True), (tf, True), (drow, True), (tb, False), (wide, False), (tb, False)],
        wscr + vmem(tf, wide, tf, tb, wide, tb) + sems(5),
    )
    dga0, dh, hal, har, root, b2, mine, dq, dkvb = call(
        functools.partial(bottom_attn_kernel, np_=len(w0)),
        (mev, dab, loc, frames) + low_parts + w0 + (q0, kv0, p0), [SM] + [VM] * 8 + [ANYS] * (len(w0) + 3),
        [(drow, True)] + grads_out + [(tb, False), (kv16, False)],
        wscr + vmem(tb, kv16, prob, tb, kv16, kv32, tb, rows32, score) + sems(5),
    )
    gains = jnp.concatenate([dga0, dgb0, dga1, dgb1], axis=1)
    ins = [hx0, dq, dkvb, o0, dab, h20, dub, act0, dxb]
    if fast:
        v1 = add(after(v1[0], dh), got)
        got = move(v1[1], "a")
        ins[8] = after(dxb, v1)
        gains_in = True
    part = ()
    for i in range(2):
        part = weight_grads(i, ins, part)
    if fast:
        v1 = add(after(v1[0], part[0]), got)
        z1 = [move(v1[k], "z", k) for k in range(1, 4)]
        ins[4] = after(dab, v1)
    grads = weight_grads(2, ins, part, gains.astype(BF16).reshape(16, 128) if fast else None)
    if fast:
        v = add(grads[0], move(grads[1], "core"))
        root = collect(after(root, v), 0)
        got = move(v[1], "b")
        v = add(v[0], got)
        total1 = functools.reduce(jnp.add, [z.astype(F32) for z in z1], after(v1[0], v).astype(F32))
        got = move(v[1], "a")
        root = collect(collect(after(root, v, total1), 1), 2)
        reduced1, head1 = to_rows(total1, me), shift(head_rows(total1, me), -1, n)
        v = add(v[0], got)
        root = after(root, v, head1)
        zs = [move(v[k], "z", k) for k in range(1, 4)]
        for i in range(3, len(tree)):
            root = collect(root, i)
        hal, har, b2 = backward_moves(hal, har, after(b2, v))
        total0 = functools.reduce(jnp.add, [z.astype(F32) for z in zs], v[0].astype(F32))
        gsum = total0[BT].reshape(layers, 2 * D)
        total0 = total0[:BT]
        reduced = [to_rows(total0, me), reduced1]
        heads = [shift(head_rows(total0, me), -1, n), head1]
    else:
        hal, har, b2 = backward_moves(hal, har, b2)
        for i in range(len(tree)):
            root = collect(root, i)
        gsum = sum_all(gains.reshape(layers, 2 * D), n)
        reduced = [reduce_plain(grads[0]), reduced1]
        heads = [shift(r[: 2 * D], -1, n) for r in reduced]
    dx = call(
        last_kernel, (mev, hal, har, root, b2, mine, dh, frames, da, gt),
        [SM] + [VM] * 9, [(tf, True)], vmem(tf), flops=10**7,
    )[0]

    own = jnp.stack(reduced)
    head = jnp.where(me == n - 1, gsum, jnp.stack(heads))
    grad = lax.dynamic_slice(jnp.concatenate([own, head], axis=1), (0, step * me), (layers, share))
    gain_out = lax.dynamic_slice(gsum, (0, step * me), (layers, step))
    new_moment = 0.5 * moment + 0.5 * grad
    new_second = 0.5 * second + 0.5 * grad * grad
    correction = 1.0 - 0.5**STEP
    update = new_moment / correction / (jnp.sqrt(new_second / correction) + 1e-08) + 0.1 * master
    new_master = master - 0.08 * update
    new_average = 0.9 * average + 0.1 * new_master
    return (output, dx, gain_out, new_moment, new_second, new_master, new_average)


def solution(mesh):
    rows, flat = P("ta", None), P(None, "ta")
    return jax.shard_map(
        per_device,
        mesh=mesh,
        in_specs=(rows, rows, rows, flat, flat, flat, flat),
        out_specs=(rows, rows, flat, flat, flat, flat, flat),
        check_vma=False,
    )
```

```python
import functools

import jax
import jax.numpy as jnp
from jax import lax
from jax.experimental import pallas as pl
from jax.experimental.pallas import tpu as pltpu
from jax.sharding import PartitionSpec as P

D = 512
HEADS = 8
FF = 2048
SEG = 16
LEFT = 30
RIGHT = 4
MEM = 4
STEP = 10
UN = 4
NEG = -1e30

TOK = 512
NSEG = TOK // SEG
LH = 32
RH = 16
EXT = LH + TOK + 2 * RH
ROWS = EXT + NSEG * MEM
BLK = 4
NBLK = NSEG // BLK
QB = BLK * SEG
KB = 128
WB = KB - BLK * MEM

TILES = 1536
QKV0, WO0, WU0, WD0 = 0, 384, 512, 1024
MATS = TILES * 16 * 128
GROUPS = 32
BT = TILES // GROUPS

F32 = jnp.float32
BF16 = jnp.bfloat16
VM = pl.BlockSpec(memory_space=pltpu.VMEM)
SM = pl.BlockSpec(memory_space=pltpu.SMEM)
ANYS = pl.BlockSpec(memory_space=pl.ANY)


def mm(a, b):
    return lax.dot_general(a, b, (((1,), (0,)), ((), ())), preferred_element_type=F32)


def mm_nt(a, b):
    return lax.dot_general(a, b, (((1,), (1,)), ((), ())), preferred_element_type=F32)


def mm_tn(a, b):
    return lax.dot_general(a, b, (((0,), (0,)), ((), ())), preferred_element_type=F32)


def wblk(w, base, nj, i0, ni, j0, nj_take):
    cols = [
        jnp.concatenate([w[base + (i0 + i) * nj + j0 + j] for i in range(ni)], axis=0)
        for j in range(nj_take)
    ]
    return cols[0] if nj_take == 1 else jnp.concatenate(cols, axis=1)


def place(me, rc, ra, rb, k):
    core = (me % 2) ^ rc
    x = ((me // 2) % 2) ^ jnp.where(core == 0, ra, rb)
    y = ((me // 4) % 2) ^ jnp.where(core == 0, rb, ra)
    z = (me // 8 + k) % 4
    return ((z * 2 + y) * 2 + x) * 2 + core


def load_weights(me, pieces, w_ref, sems, lo, hi, gt_ref=None):
    if len(pieces) < 8:
        if gt_ref is not None:
            pltpu.make_async_copy(pieces[1], gt_ref, sems.at[GROUPS]).start()
        for d in range(lo, hi):
            t = pl.ds(BT * d, BT)
            pltpu.make_async_copy(pieces[0].at[t], w_ref.at[t], sems.at[d]).start()
        return
    for rc in range(2):
        for m in range(4):
            for k in range(4):
                d = place(me, rc, m % 2, m // 2, -k % 4)
                piece = pieces[4 * rc + m].at[k]

                @pl.when((d >= lo) & (d < hi))
                def _():
                    pltpu.make_async_copy(
                        piece.at[pl.ds(0, BT)], w_ref.at[pl.ds(d * BT, BT)], sems.at[d]
                    ).start()

                if gt_ref is not None:

                    @pl.when(d == GROUPS - 1)
                    def _():
                        pltpu.make_async_copy(piece.at[BT], gt_ref, sems.at[GROUPS]).start()


def await_weights(w_ref, sems, lo, hi):
    for d in range(lo, hi):
        part = w_ref.at[pl.ds(d * BT, BT)]
        pltpu.make_async_copy(part, part, sems.at[d]).wait()


def gain_row(g_ref, layer, which):
    g = g_ref[...].astype(F32)
    r = 8 * layer + 4 * which
    return jnp.concatenate([g[r + k : r + k + 1] for k in range(4)], axis=1)


def norm_parts(v):
    mean = jnp.mean(v, axis=-1, keepdims=True)
    cen = v - mean
    rstd = lax.rsqrt(jnp.mean(cen * cen, axis=-1, keepdims=True) + 1e-05)
    return cen * rstd, rstd


def norm_back(dh, xhat, rstd, gain):
    dx = dh * gain
    return rstd * (
        dx
        - jnp.mean(dx, axis=-1, keepdims=True)
        - xhat * jnp.mean(dx * xhat, axis=-1, keepdims=True)
    )


def seg_mean(h):
    return (jnp.sum(h.astype(F32).reshape(NSEG, SEG, D), axis=1) * (1.0 / SEG)).astype(BF16)


def head_of_layer(x, gain):
    xhat, _ = norm_parts(x)
    h1 = (xhat * gain).astype(BF16)
    return h1, seg_mean(h1)


def send_on(me, rows_ref, means, ahead_ref, back_ref, root_ref, sum_ref):
    sum_ref[...] = means
    ahead_ref[0:LH] = rows_ref[TOK - LH : TOK]
    ahead_ref[LH:] = means
    back_ref[...] = rows_ref[0:RH]
    root_ref[...] = jnp.where(me == 0, means, jnp.zeros_like(means))


def first_kernel(me_ref, x_ref, ahead_ref, back_ref, root_ref, sum_ref):
    xhat, _ = norm_parts(x_ref[...].astype(F32))
    send_on(me_ref[0], x_ref, seg_mean(xhat), ahead_ref, back_ref, root_ref, sum_ref)


def lane_lo(rows):
    return lax.broadcasted_iota(jnp.int32, (rows, 128), 1) < 64


def split_heads(m, lo):
    z = jnp.zeros_like(m)
    return jnp.concatenate([jnp.where(lo, m, z), jnp.where(lo, z, m)], axis=0)


def onehot_of(loc_ref):
    ids = lax.broadcasted_iota(jnp.int32, (NSEG * MEM, 128), 1)
    return jnp.where(loc_ref[...] == ids, 1.0, 0.0).astype(BF16)


def block_keys(kv_ref, b, col):
    r0 = pl.multiple_of(b * QB, QB)
    m0 = pl.multiple_of(EXT + b * (BLK * MEM), BLK * MEM)
    return jnp.concatenate(
        [kv_ref[pl.ds(r0, WB), col : col + 128], kv_ref[pl.ds(m0, BLK * MEM), col : col + 128]], axis=0
    )


def attend(me, n, q_ref, kv_ref, vis_ref, p_ref, o_ref, s_ref):
    ki = lax.broadcasted_iota(jnp.int32, (KB, 128), 0)
    qi = (lax.broadcasted_iota(jnp.int32, (KB, 128), 1) % QB) // SEG
    off = ki - SEG * qi - (LH - LEFT)
    near = jnp.where((off >= 0) & (off < LEFT + SEG + RIGHT) & (ki < WB), 1.0, 0.0)
    memb = jnp.where((ki >= WB) & ((ki - WB) // MEM == qi), 1.0, 0.0)
    first = jnp.where(me == 0, LH, 0)
    end = jnp.where(me == n - 1, LH + TOK, EXT)
    lo = lane_lo(QB)

    def scores(b, carry):
        r0 = pl.multiple_of(b * QB, QB)
        m0 = pl.multiple_of(b * (BLK * MEM), BLK * MEM)
        inside = (ki + r0 >= first) & (ki + r0 < end)
        memv = jnp.concatenate(
            [jnp.zeros((WB, 128), F32), vis_ref[pl.ds(m0, BLK * MEM), :]], axis=0
        )
        seen = jnp.where(inside, near, 0.0) + memb * memv > 0.5
        for p in range(4):
            kc = block_keys(kv_ref, b, 128 * p)
            s = mm_nt(kc, split_heads(q_ref[pl.ds(r0, QB), 128 * p : 128 * p + 128], lo))
            s_ref[b * 4 + p] = jnp.where(seen, s, NEG)
        return carry

    def softmax(i, carry):
        s = s_ref[i]
        e = jnp.exp(s - jnp.max(s, axis=0, keepdims=True))
        p_ref[i] = (e * (1.0 / jnp.sum(e, axis=0, keepdims=True))).astype(BF16)
        return carry

    def mix(b, carry):
        r0 = pl.multiple_of(b * QB, QB)
        for p in range(4):
            o2 = mm_tn(p_ref[b * 4 + p], block_keys(kv_ref, b, D + 128 * p))
            o_ref[pl.ds(r0, QB), 128 * p : 128 * p + 128] = jnp.where(lo, o2[:QB], o2[QB:]).astype(BF16)
        return carry

    lax.fori_loop(0, NBLK, scores, 0, unroll=UN)
    lax.fori_loop(0, 4 * NBLK, softmax, 0, unroll=4)
    lax.fori_loop(0, NBLK, mix, 0, unroll=UN)


def attend_back(q_ref, kv_ref, p_ref, do_ref, dq_ref, dkv_ref, s_ref):
    dkv_ref[...] = jnp.zeros_like(dkv_ref)
    lo = lane_lo(QB)

    def weights(b, carry):
        r0 = pl.multiple_of(b * QB, QB)
        m0 = pl.multiple_of(EXT + b * (BLK * MEM), BLK * MEM)
        for p in range(4):
            vc0 = D + 128 * p
            dd = split_heads(do_ref[pl.ds(r0, QB), 128 * p : 128 * p + 128], lo)
            s_ref[b * 4 + p] = mm_nt(block_keys(kv_ref, b, vc0), dd)
            dv = mm(p_ref[b * 4 + p], dd)
            dkv_ref[pl.ds(r0, WB), vc0 : vc0 + 128] += dv[:WB]
            dkv_ref[pl.ds(m0, BLK * MEM), vc0 : vc0 + 128] = dv[WB:]
        return carry

    def softmax(i, carry):
        pf = p_ref[i].astype(F32)
        pd = pf * s_ref[i]
        p_ref[i] = (pd - pf * jnp.sum(pd, axis=0, keepdims=True)).astype(BF16)
        return carry

    def queries(b, carry):
        r0 = pl.multiple_of(b * QB, QB)
        m0 = pl.multiple_of(EXT + b * (BLK * MEM), BLK * MEM)
        for p in range(4):
            kc0 = 128 * p
            ds = p_ref[b * 4 + p]
            dk = mm(ds, split_heads(q_ref[pl.ds(r0, QB), kc0 : kc0 + 128], lo))
            dq2 = mm_tn(ds, block_keys(kv_ref, b, kc0))
            dq_ref[pl.ds(r0, QB), kc0 : kc0 + 128] = (jnp.where(lo, dq2[:QB], dq2[QB:]) * 0.125).astype(BF16)
            dkv_ref[pl.ds(r0, WB), kc0 : kc0 + 128] += dk[:WB]
            dkv_ref[pl.ds(m0, BLK * MEM), kc0 : kc0 + 128] = dk[WB:]
        return carry

    lax.fori_loop(0, NBLK, weights, 0, unroll=UN)
    lax.fori_loop(0, 4 * NBLK, softmax, 0, unroll=4)
    lax.fori_loop(0, NBLK, queries, 0, unroll=UN)


class Copies:
    def __init__(self, sems):
        self.sems, self.used, self.open = sems, 0, []

    def start(self, src, dst):
        copy = pltpu.make_async_copy(src, dst, self.sems.at[self.used])
        self.used += 1
        copy.start()
        return copy

    def out(self, src, dst):
        self.open.append(self.start(src, dst))

    def finish(self):
        for copy in self.open:
            copy.wait()


def project(hx_ref, w_ref, q_ref, kv_ref):
    q = mm(hx_ref[LH : LH + TOK], wblk(w_ref, QKV0, 12, 0, 32, 0, 4)).astype(BF16)
    q_ref[...] = q * jnp.asarray(0.125, BF16)
    for j in range(2):
        kv_ref[:, 512 * j : 512 * j + 512] = mm(hx_ref[...], wblk(w_ref, QKV0, 12, 0, 32, 4 + 4 * j, 4)).astype(BF16)


def feed_forward(h2_ref, w_ref, act_ref, gp_ref, out_ref, ready):
    for c in range(4):
        u = mm(h2_ref[...], wblk(w_ref, WU0, 16, 0, 32, 4 * c, 4))
        cc, c3 = 0.7978845608028654, 0.7978845608028654 * 0.044715
        u2 = u * u
        t = jnp.tanh(u * (cc + c3 * u2))
        hu = 0.5 * u
        act = (hu + hu * t).astype(BF16)
        gp = 0.5 + 0.5 * t + hu * (1.0 - t * t) * (cc + 3 * c3 * u2)
        act_ref[:, 512 * c : 512 * c + 512] = act
        gp_ref[:, 512 * c : 512 * c + 512] = gp.astype(BF16)
        if c == 0:
            ready()
        out_ref[...] += mm(act, wblk(w_ref, WD0, 4, 32 * c, 32, 0, 4))


def back_ffn(dx_ref, w_ref, gains, a_ref, gp_ref, da_ref, dxb_ref, dub_ref, dab_ref, dgb_ref, step):
    dxb_ref[...] = dx_ref[...].astype(BF16)
    step("dxb")
    for c in range(4):
        dact = mm_nt(dxb_ref[...], wblk(w_ref, WD0, 4, 32 * c, 32, 0, 4))
        du = (dact * gp_ref[:, 512 * c : 512 * c + 512].astype(F32)).astype(BF16)
        dub_ref[:, 512 * c : 512 * c + 512] = du
        dh2 = mm_nt(du, wblk(w_ref, WU0, 16, 0, 32, 4 * c, 4))
        if c:
            da_ref[...] += dh2
        else:
            da_ref[...] = dh2
    step("dub")
    xhat, rstd = norm_parts(a_ref[...])
    dh2 = da_ref[...]
    dgb_ref[...] = jnp.sum(dh2 * xhat, axis=0, keepdims=True)
    da = dx_ref[...] + norm_back(dh2, xhat, rstd, gains)
    da_ref[...] = da
    dab_ref[...] = da.astype(BF16)
    step("dab")


def back_attn(dab_ref, w_ref, q_ref, kv_ref, p_ref, dq_ref, dkvb_ref, dh_ref, dkv_ref, dob_ref, s_ref, step):
    dob_ref[...] = mm_nt(dab_ref[...], wblk(w_ref, WO0, 4, 0, 32, 0, 4)).astype(BF16)
    step("attend")
    attend_back(q_ref, kv_ref, p_ref, dob_ref, dq_ref, dkv_ref, s_ref)
    dkvb_ref[...] = dkv_ref[...].astype(BF16)
    step("dkvb")
    dh_ref[...] = mm_nt(dkvb_ref[...], wblk(w_ref, QKV0, 12, 0, 32, 4, 8))
    dh_ref[LH : LH + TOK] += mm_nt(dq_ref[...], wblk(w_ref, QKV0, 12, 0, 32, 0, 4))


def table_grad(loc_ref, dh_ref, hal_ref, har_ref, root_ref, b2_ref, mine_ref):
    dch = dh_ref[EXT:ROWS]
    hi = dch.astype(BF16)
    oh = onehot_of(loc_ref)
    dtab = mm_tn(oh, hi) + mm_tn(oh, (dch - hi.astype(F32)).astype(BF16))
    kind = hal_ref.dtype
    hal_ref[0:LH] = dh_ref[0:LH].astype(kind)
    hal_ref[LH:] = dtab[64:96].astype(kind)
    har_ref[...] = dh_ref[LH + TOK : LH + TOK + RH].astype(kind)
    root_ref[...] = dtab[0:32].astype(kind)
    b2_ref[...] = dtab[32:64].astype(kind)
    mine_ref[...] = dtab[96:128]
    return dtab


def low_attn_kernel(me_ref, x_ref, hl_ref, hr_ref, root_ref, b2_ref, summ_ref, loc_ref, vis_ref, *rest, np_, n):
    pieces, rest = rest[:np_], rest[np_:]
    gt_ref, hx_o, q_o, kv_o, p_o, o_o, w_ref, sems, hx_ref, q_ref, kv_ref, p_ref, o_ref, s_ref, osem = rest
    me = me_ref[0]
    load_weights(me, pieces, w_ref, sems, 0, 8, gt_ref)
    copies = Copies(osem)
    pltpu.make_async_copy(gt_ref, gt_ref, sems.at[GROUPS]).wait()
    ga = gain_row(gt_ref, 0, 0)
    for ref, rows, at in ((hl_ref, LH, 0), (x_ref, TOK, LH), (hr_ref, RH, LH + TOK)):
        xhat, _ = norm_parts(ref[0:rows].astype(F32))
        hx_ref[at : at + rows] = (xhat * ga).astype(BF16)
    means = jnp.concatenate([root_ref[...], b2_ref[...], hl_ref[LH:], summ_ref[...]], axis=0)
    hx_ref[LH + TOK + RH : EXT] = jnp.zeros((RH, D), BF16)
    hx_ref[EXT:ROWS] = mm(onehot_of(loc_ref), (means.astype(F32) * ga).astype(BF16)).astype(BF16)
    copies.out(hx_ref, hx_o)
    await_weights(w_ref, sems, 0, 8)
    project(hx_ref, w_ref, q_ref, kv_ref)
    copies.out(q_ref, q_o)
    copies.out(kv_ref, kv_o)
    attend(me, n, q_ref, kv_ref, vis_ref, p_ref, o_ref, s_ref)
    copies.out(p_ref, p_o)
    copies.out(o_ref, o_o)
    copies.finish()


def low_ffn_kernel(me_ref, x_ref, o_ref, gt_ref, *rest, np_):
    pieces, rest = rest[:np_], rest[np_:]
    (out_ref, h1n_ref, ahead_ref, back_ref, root_ref, sumn_ref, a_o, h2_o, gp_o, act_o,
     w_ref, sems, a_ref, h2_ref, gp_ref, act_ref, osem) = rest
    load_weights(me_ref[0], pieces, w_ref, sems, 8, 32)
    copies = Copies(osem)
    await_weights(w_ref, sems, 8, 11)
    a = x_ref[...].astype(F32) + mm(o_ref[...], wblk(w_ref, WO0, 4, 0, 32, 0, 4))
    a_ref[...] = a
    copies.out(a_ref, a_o)
    xhat, _ = norm_parts(a)
    h2_ref[...] = (xhat * gain_row(gt_ref, 0, 1)).astype(BF16)
    copies.out(h2_ref, h2_o)
    out_ref[...] = a
    await_weights(w_ref, sems, 11, 22)
    feed_forward(h2_ref, w_ref, act_ref, gp_ref, out_ref, lambda: await_weights(w_ref, sems, 22, 32))
    copies.out(act_ref, act_o)
    copies.out(gp_ref, gp_o)
    h1n, sumn = head_of_layer(out_ref[...], gain_row(gt_ref, 1, 0))
    h1n_ref[...] = h1n
    send_on(me_ref[0], h1n_ref, sumn, ahead_ref, back_ref, root_ref, sumn_ref)
    copies.finish()


def top_kernel(me_ref, x_ref, h1_ref, hl_ref, hr_ref, root_ref, b2_ref, summ_ref, loc_ref, vis_ref, gt_ref, cot_any,
               *rest, np_, n):
    pieces, rest = rest[:np_], rest[np_:]
    (out_o, da_ref, dhown_ref, hal_ref, har_ref, rootg_ref, b2g_ref, mine_ref, dgb_ref, hx_o, o_o, h2_o, act_o, dxb_o, dub_o, dab_o, dq_o, dkvb_o,
     w_ref, sems, hx_ref, q_ref, kv_ref, p_ref, o_ref, a_ref, h2_ref, gp_ref, act_ref,
     out_ref, dx_ref, dxb_ref, dub_ref, dab_ref, dq_ref, dkvb_ref, dkv_ref, dob_ref, dh_ref, s_ref, osem) = rest
    me = me_ref[0]
    load_weights(me, pieces, w_ref, sems, 0, 32)
    copies = Copies(osem)
    cot = copies.start(cot_any, dx_ref)
    hx_ref[0:LH] = hl_ref[0:LH]
    hx_ref[LH : LH + TOK] = h1_ref[...]
    hx_ref[LH + TOK : LH + TOK + RH] = hr_ref[...]
    hx_ref[LH + TOK + RH : EXT] = jnp.zeros((RH, D), BF16)
    table = jnp.concatenate([root_ref[...], b2_ref[...], hl_ref[LH:], summ_ref[...]], axis=0)
    hx_ref[EXT:ROWS] = mm(onehot_of(loc_ref), table).astype(BF16)
    copies.out(hx_ref, hx_o)
    await_weights(w_ref, sems, 0, 8)
    project(hx_ref, w_ref, q_ref, kv_ref)
    attend(me, n, q_ref, kv_ref, vis_ref, p_ref, o_ref, s_ref)
    copies.out(o_ref, o_o)
    await_weights(w_ref, sems, 8, 32)
    a = x_ref[...] + mm(o_ref[...], wblk(w_ref, WO0, 4, 0, 32, 0, 4))
    a_ref[...] = a
    xhat, _ = norm_parts(a)
    h2_ref[...] = (xhat * gain_row(gt_ref, 1, 1)).astype(BF16)
    copies.out(h2_ref, h2_o)
    out_ref[...] = a
    feed_forward(h2_ref, w_ref, act_ref, gp_ref, out_ref, lambda: None)
    copies.out(act_ref, act_o)
    copies.out(out_ref, out_o)
    cot.wait()
    done = {"dxb": ((dxb_ref, dxb_o),), "dub": ((dub_ref, dub_o),), "dab": ((dab_ref, dab_o),),
            "dkvb": ((dkvb_ref, dkvb_o), (dq_ref, dq_o))}

    def step(name):
        for pair in done.get(name, ()):
            copies.out(*pair)

    back_ffn(dx_ref, w_ref, gain_row(gt_ref, 1, 1), a_ref, gp_ref, da_ref, dxb_ref, dub_ref, dab_ref, dgb_ref, step)
    back_attn(dab_ref, w_ref, q_ref, kv_ref, p_ref, dq_ref, dkvb_ref, dh_ref, dkv_ref, dob_ref, s_ref, step)
    dhown_ref[...] = dh_ref[LH : LH + TOK]
    table_grad(loc_ref, dh_ref, hal_ref, har_ref, rootg_ref, b2g_ref, mine_ref)
    copies.finish()


def norm_one_back(dh_ref, hal_ref, har_ref, dsum, x, gain, da_ref, acc_ref):
    acc_ref[...] = dh_ref[...]
    acc_ref[TOK - LH : TOK] += hal_ref[0:LH].astype(F32)
    acc_ref[0:RH] += har_ref[...].astype(F32)
    for s in range(NSEG):
        acc_ref[SEG * s : SEG * s + SEG] += dsum[s : s + 1, :] * (1.0 / SEG)
    xhat, rstd = norm_parts(x)
    dh = acc_ref[...]
    return da_ref[...] + norm_back(dh, xhat, rstd, gain), jnp.sum(dh * xhat, axis=0, keepdims=True)


def summed(me_ref, hal_ref, root_ref, b2_ref, mine_ref):
    near = mine_ref[...] + hal_ref[LH:].astype(F32) + b2_ref[...].astype(F32)
    return near + jnp.where(me_ref[0] == 0, root_ref[...].astype(F32), 0.0)


def bottom_ffn_kernel(me_ref, hal_ref, har_ref, root_ref, b2_ref, dtabp_ref, dhp_ref, x_ref, dap_ref, gt_ref, *rest, np_):
    pieces, rest = rest[:np_], rest[np_:]
    (a_any, gp_any, dga_ref, da_ref, dgb_ref, dxb_o, dub_o, dab_o,
     w_ref, sems, a_ref, gp_ref, dx_ref, dxb_ref, dub_ref, dab_ref, osem) = rest
    load_weights(me_ref[0], pieces, w_ref, sems, 10, 32)
    copies = Copies(osem)
    loads = [copies.start(*pair) for pair in ((gp_any, gp_ref), (a_any, a_ref))]
    dx, dga = norm_one_back(
        dhp_ref, hal_ref, har_ref, summed(me_ref, hal_ref, root_ref, b2_ref, dtabp_ref), x_ref[...],
        gain_row(gt_ref, 1, 0), dap_ref, dx_ref,
    )
    dx_ref[...] = dx
    dga_ref[...] = dga
    await_weights(w_ref, sems, 10, 32)
    loads[0].wait()
    done = {"dxb": (dxb_ref, dxb_o), "dub": (dub_ref, dub_o), "dab": (dab_ref, dab_o)}

    def step(name):
        if name == "dub":
            loads[1].wait()
        copies.out(*done[name])

    back_ffn(dx_ref, w_ref, gain_row(gt_ref, 0, 1), a_ref, gp_ref, da_ref, dxb_ref, dub_ref, dab_ref, dgb_ref, step)
    copies.finish()


def bottom_attn_kernel(me_ref, dab_ref, loc_ref, frames_ref, ahead0_ref, hr0_ref, root0_ref, b20_ref, summ0_ref, *rest, np_):
    pieces, rest = rest[:np_], rest[np_:]
    (q_any, kv_any, p_any, dga_ref, dhown_ref, hal_ref, har_ref, rootg_ref, b2g_ref, mine_ref, dq_o, dkvb_o,
     w_ref, sems, q_ref, kv_ref, p_ref, dq_ref, dkvb_ref, dkv_ref, dob_ref, dh_ref, s_ref, osem) = rest
    load_weights(me_ref[0], pieces, w_ref, sems, 0, 11)
    copies = Copies(osem)
    loads = [copies.start(*pair) for pair in ((q_any, q_ref), (kv_any, kv_ref), (p_any, p_ref))]
    await_weights(w_ref, sems, 0, 11)

    def step(name):
        if name == "attend":
            for load in loads:
                load.wait()
        else:
            copies.out(dkvb_ref, dkvb_o)
            copies.out(dq_ref, dq_o)

    back_attn(dab_ref, w_ref, q_ref, kv_ref, p_ref, dq_ref, dkvb_ref, dh_ref, dkv_ref, dob_ref, s_ref, step)
    dhown_ref[...] = dh_ref[LH : LH + TOK]
    dtab = table_grad(loc_ref, dh_ref, hal_ref, har_ref, rootg_ref, b2g_ref, mine_ref)
    means = jnp.concatenate([root0_ref[...], b20_ref[...], ahead0_ref[LH:], summ0_ref[...]], axis=0)
    total = jnp.sum(dtab * means.astype(F32), axis=0, keepdims=True)
    for ref, rows, at in ((ahead0_ref, LH, 0), (frames_ref, TOK, LH), (hr0_ref, RH, LH + TOK)):
        xhat, _ = norm_parts(ref[0:rows].astype(F32))
        total += jnp.sum(dh_ref[at : at + rows] * xhat, axis=0, keepdims=True)
    dga_ref[...] = total
    copies.finish()


def last_kernel(me_ref, hal_ref, har_ref, root_ref, b2_ref, dtab_ref, dh_ref, x_ref, da_ref, gt_ref, dx_ref, acc_ref):
    dx, _ = norm_one_back(
        dh_ref, hal_ref, har_ref, summed(me_ref, hal_ref, root_ref, b2_ref, dtab_ref), x_ref[...].astype(F32),
        gain_row(gt_ref, 0, 0), da_ref, acc_ref,
    )
    dx_ref[...] = dx


def dw_kernel(me_ref, *rest, part, nouts, gains=False):
    srcs, rest = rest[:9], rest[9:]
    if gains:
        gain_ref, rest = rest[0], rest[1:]
    outs, rest = rest[-12 - nouts : -12], rest[-12:]
    hx_ref, dq_ref, dkv_ref, o_ref, dab_ref, h2_ref, dub_ref, act_ref, dxb_ref, g_ref, sem, isem = rest
    copies = Copies(isem)
    loads = {}
    for i in {0: (7, 8), 1: (5, 6), 2: (3, 4, 0, 1, 2)}[part]:
        loads[i] = copies.start(srcs[i], rest[i])

    def put(val, base, nj, i0, j0):
        v = val.astype(BF16)
        for i in range(val.shape[0] // 16):
            for j in range(val.shape[1] // 128):
                g_ref[base + (i0 + i) * nj + j0 + j] = v[16 * i : 16 * i + 16, 128 * j : 128 * j + 128]

    def send(lo, hi):
        if nouts == 1:
            tiles = pl.ds(lo * 16, (hi - lo) * 16)
            pltpu.make_async_copy(g_ref.at[tiles], outs[0].at[tiles], sem).start()
            return
        me = me_ref[0]
        units = {}
        for u in range(lo, hi):
            units.setdefault(u // 3, []).append(u % 3)
        for d, thirds in units.items():
            core = d % 2
            rx, ry = ((me // 2) % 2) ^ (d // 2 % 2), ((me // 4) % 2) ^ (d // 4 % 2)
            ra, rb = (rx, ry) if core == 0 else (ry, rx)
            k = (d // 8 - me // 8 + 4) % 4
            t0, t1 = 16 * thirds[0], 16 * thirds[-1] + 16
            for rc in range(2):

                @pl.when((me % 2) ^ core == rc)
                def _():
                    pltpu.make_async_copy(
                        g_ref.at[pl.ds(d * BT + t0, t1 - t0)], outs[rc].at[rb, ra, k, pl.ds(t0, t1 - t0)], sem
                    ).start()

    if part == 0:
        loads[7].wait()
        loads[8].wait()

        def down(c, carry):
            c0 = pl.multiple_of(c * 256, 256)
            put(mm_tn(act_ref[:, pl.ds(c0, 256)], dxb_ref[...]), WD0, 4, 16 * c, 0)
            return carry

        lax.fori_loop(0, FF // 256, down, 0, unroll=4)
        send(64, 96)
    if part == 1:
        loads[5].wait()
        loads[6].wait()

        def up(c, carry):
            c0 = pl.multiple_of(c * 256, 256)
            put(mm_tn(h2_ref[...], dub_ref[:, pl.ds(c0, 256)]), WU0, 16, 0, 2 * c)
            return carry

        lax.fori_loop(0, FF // 256, up, 0, unroll=4)
        send(32, 64)
    if part == 2:
        for i in (3, 4, 0, 1, 2):
            loads[i].wait()
        for j in range(2):
            put(mm_tn(o_ref[...], dab_ref[:, 256 * j : 256 * j + 256]), WO0, 4, 0, 2 * j)
        send(24, 32)
        for j in range(2):
            put(mm_tn(hx_ref[LH : LH + TOK], dq_ref[:, 256 * j : 256 * j + 256]), QKV0, 12, 0, 2 * j)
        for j in range(4):
            put(mm_tn(hx_ref[...], dkv_ref[:, 256 * j : 256 * j + 256]), QKV0, 12, 0, 4 + 2 * j)
        send(0, 24)
        if gains:
            for i in range(GROUPS):
                pltpu.make_async_copy(
                    gain_ref, outs[i // 16].at[i % 2, i // 2 % 2, i // 4 % 4, BT], sem
                ).start()
            for i in range(GROUPS):
                pltpu.make_async_copy(gain_ref, gain_ref, sem).wait()
    first, count = {0: (WD0, 512), 1: (WU0, 512), 2: (0, 512)}[part]
    all_of = g_ref.at[pl.ds(first, count)]
    pltpu.make_async_copy(all_of, all_of, sem).wait()


def sds(shape, dtype):
    return jax.ShapeDtypeStruct(shape, dtype)


PARAMS = dict(vmem_limit_bytes=56 * 1024 * 1024)


def run(kernel, outs, ins, specs=None, scratch=(), flops=0, nbytes=0, aliases=None, **kw):
    return pl.pallas_call(
        kernel,
        out_shape=outs,
        input_output_aliases=aliases or {},
        in_specs=specs or [VM] * len(ins),
        out_specs=jax.tree.map(lambda _: VM, outs) if "out_specs" not in kw else kw["out_specs"],
        scratch_shapes=list(scratch),
        compiler_params=pltpu.CompilerParams(**PARAMS),
        cost_estimate=pl.CostEstimate(flops=flops, bytes_accessed=nbytes, transcendentals=0),
    )(*ins)


def shift(value, by, n):
    return lax.ppermute(value, "ta", [(i, i + by) for i in range(n) if 0 <= i + by < n])


def strides(n):
    return [(1 << k, 2) for k in reversed(range(n.bit_length() - 1))]


def spread_round(value, digit, done, n):
    stride, radix = digit
    keep = [i for i in range(n) if all(i // s % r == 0 for s, r in strides(n) if (s, r) not in done)]
    parts = [lax.ppermute(value, "ta", [(i, i + j * stride) for i in keep]) for j in range(1, radix)]
    return functools.reduce(jnp.add, parts, value)


def collect_round(value, digit, done, n):
    stride, radix = digit
    keep = [i for i in range(n) if all(i // s % r == 0 for s, r in [digit] + done)]
    parts = [lax.ppermute(value, "ta", [(i + j * stride, i) for i in keep]) for j in range(1, radix)]
    return sum((part.astype(F32) for part in parts), value.astype(F32)).astype(value.dtype)


def from_first(value, me, n, root=0):
    value = jnp.where(me == root, value, jnp.zeros_like(value))
    if root:
        value = shift(value, -root, n)
    digits = strides(n)
    for i in range(len(digits)):
        value = spread_round(value, digits[i], digits[:i], n)
    return value


def sum_all(value, n):
    step = 1
    while step < n:
        value = value + lax.ppermute(value, "ta", [(i, i ^ step) for i in range(n)])
        step *= 2
    return value


def tiles_of(rows, ni, nj):
    return rows.reshape(ni, 16, nj, 128).transpose(0, 2, 1, 3).reshape(ni * nj, 16, 128)


def rows_of(tiles, ni, nj):
    return tiles.reshape(ni, nj, 16, 128).transpose(0, 2, 1, 3).reshape(ni * nj * 16, 128)


PIECES = ((QKV0, 32, 12), (WO0, 32, 4), (WU0, 32, 16), (WD0, 128, 4))


def gather_plain(aligned):
    full = lax.all_gather(aligned.reshape(-1, 128), "ta", axis=0, tiled=True)
    return jnp.concatenate(
        [tiles_of(full[16 * b : 16 * (b + ni * nj)], ni, nj) for b, ni, nj in PIECES], axis=0
    )


def reduce_plain(tiles):
    full = jnp.concatenate([rows_of(tiles[b : b + ni * nj], ni, nj) for b, ni, nj in PIECES], axis=0)
    return lax.psum_scatter(full, "ta", scatter_dimension=0, tiled=True).astype(F32).reshape(-1)


def links(n, kind, by=1):
    pairs = []
    for i in range(n):
        if kind == "core":
            pairs.append((i, i ^ 1))
        elif kind == "z":
            pairs.append((i, (i + 8 * by) % n))
        else:
            pairs.append((i, i ^ (2 if (kind == "a") == (i % 2 == 0) else 4)))
    return pairs


def move(value, kind, by=1):
    return lax.ppermute(value, "ta", links(32, kind, by))


def after(value, *others):
    return lax.optimization_barrier((value,) + others)[0]


def to_tiles(rows, me):
    third = 3 * me + jnp.arange(3).reshape(3, 1, 1, 1)
    qkv = tiles_of(rows, 4, 12).reshape(3, 16, 16, 128)
    four = rows.reshape(3, 4, 16, 4, 128).transpose(0, 1, 3, 2, 4).reshape(3, 16, 16, 128)
    wide = rows.reshape(3, 16, 16, 128).transpose(0, 2, 1, 3)
    out = jnp.where(third < 24, qkv, jnp.where((third >= 32) & (third < 64), wide, four))
    return out.reshape(48, 16, 128)


def to_rows(tiles, me):
    third = 3 * me + jnp.arange(3).reshape(3, 1, 1)
    qkv = rows_of(tiles, 4, 12).reshape(3, 256, 128)
    four = tiles.reshape(3, 4, 4, 16, 128).transpose(0, 1, 3, 2, 4).reshape(3, 256, 128)
    wide = tiles.reshape(3, 16, 16, 128).transpose(0, 2, 1, 3).reshape(3, 256, 128)
    out = jnp.where(third < 24, qkv, jnp.where((third >= 32) & (third < 64), wide, four))
    return out.reshape(-1)


def head_rows(tiles, me):
    third = 3 * me
    four = ((third >= 24) & (third < 32)) | (third >= 64)
    return jnp.where(four, jnp.concatenate([tiles[:4, 0], tiles[:4, 1]], axis=0), tiles[:8, 0]).reshape(-1)


def per_device(frames, cotangent, mem_index, master, moment, second, average):
    n = lax.axis_size("ta")
    me = lax.axis_index("ta")
    mev = me.astype(jnp.int32).reshape(1)
    layers, share = master.shape
    step = 2 * D // n
    fast = n == GROUPS
    digits = strides(n)

    def vmem(*shape_types):
        return [pltpu.VMEM(shape, dtype) for shape, dtype in shape_types]

    def sems(count):
        return [pltpu.SemaphoreType.DMA((count,))]

    def call(kernel, ins, specs, outs, scratch, aliases=None, flops=3 * 10**9):
        return run(
            kernel, tuple(sds(*o) for o, _ in outs), tuple(ins), specs=specs,
            out_specs=tuple(VM if keep else ANYS for _, keep in outs), scratch=scratch,
            aliases=aliases, flops=flops, nbytes=10**7,
        )

    tf, tb = ((TOK, D), F32), ((TOK, D), BF16)
    wide, rows16, kv16 = ((TOK, FF), BF16), ((ROWS, D), BF16), ((ROWS, 2 * D), BF16)
    prob, rows32, kv32 = ((NBLK * 4, KB, 128), BF16), ((ROWS, D), F32), ((ROWS, 2 * D), F32)
    drow, dtab_t, sums = ((1, D), F32), ((128, D), F32), ((NSEG, D), BF16)
    tiles_t = ((TILES, 16, 128), BF16)
    score = ((NBLK * 4, KB, 128), F32)
    wscr = vmem(tiles_t) + sems(GROUPS + 1)

    msgs = [(((LH + NSEG, D), BF16), True), (((RH, D), BF16), True), (sums, True), (sums, True)]

    def forward_moves(ahead, back, summ):
        return shift(ahead, 1, n), shift(back, -1, n), shift(summ, 2, n)

    tail = shift(master[:, share - 2 * D :], 1, n)
    ahead, back, root, summ = call(first_kernel, (mev, frames), [SM, VM], msgs, [], flops=10**7)
    ahead, back, root, summ, tail = lax.optimization_barrier((ahead, back, root, summ, tail))
    hl, hr, behind2 = forward_moves(ahead, back, summ)

    ext = jnp.concatenate([tail, master], axis=1)
    aligned = lax.dynamic_slice(ext, (0, 2 * D - step * me), (layers, MATS // n)).astype(BF16)
    gains = master[:, share - 2 * D :].astype(BF16).reshape(1, 16, 128)
    if fast:
        tiles = [to_tiles(aligned[l].reshape(-1, 128), me) for l in range(layers)]
        zd = 2
        for i in range(zd):
            root = spread_round(root, digits[i], digits[:i], n)
        b0 = after(jnp.concatenate([tiles[0], gains]), root, hl, hr, behind2)
        own0 = jnp.stack([b0] + [move(b0, "z", k) for k in range(1, 4)])
        for i in range(zd, len(digits)):
            root = spread_round(root, digits[i], digits[:i], n)
        own0 = after(own0, root)
        a0, s0 = move(own0, "a"), move(own0, "b")
        b1 = after(tiles[1], own0)
        own1 = jnp.stack([b1] + [move(b1, "z", k) for k in range(1, 4)])
        a0 = after(a0, s0, own1)
        as0 = move(a0, "b")
        w0 = [own0, a0, s0, as0]
        w0 += [move(after(v, own1), "core") for v in w0]
        a1, s1 = move(own1, "a"), move(own1, "b")
        w0 = tuple(w0)
    else:
        w0 = (gather_plain(aligned[0]), from_first(gains[0], me, n, n - 1))
        root = from_first(root, me, n)
    low_parts = (hl, hr, root, behind2, summ)

    first_seg = me * NSEG
    seg_ids = first_seg + jnp.arange(NSEG, dtype=jnp.int32)
    slot = jnp.arange(MEM, dtype=jnp.int32)
    loc = jnp.where(slot[None, :] == 0, mem_index, mem_index - first_seg + 96).reshape(-1, 1)
    loc = jnp.broadcast_to(loc, (NSEG * MEM, 128))
    vis = (mem_index < seg_ids[:, None]).astype(F32).reshape(-1, 1)
    vis = jnp.broadcast_to(vis, (NSEG * MEM, 128))

    hid = (rows16, tb, kv16, prob, tb)
    gt, hx0, q0, kv0, p0, o0 = call(
        functools.partial(low_attn_kernel, np_=len(w0), n=n), (mev, frames, *low_parts, loc, vis) + w0,
        [SM] + [VM] * 8 + [ANYS] * len(w0), [(((16, 128), BF16), True)] + [(t, False) for t in hid],
        wscr + vmem(*hid, score) + sems(5),
    )
    if fast:
        a1 = after(a1, o0)
        as1 = move(a1, "b")
        w1 = [own1, a1, s1]
        w1 = w1 + [as1] + [move(after(v, o0), "core") for v in w1]
    hid = (tf, tb, wide, wide)
    x1, h1, ahead, back, root, summ, a0, h20, gp0, act0 = call(
        functools.partial(low_ffn_kernel, np_=len(w0)), (mev, frames, o0, gt) + w0,
        [SM] + [VM] * 3 + [ANYS] * len(w0), [(tf, True), (tb, True)] + msgs + [(t, False) for t in hid],
        wscr + vmem(*hid) + sems(4),
    )
    if fast:
        ahead, back, root, summ, as1, *_ = lax.optimization_barrier((ahead, back, root, summ, as1, *w1[4:]))
        w1[3] = as1
    hl, hr, behind2 = forward_moves(ahead, back, summ)
    for i in range(len(digits)):
        root = spread_round(root, digits[i], digits[:i], n)
        if i == 1:
            root = after(root, hl, hr, behind2)
    if fast:
        w1 = tuple(w1 + [move(as1, "core")])
    else:
        w1 = (gather_plain(aligned[1]),)

    def grads_out(kind):
        shapes = ((LH + NSEG, D), kind), ((RH, D), kind), ((NSEG, D), kind), ((NSEG, D), kind), ((NSEG, D), F32)
        return [(tf, True)] + [(shape, True) for shape in shapes]

    kept = (rows16, tb, tb, wide, tb, wide, tb, tb, kv16)
    output, da, dh, hal, har, root, b2, mine, dgb1, hx1, o1, h21, act1, dxb, dub, dab, dq, dkvb = call(
        functools.partial(top_kernel, np_=len(w1), n=n),
        (mev, x1, h1, hl, hr, root, behind2, summ, loc, vis, gt, cotangent) + w1,
        [SM] + [VM] * 10 + [ANYS] * (1 + len(w1)),
        [(tf, False), (tf, True)] + grads_out(BF16) + [(drow, True)] + [(t, False) for t in kept],
        wscr + vmem(rows16, tb, kv16, prob, tb, tf, tb, wide, wide, tf, tf, tb, wide, tb, tb, kv16, kv32, tb, rows32, score) + sems(11),
        flops=8 * 10**9,
    )

    def backward_moves(hal, har, b2):
        return shift(hal, -1, n), shift(har, 1, n), shift(b2, -2, n)

    tree = digits[-1:] + digits[:-1]

    def collect(root, i):
        return collect_round(root, tree[i], tree[:i], n)

    dws = vmem(rows16, tb, kv16, tb, tb, tb, wide, wide, tb, tiles_t)
    dws += [pltpu.SemaphoreType.DMA] + sems(9)

    def weight_grads(part, ins, partial, gains=None):
        extra = BT + (1 if fast and gains_in else 0)
        outs = [(((2, 2, 4, extra, 16, 128), BF16), False)] * 2 if fast else [(tiles_t, False)]
        count = len(outs)
        ins = [mev] + list(ins) + ([] if gains is None else [gains])
        specs = [SM] + [ANYS] * 9 + [VM] * (len(ins) - 10)
        return call(
            functools.partial(dw_kernel, part=part, nouts=count, gains=gains is not None),
            ins + list(partial), specs + [ANYS] * len(partial), outs, dws,
            aliases={len(ins) + i: i for i in range(len(partial))}, flops=10**9,
        )

    gains_in = False
    hal, har, b2 = backward_moves(hal, har, b2)
    root = collect(root, 0)
    ins = [hx1, dq, dkvb, o1, dab, h21, dub, act1, after(dxb, root, hal, har, b2)]
    part = ()
    for i in range(2):
        part = weight_grads(i, ins, part)
        root = collect(root, i + 1)
        ins[6], ins[4] = after(dub, root), after(dab, root)
        root = after(root, part[0])
    for i in range(3, len(tree)):
        root = collect(root, i)
    grads = weight_grads(2, ins, part)

    def add(a, b):
        return (a.astype(F32) + b.astype(F32)).astype(BF16)

    if fast:
        v1 = after(add(grads[0], move(grads[1], "core")), root)
        got = move(v1[1], "b")
        x1 = after(x1, v1)
    else:
        reduced1 = reduce_plain(grads[0])

    dga1, da, dgb0, dxb, dub, dab = call(
        functools.partial(bottom_ffn_kernel, np_=len(w0)), (mev, hal, har, root, b2, mine, dh, x1, da, gt) + w0 + (a0, gp0),
        [SM] + [VM] * 9 + [ANYS] * (len(w0) + 2),
        [(drow, True), (tf, True), (drow, True), (tb, False), (wide, False), (tb, False)],
        wscr + vmem(tf, wide, tf, tb, wide, tb) + sems(5),
    )
    dga0, dh, hal, har, root, b2, mine, dq, dkvb = call(
        functools.partial(bottom_attn_kernel, np_=len(w0)),
        (mev, dab, loc, frames) + low_parts + w0 + (q0, kv0, p0), [SM] + [VM] * 8 + [ANYS] * (len(w0) + 3),
        [(drow, True)] + grads_out(F32) + [(tb, False), (kv16, False)],
        wscr + vmem(tb, kv16, prob, tb, kv16, kv32, tb, rows32, score) + sems(5),
    )
    gains = jnp.concatenate([dga0, dgb0, dga1, dgb1], axis=1)
    ins = [hx0, dq, dkvb, o0, dab, h20, dub, act0, dxb]
    if fast:
        v1 = add(after(v1[0], dh), got)
        got = move(v1[1], "a")
        ins[8] = after(dxb, v1)
        gains_in = True
    part = ()
    for i in range(2):
        part = weight_grads(i, ins, part)
    if fast:
        v1 = add(after(v1[0], part[0]), got)
        z1 = [move(v1[k], "z", k) for k in range(1, 4)]
        ins[4] = after(dab, v1)
    grads = weight_grads(2, ins, part, gains.astype(BF16).reshape(16, 128) if fast else None)
    if fast:
        v = add(grads[0], move(grads[1], "core"))
        root = collect(after(root, v), 0)
        got = move(v[1], "b")
        v = add(v[0], got)
        total1 = functools.reduce(jnp.add, [z.astype(F32) for z in z1], after(v1[0], v).astype(F32))
        got = move(v[1], "a")
        root = collect(collect(after(root, v, total1), 1), 2)
        reduced1, head1 = to_rows(total1, me), shift(head_rows(total1, me), -1, n)
        v = add(v[0], got)
        root = after(root, v, head1)
        zs = [move(v[k], "z", k) for k in range(1, 4)]
        for i in range(3, len(tree)):
            root = collect(root, i)
        hal, har, b2 = backward_moves(hal, har, after(b2, v))
        total0 = functools.reduce(jnp.add, [z.astype(F32) for z in zs], v[0].astype(F32))
        gsum = total0[BT].reshape(layers, 2 * D)
        total0 = total0[:BT]
        reduced = [to_rows(total0, me), reduced1]
        heads = [shift(head_rows(total0, me), -1, n), head1]
    else:
        hal, har, b2 = backward_moves(hal, har, b2)
        for i in range(len(tree)):
            root = collect(root, i)
        gsum = sum_all(gains.reshape(layers, 2 * D), n)
        reduced = [reduce_plain(grads[0]), reduced1]
        heads = [shift(r[: 2 * D], -1, n) for r in reduced]
    dx = call(
        last_kernel, (mev, hal, har, root, b2, mine, dh, frames, da, gt),
        [SM] + [VM] * 9, [(tf, True)], vmem(tf), flops=10**7,
    )[0]

    own = jnp.stack(reduced)
    head = jnp.where(me == n - 1, gsum, jnp.stack(heads))
    grad = lax.dynamic_slice(jnp.concatenate([own, head], axis=1), (0, step * me), (layers, share))
    gain_out = lax.dynamic_slice(gsum, (0, step * me), (layers, step))
    new_moment = 0.5 * moment + 0.5 * grad
    new_second = 0.5 * second + 0.5 * grad * grad
    correction = 1.0 - 0.5**STEP
    update = new_moment / correction / (jnp.sqrt(new_second / correction) + 1e-08) + 0.1 * master
    new_master = master - 0.08 * update
    new_average = 0.9 * average + 0.1 * new_master
    return (output, dx, gain_out, new_moment, new_second, new_master, new_average)


def solution(mesh):
    rows, flat = P("ta", None), P(None, "ta")
    return jax.shard_map(
        per_device,
        mesh=mesh,
        in_specs=(rows, rows, rows, flat, flat, flat, flat),
        out_specs=(rows, rows, flat, flat, flat, flat, flat),
        check_vma=False,
    )
```

```python
import functools

import jax
import jax.numpy as jnp
from jax import lax
from jax.experimental import pallas as pl
from jax.experimental.pallas import tpu as pltpu
from jax.sharding import PartitionSpec as P

D = 512
HEADS = 8
FF = 2048
SEG = 16
LEFT = 30
RIGHT = 4
MEM = 4
STEP = 10
UN = 8
NEG = -1e30

TOK = 512
NSEG = TOK // SEG
LH = 32
RH = 16
EXT = LH + TOK + 2 * RH
ROWS = EXT + NSEG * MEM
BLK = 4
NBLK = NSEG // BLK
QB = BLK * SEG
KB = 128
WB = KB - BLK * MEM

TILES = 1536
QKV0, WO0, WU0, WD0 = 0, 384, 512, 1024
MATS = TILES * 16 * 128
GROUPS = 32
BT = TILES // GROUPS

F32 = jnp.float32
BF16 = jnp.bfloat16
VM = pl.BlockSpec(memory_space=pltpu.VMEM)
SM = pl.BlockSpec(memory_space=pltpu.SMEM)
ANYS = pl.BlockSpec(memory_space=pl.ANY)


def mm(a, b):
    return lax.dot_general(a, b, (((1,), (0,)), ((), ())), preferred_element_type=F32)


def mm_nt(a, b):
    return lax.dot_general(a, b, (((1,), (1,)), ((), ())), preferred_element_type=F32)


def mm_tn(a, b):
    return lax.dot_general(a, b, (((0,), (0,)), ((), ())), preferred_element_type=F32)


def wblk(w, base, nj, i0, ni, j0, nj_take):
    cols = [
        jnp.concatenate([w[base + (i0 + i) * nj + j0 + j] for i in range(ni)], axis=0)
        for j in range(nj_take)
    ]
    return cols[0] if nj_take == 1 else jnp.concatenate(cols, axis=1)


def place(me, rc, ra, rb, k):
    core = (me % 2) ^ rc
    x = ((me // 2) % 2) ^ jnp.where(core == 0, ra, rb)
    y = ((me // 4) % 2) ^ jnp.where(core == 0, rb, ra)
    z = (me // 8 + k) % 4
    return ((z * 2 + y) * 2 + x) * 2 + core


def load_weights(me, pieces, w_ref, sems, lo, hi, gt_ref=None):
    if len(pieces) < 8:
        if gt_ref is not None:
            pltpu.make_async_copy(pieces[1], gt_ref, sems.at[GROUPS]).start()
        for d in range(lo, hi):
            t = pl.ds(BT * d, BT)
            pltpu.make_async_copy(pieces[0].at[t], w_ref.at[t], sems.at[d]).start()
        return
    for rc in range(2):
        for m in range(4):
            for k in range(4):
                d = place(me, rc, m % 2, m // 2, -k % 4)
                piece = pieces[4 * rc + m].at[k]

                @pl.when((d >= lo) & (d < hi))
                def _():
                    pltpu.make_async_copy(
                        piece.at[pl.ds(0, BT)], w_ref.at[pl.ds(d * BT, BT)], sems.at[d]
                    ).start()

                if gt_ref is not None:

                    @pl.when(d == GROUPS - 1)
                    def _():
                        pltpu.make_async_copy(piece.at[BT], gt_ref, sems.at[GROUPS]).start()


def await_weights(w_ref, sems, lo, hi):
    for d in range(lo, hi):
        part = w_ref.at[pl.ds(d * BT, BT)]
        pltpu.make_async_copy(part, part, sems.at[d]).wait()


def gain_row(g_ref, layer, which):
    g = g_ref[...].astype(F32)
    r = 8 * layer + 4 * which
    return jnp.concatenate([g[r + k : r + k + 1] for k in range(4)], axis=1)


def norm_parts(v):
    mean = jnp.mean(v, axis=-1, keepdims=True)
    cen = v - mean
    rstd = lax.rsqrt(jnp.mean(cen * cen, axis=-1, keepdims=True) + 1e-05)
    return cen * rstd, rstd


def norm_back(dh, xhat, rstd, gain):
    dx = dh * gain
    return rstd * (
        dx
        - jnp.mean(dx, axis=-1, keepdims=True)
        - xhat * jnp.mean(dx * xhat, axis=-1, keepdims=True)
    )


def seg_mean(h):
    return (jnp.sum(h.astype(F32).reshape(NSEG, SEG, D), axis=1) * (1.0 / SEG)).astype(BF16)


def head_of_layer(x, gain):
    xhat, _ = norm_parts(x)
    h1 = (xhat * gain).astype(BF16)
    return h1, seg_mean(h1)


def send_on(me, rows_ref, means, ahead_ref, back_ref, root_ref, sum_ref):
    sum_ref[...] = means
    ahead_ref[0:LH] = rows_ref[TOK - LH : TOK]
    ahead_ref[LH:] = means
    back_ref[...] = rows_ref[0:RH]
    root_ref[...] = jnp.where(me == 0, means, jnp.zeros_like(means))


def first_kernel(me_ref, x_ref, ahead_ref, back_ref, root_ref, sum_ref):
    xhat, _ = norm_parts(x_ref[...].astype(F32))
    send_on(me_ref[0], x_ref, seg_mean(xhat), ahead_ref, back_ref, root_ref, sum_ref)


def lane_lo(rows):
    return lax.broadcasted_iota(jnp.int32, (rows, 128), 1) < 64


def split_heads(m, lo):
    z = jnp.zeros_like(m)
    return jnp.concatenate([jnp.where(lo, m, z), jnp.where(lo, z, m)], axis=0)


def onehot_of(loc_ref):
    ids = lax.broadcasted_iota(jnp.int32, (NSEG * MEM, 128), 1)
    return jnp.where(loc_ref[...] == ids, 1.0, 0.0).astype(BF16)


def block_keys(kv_ref, b, col):
    r0 = pl.multiple_of(b * QB, QB)
    m0 = pl.multiple_of(EXT + b * (BLK * MEM), BLK * MEM)
    return jnp.concatenate(
        [kv_ref[pl.ds(r0, WB), col : col + 128], kv_ref[pl.ds(m0, BLK * MEM), col : col + 128]], axis=0
    )


def attend(me, n, q_ref, kv_ref, vis_ref, p_ref, o_ref, s_ref):
    ki = lax.broadcasted_iota(jnp.int32, (KB, 128), 0)
    qi = (lax.broadcasted_iota(jnp.int32, (KB, 128), 1) % QB) // SEG
    off = ki - SEG * qi - (LH - LEFT)
    near = jnp.where((off >= 0) & (off < LEFT + SEG + RIGHT) & (ki < WB), 1.0, 0.0)
    memb = jnp.where((ki >= WB) & ((ki - WB) // MEM == qi), 1.0, 0.0)
    first = jnp.where(me == 0, LH, 0)
    end = jnp.where(me == n - 1, LH + TOK, EXT)
    lo = lane_lo(QB)

    def scores(b, carry):
        r0 = pl.multiple_of(b * QB, QB)
        m0 = pl.multiple_of(b * (BLK * MEM), BLK * MEM)
        inside = (ki + r0 >= first) & (ki + r0 < end)
        memv = jnp.concatenate(
            [jnp.zeros((WB, 128), F32), vis_ref[pl.ds(m0, BLK * MEM), :]], axis=0
        )
        seen = jnp.where(inside, near, 0.0) + memb * memv > 0.5
        for p in range(4):
            kc = block_keys(kv_ref, b, 128 * p)
            s = mm_nt(kc, split_heads(q_ref[pl.ds(r0, QB), 128 * p : 128 * p + 128], lo))
            s_ref[b * 4 + p] = jnp.where(seen, s, NEG)
        return carry

    def softmax(i, carry):
        s = s_ref[i]
        e = jnp.exp(s - jnp.max(s, axis=0, keepdims=True))
        p_ref[i] = (e * (1.0 / jnp.sum(e, axis=0, keepdims=True))).astype(BF16)
        return carry

    def mix(b, carry):
        r0 = pl.multiple_of(b * QB, QB)
        for p in range(4):
            o2 = mm_tn(p_ref[b * 4 + p], block_keys(kv_ref, b, D + 128 * p))
            o_ref[pl.ds(r0, QB), 128 * p : 128 * p + 128] = jnp.where(lo, o2[:QB], o2[QB:]).astype(BF16)
        return carry

    lax.fori_loop(0, NBLK, scores, 0, unroll=UN)
    lax.fori_loop(0, 4 * NBLK, softmax, 0, unroll=8)
    lax.fori_loop(0, NBLK, mix, 0, unroll=UN)


def attend_back(q_ref, kv_ref, p_ref, do_ref, dq_ref, dkv_ref, s_ref):
    dkv_ref[...] = jnp.zeros_like(dkv_ref)
    lo = lane_lo(QB)

    def weights(b, carry):
        r0 = pl.multiple_of(b * QB, QB)
        m0 = pl.multiple_of(EXT + b * (BLK * MEM), BLK * MEM)
        for p in range(4):
            vc0 = D + 128 * p
            dd = split_heads(do_ref[pl.ds(r0, QB), 128 * p : 128 * p + 128], lo)
            s_ref[b * 4 + p] = mm_nt(block_keys(kv_ref, b, vc0), dd)
            dv = mm(p_ref[b * 4 + p], dd)
            dkv_ref[pl.ds(r0, WB), vc0 : vc0 + 128] += dv[:WB]
            dkv_ref[pl.ds(m0, BLK * MEM), vc0 : vc0 + 128] = dv[WB:]
        return carry

    def softmax(i, carry):
        pf = p_ref[i].astype(F32)
        pd = pf * s_ref[i]
        p_ref[i] = (pd - pf * jnp.sum(pd, axis=0, keepdims=True)).astype(BF16)
        return carry

    def queries(b, carry):
        r0 = pl.multiple_of(b * QB, QB)
        m0 = pl.multiple_of(EXT + b * (BLK * MEM), BLK * MEM)
        for p in range(4):
            kc0 = 128 * p
            ds = p_ref[b * 4 + p]
            dk = mm(ds, split_heads(q_ref[pl.ds(r0, QB), kc0 : kc0 + 128], lo))
            dq2 = mm_tn(ds, block_keys(kv_ref, b, kc0))
            dq_ref[pl.ds(r0, QB), kc0 : kc0 + 128] = (jnp.where(lo, dq2[:QB], dq2[QB:]) * 0.125).astype(BF16)
            dkv_ref[pl.ds(r0, WB), kc0 : kc0 + 128] += dk[:WB]
            dkv_ref[pl.ds(m0, BLK * MEM), kc0 : kc0 + 128] = dk[WB:]
        return carry

    lax.fori_loop(0, NBLK, weights, 0, unroll=UN)
    lax.fori_loop(0, 4 * NBLK, softmax, 0, unroll=8)
    lax.fori_loop(0, NBLK, queries, 0, unroll=UN)


class Copies:
    def __init__(self, sems):
        self.sems, self.used, self.open = sems, 0, []

    def start(self, src, dst):
        copy = pltpu.make_async_copy(src, dst, self.sems.at[self.used])
        self.used += 1
        copy.start()
        return copy

    def out(self, src, dst):
        self.open.append(self.start(src, dst))

    def finish(self):
        for copy in self.open:
            copy.wait()


def project(hx_ref, w_ref, q_ref, kv_ref):
    q = mm(hx_ref[LH : LH + TOK], wblk(w_ref, QKV0, 12, 0, 32, 0, 4)).astype(BF16)
    q_ref[...] = q * jnp.asarray(0.125, BF16)
    for j in range(2):
        kv_ref[:, 512 * j : 512 * j + 512] = mm(hx_ref[...], wblk(w_ref, QKV0, 12, 0, 32, 4 + 4 * j, 4)).astype(BF16)


def feed_forward(h2_ref, w_ref, act_ref, gp_ref, out_ref, ready):
    for c in range(4):
        u = mm(h2_ref[...], wblk(w_ref, WU0, 16, 0, 32, 4 * c, 4))
        cc, c3 = 0.7978845608028654, 0.7978845608028654 * 0.044715
        u2 = u * u
        t = jnp.tanh(u * (cc + c3 * u2))
        hu = 0.5 * u
        act = (hu + hu * t).astype(BF16)
        gp = 0.5 + 0.5 * t + hu * (1.0 - t * t) * (cc + 3 * c3 * u2)
        act_ref[:, 512 * c : 512 * c + 512] = act
        gp_ref[:, 512 * c : 512 * c + 512] = gp.astype(BF16)
        if c == 0:
            ready()
        out_ref[...] += mm(act, wblk(w_ref, WD0, 4, 32 * c, 32, 0, 4))


def back_ffn(dx_ref, w_ref, gains, a_ref, gp_ref, da_ref, dxb_ref, dub_ref, dab_ref, dgb_ref, step):
    dxb_ref[...] = dx_ref[...].astype(BF16)
    step("dxb")
    for c in range(4):
        dact = mm_nt(dxb_ref[...], wblk(w_ref, WD0, 4, 32 * c, 32, 0, 4))
        du = (dact * gp_ref[:, 512 * c : 512 * c + 512].astype(F32)).astype(BF16)
        dub_ref[:, 512 * c : 512 * c + 512] = du
        dh2 = mm_nt(du, wblk(w_ref, WU0, 16, 0, 32, 4 * c, 4))
        if c:
            da_ref[...] += dh2
        else:
            da_ref[...] = dh2
    step("dub")
    xhat, rstd = norm_parts(a_ref[...])
    dh2 = da_ref[...]
    dgb_ref[...] = jnp.sum(dh2 * xhat, axis=0, keepdims=True)
    da = dx_ref[...] + norm_back(dh2, xhat, rstd, gains)
    da_ref[...] = da
    dab_ref[...] = da.astype(BF16)
    step("dab")


def back_attn(dab_ref, w_ref, q_ref, kv_ref, p_ref, dq_ref, dkvb_ref, dh_ref, dkv_ref, dob_ref, s_ref, step):
    dob_ref[...] = mm_nt(dab_ref[...], wblk(w_ref, WO0, 4, 0, 32, 0, 4)).astype(BF16)
    step("attend")
    attend_back(q_ref, kv_ref, p_ref, dob_ref, dq_ref, dkv_ref, s_ref)
    dkvb_ref[...] = dkv_ref[...].astype(BF16)
    step("dkvb")
    dh_ref[...] = mm_nt(dkvb_ref[...], wblk(w_ref, QKV0, 12, 0, 32, 4, 8))
    dh_ref[LH : LH + TOK] += mm_nt(dq_ref[...], wblk(w_ref, QKV0, 12, 0, 32, 0, 4))


def table_grad(loc_ref, dh_ref, hal_ref, har_ref, root_ref, b2_ref, mine_ref):
    dch = dh_ref[EXT:ROWS]
    hi = dch.astype(BF16)
    oh = onehot_of(loc_ref)
    dtab = mm_tn(oh, hi) + mm_tn(oh, (dch - hi.astype(F32)).astype(BF16))
    kind = hal_ref.dtype
    hal_ref[0:LH] = dh_ref[0:LH].astype(kind)
    hal_ref[LH:] = dtab[64:96].astype(kind)
    har_ref[...] = dh_ref[LH + TOK : LH + TOK + RH].astype(kind)
    root_ref[...] = dtab[0:32].astype(kind)
    b2_ref[...] = dtab[32:64].astype(kind)
    mine_ref[...] = dtab[96:128]
    return dtab


def low_attn_kernel(me_ref, x_ref, hl_ref, hr_ref, root_ref, b2_ref, summ_ref, loc_ref, vis_ref, *rest, np_, n):
    pieces, rest = rest[:np_], rest[np_:]
    gt_ref, hx_o, q_o, kv_o, p_o, o_o, w_ref, sems, hx_ref, q_ref, kv_ref, p_ref, o_ref, s_ref, osem = rest
    me = me_ref[0]
    load_weights(me, pieces, w_ref, sems, 0, 8, gt_ref)
    copies = Copies(osem)
    pltpu.make_async_copy(gt_ref, gt_ref, sems.at[GROUPS]).wait()
    ga = gain_row(gt_ref, 0, 0)
    for ref, rows, at in ((hl_ref, LH, 0), (x_ref, TOK, LH), (hr_ref, RH, LH + TOK)):
        xhat, _ = norm_parts(ref[0:rows].astype(F32))
        hx_ref[at : at + rows] = (xhat * ga).astype(BF16)
    means = jnp.concatenate([root_ref[...], b2_ref[...], hl_ref[LH:], summ_ref[...]], axis=0)
    hx_ref[LH + TOK + RH : EXT] = jnp.zeros((RH, D), BF16)
    hx_ref[EXT:ROWS] = mm(onehot_of(loc_ref), (means.astype(F32) * ga).astype(BF16)).astype(BF16)
    copies.out(hx_ref, hx_o)
    await_weights(w_ref, sems, 0, 8)
    project(hx_ref, w_ref, q_ref, kv_ref)
    copies.out(q_ref, q_o)
    copies.out(kv_ref, kv_o)
    attend(me, n, q_ref, kv_ref, vis_ref, p_ref, o_ref, s_ref)
    copies.out(p_ref, p_o)
    copies.out(o_ref, o_o)
    copies.finish()


def low_ffn_kernel(me_ref, x_ref, o_ref, gt_ref, *rest, np_):
    pieces, rest = rest[:np_], rest[np_:]
    (out_ref, h1n_ref, ahead_ref, back_ref, root_ref, sumn_ref, a_o, h2_o, gp_o, act_o,
     w_ref, sems, a_ref, h2_ref, gp_ref, act_ref, osem) = rest
    load_weights(me_ref[0], pieces, w_ref, sems, 8, 32)
    copies = Copies(osem)
    await_weights(w_ref, sems, 8, 11)
    a = x_ref[...].astype(F32) + mm(o_ref[...], wblk(w_ref, WO0, 4, 0, 32, 0, 4))
    a_ref[...] = a
    copies.out(a_ref, a_o)
    xhat, _ = norm_parts(a)
    h2_ref[...] = (xhat * gain_row(gt_ref, 0, 1)).astype(BF16)
    copies.out(h2_ref, h2_o)
    out_ref[...] = a
    await_weights(w_ref, sems, 11, 22)
    feed_forward(h2_ref, w_ref, act_ref, gp_ref, out_ref, lambda: await_weights(w_ref, sems, 22, 32))
    copies.out(act_ref, act_o)
    copies.out(gp_ref, gp_o)
    h1n, sumn = head_of_layer(out_ref[...], gain_row(gt_ref, 1, 0))
    h1n_ref[...] = h1n
    send_on(me_ref[0], h1n_ref, sumn, ahead_ref, back_ref, root_ref, sumn_ref)
    copies.finish()


def top_kernel(me_ref, x_ref, h1_ref, hl_ref, hr_ref, root_ref, b2_ref, summ_ref, loc_ref, vis_ref, gt_ref, cot_any,
               *rest, np_, n):
    pieces, rest = rest[:np_], rest[np_:]
    (out_o, da_ref, dhown_ref, hal_ref, har_ref, rootg_ref, b2g_ref, mine_ref, dgb_ref, hx_o, o_o, h2_o, act_o, dxb_o, dub_o, dab_o, dq_o, dkvb_o,
     w_ref, sems, hx_ref, q_ref, kv_ref, p_ref, o_ref, a_ref, h2_ref, gp_ref, act_ref,
     out_ref, dx_ref, dxb_ref, dub_ref, dab_ref, dq_ref, dkvb_ref, dkv_ref, dob_ref, dh_ref, s_ref, osem) = rest
    me = me_ref[0]
    load_weights(me, pieces, w_ref, sems, 0, 32)
    copies = Copies(osem)
    cot = copies.start(cot_any, dx_ref)
    hx_ref[0:LH] = hl_ref[0:LH]
    hx_ref[LH : LH + TOK] = h1_ref[...]
    hx_ref[LH + TOK : LH + TOK + RH] = hr_ref[...]
    hx_ref[LH + TOK + RH : EXT] = jnp.zeros((RH, D), BF16)
    table = jnp.concatenate([root_ref[...], b2_ref[...], hl_ref[LH:], summ_ref[...]], axis=0)
    hx_ref[EXT:ROWS] = mm(onehot_of(loc_ref), table).astype(BF16)
    copies.out(hx_ref, hx_o)
    await_weights(w_ref, sems, 0, 8)
    project(hx_ref, w_ref, q_ref, kv_ref)
    attend(me, n, q_ref, kv_ref, vis_ref, p_ref, o_ref, s_ref)
    copies.out(o_ref, o_o)
    await_weights(w_ref, sems, 8, 32)
    a = x_ref[...] + mm(o_ref[...], wblk(w_ref, WO0, 4, 0, 32, 0, 4))
    a_ref[...] = a
    xhat, _ = norm_parts(a)
    h2_ref[...] = (xhat * gain_row(gt_ref, 1, 1)).astype(BF16)
    copies.out(h2_ref, h2_o)
    out_ref[...] = a
    feed_forward(h2_ref, w_ref, act_ref, gp_ref, out_ref, lambda: None)
    copies.out(act_ref, act_o)
    copies.out(out_ref, out_o)
    cot.wait()
    done = {"dxb": ((dxb_ref, dxb_o),), "dub": ((dub_ref, dub_o),), "dab": ((dab_ref, dab_o),),
            "dkvb": ((dkvb_ref, dkvb_o), (dq_ref, dq_o))}

    def step(name):
        for pair in done.get(name, ()):
            copies.out(*pair)

    back_ffn(dx_ref, w_ref, gain_row(gt_ref, 1, 1), a_ref, gp_ref, da_ref, dxb_ref, dub_ref, dab_ref, dgb_ref, step)
    back_attn(dab_ref, w_ref, q_ref, kv_ref, p_ref, dq_ref, dkvb_ref, dh_ref, dkv_ref, dob_ref, s_ref, step)
    dhown_ref[...] = dh_ref[LH : LH + TOK]
    table_grad(loc_ref, dh_ref, hal_ref, har_ref, rootg_ref, b2g_ref, mine_ref)
    copies.finish()


def norm_one_back(dh_ref, hal_ref, har_ref, dsum, x, gain, da_ref, acc_ref):
    acc_ref[...] = dh_ref[...]
    acc_ref[TOK - LH : TOK] += hal_ref[0:LH].astype(F32)
    acc_ref[0:RH] += har_ref[...].astype(F32)
    for s in range(NSEG):
        acc_ref[SEG * s : SEG * s + SEG] += dsum[s : s + 1, :] * (1.0 / SEG)
    xhat, rstd = norm_parts(x)
    dh = acc_ref[...]
    return da_ref[...] + norm_back(dh, xhat, rstd, gain), jnp.sum(dh * xhat, axis=0, keepdims=True)


def summed(me_ref, hal_ref, root_ref, b2_ref, mine_ref):
    near = mine_ref[...] + hal_ref[LH:].astype(F32) + b2_ref[...].astype(F32)
    return near + jnp.where(me_ref[0] == 0, root_ref[...].astype(F32), 0.0)


def bottom_ffn_kernel(me_ref, hal_ref, har_ref, root_ref, b2_ref, dtabp_ref, dhp_ref, x_ref, dap_ref, gt_ref, *rest, np_):
    pieces, rest = rest[:np_], rest[np_:]
    (a_any, gp_any, dga_ref, da_ref, dgb_ref, dxb_o, dub_o, dab_o,
     w_ref, sems, a_ref, gp_ref, dx_ref, dxb_ref, dub_ref, dab_ref, osem) = rest
    load_weights(me_ref[0], pieces, w_ref, sems, 10, 32)
    copies = Copies(osem)
    loads = [copies.start(*pair) for pair in ((gp_any, gp_ref), (a_any, a_ref))]
    dx, dga = norm_one_back(
        dhp_ref, hal_ref, har_ref, summed(me_ref, hal_ref, root_ref, b2_ref, dtabp_ref), x_ref[...],
        gain_row(gt_ref, 1, 0), dap_ref, dx_ref,
    )
    dx_ref[...] = dx
    dga_ref[...] = dga
    await_weights(w_ref, sems, 10, 32)
    loads[0].wait()
    done = {"dxb": (dxb_ref, dxb_o), "dub": (dub_ref, dub_o), "dab": (dab_ref, dab_o)}

    def step(name):
        if name == "dub":
            loads[1].wait()
        copies.out(*done[name])

    back_ffn(dx_ref, w_ref, gain_row(gt_ref, 0, 1), a_ref, gp_ref, da_ref, dxb_ref, dub_ref, dab_ref, dgb_ref, step)
    copies.finish()


def bottom_attn_kernel(me_ref, dab_ref, loc_ref, frames_ref, ahead0_ref, hr0_ref, root0_ref, b20_ref, summ0_ref, *rest, np_):
    pieces, rest = rest[:np_], rest[np_:]
    (q_any, kv_any, p_any, dga_ref, dhown_ref, hal_ref, har_ref, rootg_ref, b2g_ref, mine_ref, dq_o, dkvb_o,
     w_ref, sems, q_ref, kv_ref, p_ref, dq_ref, dkvb_ref, dkv_ref, dob_ref, dh_ref, s_ref, osem) = rest
    load_weights(me_ref[0], pieces, w_ref, sems, 0, 11)
    copies = Copies(osem)
    loads = [copies.start(*pair) for pair in ((q_any, q_ref), (kv_any, kv_ref), (p_any, p_ref))]
    await_weights(w_ref, sems, 0, 11)

    def step(name):
        if name == "attend":
            for load in loads:
                load.wait()
        else:
            copies.out(dkvb_ref, dkvb_o)
            copies.out(dq_ref, dq_o)

    back_attn(dab_ref, w_ref, q_ref, kv_ref, p_ref, dq_ref, dkvb_ref, dh_ref, dkv_ref, dob_ref, s_ref, step)
    dhown_ref[...] = dh_ref[LH : LH + TOK]
    dtab = table_grad(loc_ref, dh_ref, hal_ref, har_ref, rootg_ref, b2g_ref, mine_ref)
    means = jnp.concatenate([root0_ref[...], b20_ref[...], ahead0_ref[LH:], summ0_ref[...]], axis=0)
    total = jnp.sum(dtab * means.astype(F32), axis=0, keepdims=True)
    for ref, rows, at in ((ahead0_ref, LH, 0), (frames_ref, TOK, LH), (hr0_ref, RH, LH + TOK)):
        xhat, _ = norm_parts(ref[0:rows].astype(F32))
        total += jnp.sum(dh_ref[at : at + rows] * xhat, axis=0, keepdims=True)
    dga_ref[...] = total
    copies.finish()


def last_kernel(me_ref, hal_ref, har_ref, root_ref, b2_ref, dtab_ref, dh_ref, x_ref, da_ref, gt_ref, dx_ref, acc_ref):
    dx, _ = norm_one_back(
        dh_ref, hal_ref, har_ref, summed(me_ref, hal_ref, root_ref, b2_ref, dtab_ref), x_ref[...].astype(F32),
        gain_row(gt_ref, 0, 0), da_ref, acc_ref,
    )
    dx_ref[...] = dx


def dw_kernel(me_ref, *rest, part, nouts, gains=False):
    srcs, rest = rest[:9], rest[9:]
    if gains:
        gain_ref, rest = rest[0], rest[1:]
    outs, rest = rest[-12 - nouts : -12], rest[-12:]
    hx_ref, dq_ref, dkv_ref, o_ref, dab_ref, h2_ref, dub_ref, act_ref, dxb_ref, g_ref, sem, isem = rest
    copies = Copies(isem)
    loads = {}
    for i in {0: (7, 8), 1: (5, 6), 2: (3, 4, 0, 1, 2)}[part]:
        loads[i] = copies.start(srcs[i], rest[i])

    def put(val, base, nj, i0, j0):
        v = val.astype(BF16)
        for i in range(val.shape[0] // 16):
            for j in range(val.shape[1] // 128):
                g_ref[base + (i0 + i) * nj + j0 + j] = v[16 * i : 16 * i + 16, 128 * j : 128 * j + 128]

    def send(lo, hi):
        if nouts == 1:
            tiles = pl.ds(lo * 16, (hi - lo) * 16)
            pltpu.make_async_copy(g_ref.at[tiles], outs[0].at[tiles], sem).start()
            return
        me = me_ref[0]
        units = {}
        for u in range(lo, hi):
            units.setdefault(u // 3, []).append(u % 3)
        for d, thirds in units.items():
            core = d % 2
            rx, ry = ((me // 2) % 2) ^ (d // 2 % 2), ((me // 4) % 2) ^ (d // 4 % 2)
            ra, rb = (rx, ry) if core == 0 else (ry, rx)
            k = (d // 8 - me // 8 + 4) % 4
            t0, t1 = 16 * thirds[0], 16 * thirds[-1] + 16
            for rc in range(2):

                @pl.when((me % 2) ^ core == rc)
                def _():
                    pltpu.make_async_copy(
                        g_ref.at[pl.ds(d * BT + t0, t1 - t0)], outs[rc].at[rb, ra, k, pl.ds(t0, t1 - t0)], sem
                    ).start()

    if part == 0:
        loads[7].wait()
        loads[8].wait()

        def down(c, carry):
            c0 = pl.multiple_of(c * 256, 256)
            put(mm_tn(act_ref[:, pl.ds(c0, 256)], dxb_ref[...]), WD0, 4, 16 * c, 0)
            return carry

        lax.fori_loop(0, FF // 256, down, 0, unroll=8)
        send(64, 96)
    if part == 1:
        loads[5].wait()
        loads[6].wait()

        def up(c, carry):
            c0 = pl.multiple_of(c * 256, 256)
            put(mm_tn(h2_ref[...], dub_ref[:, pl.ds(c0, 256)]), WU0, 16, 0, 2 * c)
            return carry

        lax.fori_loop(0, FF // 256, up, 0, unroll=8)
        send(32, 64)
    if part == 2:
        for i in (3, 4, 0, 1, 2):
            loads[i].wait()
        for j in range(2):
            put(mm_tn(o_ref[...], dab_ref[:, 256 * j : 256 * j + 256]), WO0, 4, 0, 2 * j)
        send(24, 32)
        for j in range(2):
            put(mm_tn(hx_ref[LH : LH + TOK], dq_ref[:, 256 * j : 256 * j + 256]), QKV0, 12, 0, 2 * j)
        for j in range(4):
            put(mm_tn(hx_ref[...], dkv_ref[:, 256 * j : 256 * j + 256]), QKV0, 12, 0, 4 + 2 * j)
        send(0, 24)
        if gains:
            for i in range(GROUPS):
                pltpu.make_async_copy(
                    gain_ref, outs[i // 16].at[i % 2, i // 2 % 2, i // 4 % 4, BT], sem
                ).start()
            for i in range(GROUPS):
                pltpu.make_async_copy(gain_ref, gain_ref, sem).wait()
    first, count = {0: (WD0, 512), 1: (WU0, 512), 2: (0, 512)}[part]
    all_of = g_ref.at[pl.ds(first, count)]
    pltpu.make_async_copy(all_of, all_of, sem).wait()


def sds(shape, dtype):
    return jax.ShapeDtypeStruct(shape, dtype)


PARAMS = dict(vmem_limit_bytes=56 * 1024 * 1024)


def run(kernel, outs, ins, specs=None, scratch=(), flops=0, nbytes=0, aliases=None, **kw):
    return pl.pallas_call(
        kernel,
        out_shape=outs,
        input_output_aliases=aliases or {},
        in_specs=specs or [VM] * len(ins),
        out_specs=jax.tree.map(lambda _: VM, outs) if "out_specs" not in kw else kw["out_specs"],
        scratch_shapes=list(scratch),
        compiler_params=pltpu.CompilerParams(**PARAMS),
        cost_estimate=pl.CostEstimate(flops=flops, bytes_accessed=nbytes, transcendentals=0),
    )(*ins)


def shift(value, by, n):
    return lax.ppermute(value, "ta", [(i, i + by) for i in range(n) if 0 <= i + by < n])


def strides(n):
    return [(1 << k, 2) for k in reversed(range(n.bit_length() - 1))]


def spread_round(value, digit, done, n):
    stride, radix = digit
    keep = [i for i in range(n) if all(i // s % r == 0 for s, r in strides(n) if (s, r) not in done)]
    parts = [lax.ppermute(value, "ta", [(i, i + j * stride) for i in keep]) for j in range(1, radix)]
    return functools.reduce(jnp.add, parts, value)


def collect_round(value, digit, done, n):
    stride, radix = digit
    keep = [i for i in range(n) if all(i // s % r == 0 for s, r in [digit] + done)]
    parts = [lax.ppermute(value, "ta", [(i + j * stride, i) for i in keep]) for j in range(1, radix)]
    return sum((part.astype(F32) for part in parts), value.astype(F32)).astype(value.dtype)


def from_first(value, me, n, root=0):
    value = jnp.where(me == root, value, jnp.zeros_like(value))
    if root:
        value = shift(value, -root, n)
    digits = strides(n)
    for i in range(len(digits)):
        value = spread_round(value, digits[i], digits[:i], n)
    return value


def sum_all(value, n):
    step = 1
    while step < n:
        value = value + lax.ppermute(value, "ta", [(i, i ^ step) for i in range(n)])
        step *= 2
    return value


def tiles_of(rows, ni, nj):
    return rows.reshape(ni, 16, nj, 128).transpose(0, 2, 1, 3).reshape(ni * nj, 16, 128)


def rows_of(tiles, ni, nj):
    return tiles.reshape(ni, nj, 16, 128).transpose(0, 2, 1, 3).reshape(ni * nj * 16, 128)


PIECES = ((QKV0, 32, 12), (WO0, 32, 4), (WU0, 32, 16), (WD0, 128, 4))


def gather_plain(aligned):
    full = lax.all_gather(aligned.reshape(-1, 128), "ta", axis=0, tiled=True)
    return jnp.concatenate(
        [tiles_of(full[16 * b : 16 * (b + ni * nj)], ni, nj) for b, ni, nj in PIECES], axis=0
    )


def reduce_plain(tiles):
    full = jnp.concatenate([rows_of(tiles[b : b + ni * nj], ni, nj) for b, ni, nj in PIECES], axis=0)
    return lax.psum_scatter(full, "ta", scatter_dimension=0, tiled=True).astype(F32).reshape(-1)


def links(n, kind, by=1):
    pairs = []
    for i in range(n):
        if kind == "core":
            pairs.append((i, i ^ 1))
        elif kind == "z":
            pairs.append((i, (i + 8 * by) % n))
        else:
            pairs.append((i, i ^ (2 if (kind == "a") == (i % 2 == 0) else 4)))
    return pairs


def move(value, kind, by=1):
    return lax.ppermute(value, "ta", links(32, kind, by))


def after(value, *others):
    return lax.optimization_barrier((value,) + others)[0]


def to_tiles(rows, me):
    third = 3 * me + jnp.arange(3).reshape(3, 1, 1, 1)
    qkv = tiles_of(rows, 4, 12).reshape(3, 16, 16, 128)
    four = rows.reshape(3, 4, 16, 4, 128).transpose(0, 1, 3, 2, 4).reshape(3, 16, 16, 128)
    wide = rows.reshape(3, 16, 16, 128).transpose(0, 2, 1, 3)
    out = jnp.where(third < 24, qkv, jnp.where((third >= 32) & (third < 64), wide, four))
    return out.reshape(48, 16, 128)


def to_rows(tiles, me):
    third = 3 * me + jnp.arange(3).reshape(3, 1, 1)
    qkv = rows_of(tiles, 4, 12).reshape(3, 256, 128)
    four = tiles.reshape(3, 4, 4, 16, 128).transpose(0, 1, 3, 2, 4).reshape(3, 256, 128)
    wide = tiles.reshape(3, 16, 16, 128).transpose(0, 2, 1, 3).reshape(3, 256, 128)
    out = jnp.where(third < 24, qkv, jnp.where((third >= 32) & (third < 64), wide, four))
    return out.reshape(-1)


def head_rows(tiles, me):
    third = 3 * me
    four = ((third >= 24) & (third < 32)) | (third >= 64)
    return jnp.where(four, jnp.concatenate([tiles[:4, 0], tiles[:4, 1]], axis=0), tiles[:8, 0]).reshape(-1)


def per_device(frames, cotangent, mem_index, master, moment, second, average):
    n = lax.axis_size("ta")
    me = lax.axis_index("ta")
    mev = me.astype(jnp.int32).reshape(1)
    layers, share = master.shape
    step = 2 * D // n
    fast = n == GROUPS
    digits = strides(n)

    def vmem(*shape_types):
        return [pltpu.VMEM(shape, dtype) for shape, dtype in shape_types]

    def sems(count):
        return [pltpu.SemaphoreType.DMA((count,))]

    def call(kernel, ins, specs, outs, scratch, aliases=None, flops=3 * 10**9):
        return run(
            kernel, tuple(sds(*o) for o, _ in outs), tuple(ins), specs=specs,
            out_specs=tuple(VM if keep else ANYS for _, keep in outs), scratch=scratch,
            aliases=aliases, flops=flops, nbytes=10**7,
        )

    tf, tb = ((TOK, D), F32), ((TOK, D), BF16)
    wide, rows16, kv16 = ((TOK, FF), BF16), ((ROWS, D), BF16), ((ROWS, 2 * D), BF16)
    prob, rows32, kv32 = ((NBLK * 4, KB, 128), BF16), ((ROWS, D), F32), ((ROWS, 2 * D), F32)
    drow, dtab_t, sums = ((1, D), F32), ((128, D), F32), ((NSEG, D), BF16)
    tiles_t = ((TILES, 16, 128), BF16)
    score = ((NBLK * 4, KB, 128), F32)
    wscr = vmem(tiles_t) + sems(GROUPS + 1)

    msgs = [(((LH + NSEG, D), BF16), True), (((RH, D), BF16), True), (sums, True), (sums, True)]

    def forward_moves(ahead, back, summ):
        return shift(ahead, 1, n), shift(back, -1, n), shift(summ, 2, n)

    tail = shift(master[:, share - 2 * D :], 1, n)
    ahead, back, root, summ = call(first_kernel, (mev, frames), [SM, VM], msgs, [], flops=10**7)
    ahead, back, root, summ, tail = lax.optimization_barrier((ahead, back, root, summ, tail))
    hl, hr, behind2 = forward_moves(ahead, back, summ)

    ext = jnp.concatenate([tail, master], axis=1)
    aligned = lax.dynamic_slice(ext, (0, 2 * D - step * me), (layers, MATS // n)).astype(BF16)
    gains = master[:, share - 2 * D :].astype(BF16).reshape(1, 16, 128)
    if fast:
        tiles = [to_tiles(aligned[l].reshape(-1, 128), me) for l in range(layers)]
        zd = 2
        for i in range(zd):
            root = spread_round(root, digits[i], digits[:i], n)
        b0 = after(jnp.concatenate([tiles[0], gains]), root, hl, hr, behind2)
        own0 = jnp.stack([b0] + [move(b0, "z", k) for k in range(1, 4)])
        for i in range(zd, len(digits)):
            root = spread_round(root, digits[i], digits[:i], n)
        own0 = after(own0, root)
        a0, s0 = move(own0, "a"), move(own0, "b")
        b1 = after(tiles[1], own0)
        own1 = jnp.stack([b1] + [move(b1, "z", k) for k in range(1, 4)])
        a0 = after(a0, s0, own1)
        as0 = move(a0, "b")
        w0 = [own0, a0, s0, as0]
        w0 += [move(after(v, own1), "core") for v in w0]
        a1, s1 = move(own1, "a"), move(own1, "b")
        w0 = tuple(w0)
    else:
        w0 = (gather_plain(aligned[0]), from_first(gains[0], me, n, n - 1))
        root = from_first(root, me, n)
    low_parts = (hl, hr, root, behind2, summ)

    first_seg = me * NSEG
    seg_ids = first_seg + jnp.arange(NSEG, dtype=jnp.int32)
    slot = jnp.arange(MEM, dtype=jnp.int32)
    loc = jnp.where(slot[None, :] == 0, mem_index, mem_index - first_seg + 96).reshape(-1, 1)
    loc = jnp.broadcast_to(loc, (NSEG * MEM, 128))
    vis = (mem_index < seg_ids[:, None]).astype(F32).reshape(-1, 1)
    vis = jnp.broadcast_to(vis, (NSEG * MEM, 128))

    hid = (rows16, tb, kv16, prob, tb)
    gt, hx0, q0, kv0, p0, o0 = call(
        functools.partial(low_attn_kernel, np_=len(w0), n=n), (mev, frames, *low_parts, loc, vis) + w0,
        [SM] + [VM] * 8 + [ANYS] * len(w0), [(((16, 128), BF16), True)] + [(t, False) for t in hid],
        wscr + vmem(*hid, score) + sems(5),
    )
    if fast:
        a1 = after(a1, o0)
        as1 = move(a1, "b")
        w1 = [own1, a1, s1]
        w1 = w1 + [as1] + [move(after(v, o0), "core") for v in w1]
    hid = (tf, tb, wide, wide)
    x1, h1, ahead, back, root, summ, a0, h20, gp0, act0 = call(
        functools.partial(low_ffn_kernel, np_=len(w0)), (mev, frames, o0, gt) + w0,
        [SM] + [VM] * 3 + [ANYS] * len(w0), [(tf, True), (tb, True)] + msgs + [(t, False) for t in hid],
        wscr + vmem(*hid) + sems(4),
    )
    if fast:
        ahead, back, root, summ, as1, *_ = lax.optimization_barrier((ahead, back, root, summ, as1, *w1[4:]))
        w1[3] = as1
    hl, hr, behind2 = forward_moves(ahead, back, summ)
    for i in range(len(digits)):
        root = spread_round(root, digits[i], digits[:i], n)
        if i == 1:
            root = after(root, hl, hr, behind2)
    if fast:
        w1 = tuple(w1 + [move(as1, "core")])
    else:
        w1 = (gather_plain(aligned[1]),)

    def grads_out(kind):
        shapes = ((LH + NSEG, D), kind), ((RH, D), kind), ((NSEG, D), kind), ((NSEG, D), kind), ((NSEG, D), F32)
        return [(tf, True)] + [(shape, True) for shape in shapes]

    kept = (rows16, tb, tb, wide, tb, wide, tb, tb, kv16)
    output, da, dh, hal, har, root, b2, mine, dgb1, hx1, o1, h21, act1, dxb, dub, dab, dq, dkvb = call(
        functools.partial(top_kernel, np_=len(w1), n=n),
        (mev, x1, h1, hl, hr, root, behind2, summ, loc, vis, gt, cotangent) + w1,
        [SM] + [VM] * 10 + [ANYS] * (1 + len(w1)),
        [(tf, False), (tf, True)] + grads_out(BF16) + [(drow, True)] + [(t, False) for t in kept],
        wscr + vmem(rows16, tb, kv16, prob, tb, tf, tb, wide, wide, tf, tf, tb, wide, tb, tb, kv16, kv32, tb, rows32, score) + sems(11),
        flops=8 * 10**9,
    )

    def backward_moves(hal, har, b2):
        return shift(hal, -1, n), shift(har, 1, n), shift(b2, -2, n)

    tree = digits[-1:] + digits[:-1]

    def collect(root, i):
        return collect_round(root, tree[i], tree[:i], n)

    dws = vmem(rows16, tb, kv16, tb, tb, tb, wide, wide, tb, tiles_t)
    dws += [pltpu.SemaphoreType.DMA] + sems(9)

    def weight_grads(part, ins, partial, gains=None):
        extra = BT + (1 if fast and gains_in else 0)
        outs = [(((2, 2, 4, extra, 16, 128), BF16), False)] * 2 if fast else [(tiles_t, False)]
        count = len(outs)
        ins = [mev] + list(ins) + ([] if gains is None else [gains])
        specs = [SM] + [ANYS] * 9 + [VM] * (len(ins) - 10)
        return call(
            functools.partial(dw_kernel, part=part, nouts=count, gains=gains is not None),
            ins + list(partial), specs + [ANYS] * len(partial), outs, dws,
            aliases={len(ins) + i: i for i in range(len(partial))}, flops=10**9,
        )

    gains_in = False
    hal, har, b2 = backward_moves(hal, har, b2)
    root = collect(root, 0)
    ins = [hx1, dq, dkvb, o1, dab, h21, dub, act1, after(dxb, root, hal, har, b2)]
    part = ()
    for i in range(2):
        part = weight_grads(i, ins, part)
        root = collect(root, i + 1)
        ins[6], ins[4] = after(dub, root), after(dab, root)
        root = after(root, part[0])
    for i in range(3, len(tree)):
        root = collect(root, i)
    grads = weight_grads(2, ins, part)

    def add(a, b):
        return (a.astype(F32) + b.astype(F32)).astype(BF16)

    if fast:
        v1 = after(add(grads[0], move(grads[1], "core")), root)
        got = move(v1[1], "b")
        x1 = after(x1, v1)
    else:
        reduced1 = reduce_plain(grads[0])

    dga1, da, dgb0, dxb, dub, dab = call(
        functools.partial(bottom_ffn_kernel, np_=len(w0)), (mev, hal, har, root, b2, mine, dh, x1, da, gt) + w0 + (a0, gp0),
        [SM] + [VM] * 9 + [ANYS] * (len(w0) + 2),
        [(drow, True), (tf, True), (drow, True), (tb, False), (wide, False), (tb, False)],
        wscr + vmem(tf, wide, tf, tb, wide, tb) + sems(5),
    )
    dga0, dh, hal, har, root, b2, mine, dq, dkvb = call(
        functools.partial(bottom_attn_kernel, np_=len(w0)),
        (mev, dab, loc, frames) + low_parts + w0 + (q0, kv0, p0), [SM] + [VM] * 8 + [ANYS] * (len(w0) + 3),
        [(drow, True)] + grads_out(F32) + [(tb, False), (kv16, False)],
        wscr + vmem(tb, kv16, prob, tb, kv16, kv32, tb, rows32, score) + sems(5),
    )
    gains = jnp.concatenate([dga0, dgb0, dga1, dgb1], axis=1)
    ins = [hx0, dq, dkvb, o0, dab, h20, dub, act0, dxb]
    if fast:
        v1 = add(after(v1[0], dh), got)
        got = move(v1[1], "a")
        ins[8] = after(dxb, v1)
        gains_in = True
    part = ()
    for i in range(2):
        part = weight_grads(i, ins, part)
    if fast:
        v1 = add(after(v1[0], part[0]), got)
        z1 = [move(v1[k], "z", k) for k in range(1, 4)]
        ins[4] = after(dab, v1)
    grads = weight_grads(2, ins, part, gains.astype(BF16).reshape(16, 128) if fast else None)
    if fast:
        v = add(grads[0], move(grads[1], "core"))
        root = collect(after(root, v), 0)
        got = move(v[1], "b")
        v = add(v[0], got)
        total1 = functools.reduce(jnp.add, [z.astype(F32) for z in z1], after(v1[0], v).astype(F32))
        got = move(v[1], "a")
        root = collect(collect(after(root, v, total1), 1), 2)
        reduced1, head1 = to_rows(total1, me), shift(head_rows(total1, me), -1, n)
        v = add(v[0], got)
        root = after(root, v, head1)
        zs = [move(v[k], "z", k) for k in range(1, 4)]
        for i in range(3, len(tree)):
            root = collect(root, i)
        hal, har, b2 = backward_moves(hal, har, after(b2, v))
        total0 = functools.reduce(jnp.add, [z.astype(F32) for z in zs], v[0].astype(F32))
        gsum = total0[BT].reshape(layers, 2 * D)
        total0 = total0[:BT]
        reduced = [to_rows(total0, me), reduced1]
        heads = [shift(head_rows(total0, me), -1, n), head1]
    else:
        hal, har, b2 = backward_moves(hal, har, b2)
        for i in range(len(tree)):
            root = collect(root, i)
        gsum = sum_all(gains.reshape(layers, 2 * D), n)
        reduced = [reduce_plain(grads[0]), reduced1]
        heads = [shift(r[: 2 * D], -1, n) for r in reduced]
    dx = call(
        last_kernel, (mev, hal, har, root, b2, mine, dh, frames, da, gt),
        [SM] + [VM] * 9, [(tf, True)], vmem(tf), flops=10**7,
    )[0]

    own = jnp.stack(reduced)
    head = jnp.where(me == n - 1, gsum, jnp.stack(heads))
    grad = lax.dynamic_slice(jnp.concatenate([own, head], axis=1), (0, step * me), (layers, share))
    gain_out = lax.dynamic_slice(gsum, (0, step * me), (layers, step))
    new_moment = 0.5 * moment + 0.5 * grad
    new_second = 0.5 * second + 0.5 * grad * grad
    correction = 1.0 - 0.5**STEP
    update = new_moment / correction / (jnp.sqrt(new_second / correction) + 1e-08) + 0.1 * master
    new_master = master - 0.08 * update
    new_average = 0.9 * average + 0.1 * new_master
    return (output, dx, gain_out, new_moment, new_second, new_master, new_average)


def solution(mesh):
    rows, flat = P("ta", None), P(None, "ta")
    return jax.shard_map(
        per_device,
        mesh=mesh,
        in_specs=(rows, rows, rows, flat, flat, flat, flat),
        out_specs=(rows, rows, flat, flat, flat, flat, flat),
        check_vma=False,
    )
```
